32 devices in a mesh: state: 8 (over y, x, core), probe: 4 (over z).
Axes of the slice: x: 2, y: 2, z: 4, core: 2. Of those that a mesh axis runs over, the one named last changes fastest.
Arguments:
- sensor_field: float32 [4, 32, 64, 512], P('probe', 'state'), may hold values from -1 to 1
- courant: float32 [64], replicated, may hold values from 0.1 to 0.45
- diffusivity: float32 [64], replicated, may hold values from 0.01 to 0.085
- probe_offset: int32 [4], P('probe'), may hold values from 0 to 511
- tile_index: int32 [8, 4096], P('state'), may hold values from 0 to 1023
- actuator_panel: bfloat16 [8, 4096, 128], P('state', 'probe'), may hold values from -3 to 3
Outputs:
- projections: float32 [4, 4, 4096], P(None, 'probe')
- response: float32 [4, 32, 64, 512], P('probe', 'state')
The draws below stay inside these ranges and needn't reach their ends.
All inputs are finite; a program needn't handle non-finite values.
Results may differ from the reference program's by a relative error of at most 0.0003.
Values may be sent and summed in bfloat16 or wider, within the bound.
No kernel may reach another device: no remote copies, remote signals or barrier semaphores. Data moves between devices by JAX's collectives and lax.ppermute only.
A program may use at most 64 MiB of HBM per device.

```python
import math
import jax
import jax.numpy as jnp
from jax import lax

CX = 4
NY = 64
NZ = 512
M = 4096
TILE = 128
STEPS = 4
PROBES = 4
SLABS = 8
NX = 32
TILES = 1024
ACT_TILE = 4


def draw_sensor_field(key, part):
    slab_count = NX // CX
    amplitude = 2.5 * math.sqrt(ACT_TILE / (TILE * slab_count))
    values = jax.random.truncated_normal(key, -3.0, 3.0, (PROBES, NX, NY, NZ), jnp.float32)
    return (values * amplitude).astype(jnp.float32)


def touch_ends(entries, key, low, largest):
    longest = entries.shape.index(max(entries.shape))
    spots = []
    for shift in (0, 1):
        where = [jax.random.randint(jax.random.fold_in(key, axis), (), 0, length) for axis, length in enumerate(entries.shape)]
        where[longest] = (where[longest] + shift) % entries.shape[longest]
        spots.append(tuple(where))
    return entries.at[spots[0]].set(low).at[spots[1]].set(largest)


def block_levels(rng, dims, split, least, high):
    def one(position, shards_of):
        heights = jax.random.uniform(jax.random.fold_in(jax.random.fold_in(rng, 6), position), (shards_of,), jnp.float32, least / len(split), high / len(split))
        return jnp.repeat(jnp.exp(heights), dims[position] // shards_of).reshape((-1,) + (1,) * (len(dims) - position - 1))

    gain = one(*split[0])
    for cut in split[1:]:
        gain = gain * one(*cut)
    return gain


def centred(key, dims, width, most, shards=(), held_as=jnp.bfloat16):
    loudness = block_levels(key, dims, shards, -0.22, 0.18) if shards else 1.0
    result = jax.random.normal(key, dims, jnp.float32) * width * loudness
    return jnp.minimum(jnp.maximum(result, -most), most).astype(held_as)


def setup_inputs(seed: int = 0) -> dict:
    key_list = jax.random.split(jax.random.key(seed), 7)
    sensor_field = draw_sensor_field(jax.random.fold_in(key_list[6], 71), 0)
    courant = jnp.clip(jax.random.uniform(key_list[1], (NY,), jnp.float32, 0.1, 0.45), 0.1, 0.45)
    diffusivity = jnp.clip(jnp.exp(jax.random.uniform(key_list[2], (NY,), jnp.float32, math.log(0.01), math.log(0.085))), 0.01, 0.085)
    probe_offset = touch_ends(jax.random.randint(key_list[3], (PROBES,), 0, NZ), jax.random.fold_in(key_list[3], 1), 0, NZ - 1).astype(jnp.int32)
    tile_index = touch_ends(jax.random.randint(key_list[4], (SLABS, M), 0, TILES), jax.random.fold_in(key_list[4], 1), 0, TILES - 1).astype(jnp.int32)
    actuator_panel = centred(key_list[5], (SLABS, M, TILE), ACT_TILE ** -0.5, 3.0, ((0, 8), (1, 4)))
    return dict(sensor_field=sensor_field, courant=courant, diffusivity=diffusivity, probe_offset=probe_offset, tile_index=tile_index, actuator_panel=actuator_panel)


def advance(center, lower_x, upper_x, courant, diffusion, adjoint):
    advect_rate = courant[:, None]
    diff_rate = diffusion[:, None]
    upper_z = jnp.roll(center, -1, axis=-1)
    lower_z = jnp.roll(center, 1, axis=-1)
    zero_row = jnp.zeros_like(center[..., :1, :])
    upper_y = jnp.concatenate([center[..., 1:, :], zero_row], axis=-2)
    lower_y = jnp.concatenate([zero_row, center[..., :-1, :]], axis=-2)
    doubled_center = 2.0 * center
    lateral = (lower_x + upper_x - doubled_center) + (upper_z + lower_z - doubled_center)
    if adjoint:
        upwind = upper_x
        edge_zero = jnp.zeros((1,), diffusion.dtype)
        rate_above = jnp.concatenate([diffusion[1:], edge_zero])[:, None]
        rate_below = jnp.concatenate([edge_zero, diffusion[:-1]])[:, None]
        normal = rate_above * upper_y + rate_below * lower_y - diff_rate * doubled_center
    else:
        upwind = lower_x
        normal = diff_rate * (upper_y + lower_y - doubled_center)
    return center + advect_rate * (upwind - center) + diff_rate * lateral + normal


def shifted_sensor(sensor, offset):
    doubled = jnp.concatenate([sensor, sensor], axis=-1)
    span_z = sensor.shape[-1]
    begin_at = (span_z - offset).astype(jnp.int32)
    return lax.dynamic_slice_in_dim(doubled, begin_at, span_z, axis=doubled.ndim - 1)


def reference(sensor_field, courant, diffusivity, probe_offset, tile_index, actuator_panel):
    panel_wide = actuator_panel.astype(jnp.float32)
    slab_ids = jnp.broadcast_to(jnp.arange(SLABS, dtype=jnp.int32)[:, None], tile_index.shape)

    def one_probe(inputs):
        sensor_one, offset = inputs
        field_now = shifted_sensor(sensor_one, offset)
        collected = []
        for sweep_index in range(STEPS):
            field_now = advance(field_now, jnp.roll(field_now, 1, axis=0), jnp.roll(field_now, -1, axis=0), courant, diffusivity, True)
            tile_view = field_now.reshape(SLABS, TILES, TILE)
            picked = jnp.take_along_axis(tile_view, tile_index[:, :, None], axis=1)
            collected.append(jnp.sum(picked * panel_wide, axis=(0, 2)))
        drive_input = collected[-1]
        deposit = jnp.zeros((SLABS, TILES, TILE), jnp.float32)
        deposit = deposit.at[slab_ids, tile_index].add(drive_input[None, :, None] * panel_wide)
        field_now = deposit.reshape(NX, NY, NZ)
        for sweep_index in range(STEPS):
            field_now = advance(field_now, jnp.roll(field_now, 1, axis=0), jnp.roll(field_now, -1, axis=0), courant, diffusivity, False)
        return jnp.stack(collected), field_now

    stacked, response = lax.map(one_probe, (sensor_field, probe_offset))
    return jnp.transpose(stacked, (1, 0, 2)), response
```

```python
import jax
import jax.numpy as jnp
from jax import lax
from jax.experimental import pallas as pl
from jax.experimental.pallas import tpu as pltpu
from jax.sharding import PartitionSpec as P

TILE = 128
STEPS = 4
PAD = 8
GROUP = 256
VMEM_LIMIT = 48 * 1024 * 1024


def shift_pairs(count, by):
    return [(i, (i + by) % count) for i in range(count)]


def coefficients(courant, diffusivity):
    zero = jnp.zeros((1,), diffusivity.dtype)
    rows = jnp.stack(
        [
            1.0 - courant - 6.0 * diffusivity,
            courant + diffusivity,
            diffusivity,
            jnp.concatenate([diffusivity[1:], zero]),
            jnp.concatenate([zero, diffusivity[:-1]]),
        ]
    )
    return jnp.broadcast_to(rows[:, :, None], rows.shape + (TILE,))


def clear_pads(buffer):
    planes, columns, rows, lanes = buffer.shape
    edge = jnp.zeros((columns, PAD, lanes), buffer.dtype)

    def body(plane, carry):
        buffer[plane, :, :PAD, :] = edge
        buffer[plane, :, rows - PAD :, :] = edge
        return carry

    lax.fori_loop(0, planes, body, 0)


def stencil_block(source, coef, plane, row, height, adjoint):
    centre = source[plane, :, pl.ds(PAD + row, height), :]
    above = source[plane, :, pl.ds(PAD + row + 1, height), :]
    below = source[plane, :, pl.ds(PAD + row - 1, height), :]
    upper_x = source[plane + 1, :, pl.ds(PAD + row, height), :]
    lower_x = source[plane - 1, :, pl.ds(PAD + row, height), :]
    columns = centre.shape[0]
    lane = lax.broadcasted_iota(jnp.int32, (height, TILE), 1)
    left = [pltpu.roll(centre[c], TILE - 1, 1) for c in range(columns)]
    right = [pltpu.roll(centre[c], 1, 1) for c in range(columns)]
    block = pl.ds(row, height)
    w_centre, w_up, w_diff = coef[0, block, :], coef[1, block, :], coef[2, block, :]
    out = []
    for c in range(columns):
        upper_z = jnp.where(lane == TILE - 1, left[(c + 1) % columns], left[c])
        lower_z = jnp.where(lane == 0, right[(c - 1) % columns], right[c])
        if adjoint:
            total = w_centre * centre[c] + w_up * upper_x[c]
            total = total + w_diff * (lower_x[c] + (upper_z + lower_z))
            total = total + coef[3, block, :] * above[c] + coef[4, block, :] * below[c]
        else:
            total = w_centre * centre[c] + w_up * lower_x[c]
            total = total + w_diff * ((upper_x[c] + (upper_z + lower_z)) + (above[c] + below[c]))
        out.append(total)
    return out


def split(value):
    high = value.astype(jnp.bfloat16)
    low = (value - high.astype(jnp.float32)).astype(jnp.bfloat16)
    return high, low


def adjoint_kernel(offset, coef, own, low, high, tiles, first, second):
    cells, height, width = own.shape
    columns = width // TILE
    steps = tiles.shape[0]
    clear_pads(first)
    clear_pads(second)
    turn = offset[0] // TILE
    rest = offset[0] % TILE
    lane = lax.broadcasted_iota(jnp.int32, (height, TILE), 1)
    for slab, field in enumerate((low, own, high)):

        def load(plane, carry, slab=slab, field=field):
            rolled = [
                pltpu.roll(field[plane, :, pl.ds(c * TILE, TILE)], rest, 1) for c in range(columns)
            ]
            for c in range(columns):
                value = jnp.where(lane >= rest, rolled[c], rolled[c - 1])
                first[slab * cells + plane, lax.rem(c + turn, columns), pl.ds(PAD, height), :] = value
            return carry

        lax.fori_loop(0, cells, load, 0)
    buffers = (first, second)
    rows = 16
    for step in range(steps):
        source, target = buffers[step % 2], buffers[(step + 1) % 2]

        def outer(plane, carry, source=source, target=target):
            for row in range(0, height, rows):
                block = stencil_block(source, coef, plane, row, rows, True)
                for c in range(columns):
                    target[plane, c, pl.ds(PAD + row, rows), :] = block[c]
            return carry

        def inner(plane, carry, source=source, target=target, step=step):
            for row in range(0, height, rows):
                block = stencil_block(source, coef, plane, row, rows, True)
                for c in range(columns):
                    target[plane, c, pl.ds(PAD + row, rows), :] = block[c]
                    start = (plane - cells) * columns * height + c * height + row
                    where = pl.ds(pl.multiple_of(start, rows), rows)
                    head, tail = split(block[c])
                    tiles[step, where, pl.ds(0, TILE)] = head
                    tiles[step, where, pl.ds(TILE, TILE)] = tail
            return carry

        lax.fori_loop(step + 1, cells, outer, 0)
        lax.fori_loop(cells, 2 * cells, inner, 0)
        lax.fori_loop(2 * cells, 3 * cells - step - 1, outer, 0)


def forward_kernel(coef, own, low, high, out, first, second):
    cells, height, width = out.shape
    columns = width // TILE
    steps = STEPS
    clear_pads(first)
    clear_pads(second)
    for plane in range(cells):
        for c in range(columns):
            where = pl.ds(c * height, height)
            inside = pl.ds(PAD, height)
            first[cells + plane, c, inside, :] = own[plane, where, :]
            first[2 * cells + plane, c, inside, :] = high[plane, where, :].astype(jnp.float32)
            value = low[plane, where, :].astype(jnp.float32)
            if plane > 0:
                value = value + low[cells + plane - 1, where, :].astype(jnp.float32)
            first[plane, c, inside, :] = value
    buffers = (first, second)
    rows = 16
    for step in range(steps):
        source, target = buffers[step % 2], buffers[(step + 1) % 2]
        last = step == steps - 1

        def body(plane, carry, source=source, target=target, last=last):
            for row in range(0, height, rows):
                block = stencil_block(source, coef, plane, row, rows, False)
                for c in range(columns):
                    if last:
                        out[plane - cells, pl.ds(row, rows), pl.ds(c * TILE, TILE)] = block[c]
                    else:
                        target[plane, c, pl.ds(PAD + row, rows), :] = block[c]
            return carry

        lax.fori_loop(step + 1, 3 * cells - step - 1, body, 0)


def project_kernel(index, panel, tiles, out):
    groups = index.shape[0]
    steps, total = tiles.shape[0], tiles.shape[1]
    chunk = 256

    def body(group, carry):
        rows = panel[pl.ds(pl.multiple_of(group * GROUP, GROUP), GROUP), :]
        doubled = jnp.concatenate([rows, rows], axis=1)
        wanted = index[group]
        for step in range(steps):
            partial = jnp.zeros((8, GROUP), jnp.float32)
            for start in range(0, total, chunk):
                gram = lax.dot_general(
                    tiles[step, pl.ds(start, chunk), :],
                    doubled,
                    (((1,), (1,)), ((), ())),
                    preferred_element_type=jnp.float32,
                )
                number = lax.broadcasted_iota(jnp.int32, (chunk, GROUP), 0) + start
                kept = jnp.where(number == wanted, gram, 0.0)
                partial = partial + jnp.sum(kept.reshape(chunk // 8, 8, GROUP), axis=0)
            out[step, group] = jnp.sum(partial, axis=0, keepdims=True)
        return carry

    lax.fori_loop(0, groups, body, 0)


def deposit_kernel(count, index, panel, *refs):
    parts, (total, field, rightward, leftward, scaled) = refs[:count], refs[count:]
    groups = index.shape[0]
    cells, per_plane = field.shape[0], field.shape[1]
    values = [part[...] for part in parts]
    while len(values) > 1:
        values = [values[i] + values[i + 1] for i in range(0, len(values), 2)]
    total[...] = values[0]
    drive = values[0].reshape(groups, GROUP).T
    for group in range(groups):
        where = pl.ds(group * GROUP, GROUP)
        product = drive[:, group : group + 1] * panel[where, :].astype(jnp.float32)
        head, tail = split(product)
        scaled[where, pl.ds(0, TILE)] = head
        scaled[where, pl.ds(TILE, TILE)] = tail

    def body(plane, carry):
        number = lax.broadcasted_iota(jnp.int32, (per_plane, GROUP), 0) + plane * per_plane
        sums = jnp.zeros((per_plane, 2 * TILE), jnp.float32)
        for group in range(groups):
            chosen = jnp.where(number == index[group], 1.0, 0.0).astype(jnp.bfloat16)
            sums = sums + lax.dot_general(
                chosen,
                scaled[pl.ds(group * GROUP, GROUP), :],
                (((1,), (0,)), ((), ())),
                preferred_element_type=jnp.float32,
            )
        value = sums[:, :TILE] + sums[:, TILE:]
        field[plane] = value
        head, tail = split(value)
        leftward[plane] = head
        rightward[plane] = head

        @pl.when(plane > 0)
        def _():
            rightward[cells + plane - 1] = tail

        return carry

    lax.fori_loop(0, cells, body, 0)


def call(kernel, out_shape, scratch=(), smem=0, inputs=0, flops=0):
    in_specs = [pl.BlockSpec(memory_space=pltpu.SMEM)] * smem
    in_specs += [pl.BlockSpec(memory_space=pltpu.VMEM)] * (inputs - smem)
    out_specs = jax.tree.map(lambda _: pl.BlockSpec(memory_space=pltpu.VMEM), out_shape)
    return pl.pallas_call(
        kernel,
        out_shape=out_shape,
        in_specs=in_specs,
        out_specs=out_specs,
        scratch_shapes=list(scratch),
        compiler_params=pltpu.CompilerParams(vmem_limit_bytes=VMEM_LIMIT),
        cost_estimate=pl.CostEstimate(flops=flops, bytes_accessed=4 * 1024 * 1024, transcendentals=0),
    )


def gathered_panel(panel, axis):
    count = lax.axis_size(axis)
    if count == 1:
        return panel
    place = lax.axis_index(axis)
    up = [(i, i + 1) for i in range(count - 1)]
    down = [(i + 1, i) for i in range(count - 1)]
    from_below, from_above = [panel], [panel]
    for stage in range(1, count):
        from_below.append(lax.ppermute(from_below[-1], axis, up[stage - 1 :]))
        from_above.append(lax.ppermute(from_above[-1], axis, down[: count - stage]))
    pieces = [panel]
    for shift in range(1, count):
        pieces.append(jnp.where(place >= shift, from_below[shift], from_above[count - shift]))
    return jnp.concatenate(pieces, axis=0)


def summands(part, axis):
    count = lax.axis_size(axis)
    if count & (count - 1):
        return [lax.psum(part, axis)]
    done = 1
    while True:
        span = min(8, count // done)
        parts = [part]
        for mask in range(1, span):
            parts.append(lax.ppermute(part, axis, [(i, i ^ (mask * done)) for i in range(count)]))
        done *= span
        if done == count:
            return parts
        part = tree_sum(parts)


def tree_sum(parts):
    while len(parts) > 1:
        parts = [parts[i] + parts[i + 1] for i in range(0, len(parts), 2)]
    return parts[0]


def doubling_sum(part, axis):
    count = lax.axis_size(axis)
    if count & (count - 1):
        return lax.psum(part, axis)
    mask = 1
    while mask < count:
        part = part + lax.ppermute(part, axis, [(i, i ^ mask) for i in range(count)])
        mask *= 2
    return part


def local(sensor_field, courant, diffusivity, probe_offset, tile_index, actuator_panel):
    slabs, probes = lax.axis_size("state"), lax.axis_size("probe")
    place = lax.axis_index("probe")
    own = sensor_field[0]
    cells, height, width = own.shape
    columns = width // TILE
    tile_total = cells * height * columns
    actuators = tile_index.shape[1]
    groups = actuators // GROUP
    planes = 3 * cells
    f32, bf16 = jnp.float32, jnp.bfloat16

    low = lax.ppermute(own, "state", shift_pairs(slabs, 1))
    high = lax.ppermute(own, "state", shift_pairs(slabs, -1))
    panel = gathered_panel(actuator_panel[0], "probe")

    coef = coefficients(courant, diffusivity)
    order = lax.rem(place - jnp.arange(probes, dtype=jnp.int32) + probes, probes)
    tile = jnp.take(tile_index[0].reshape(probes, -1), order, axis=0)
    plane, inside = tile // (height * columns), tile % (height * columns)
    index = plane * (height * columns) + (inside % columns) * height + inside // columns
    index = index.reshape(groups, 1, GROUP)

    field_shape = pltpu.VMEM((planes, columns, height + 2 * PAD, TILE), f32)
    tiles = call(
        adjoint_kernel,
        jax.ShapeDtypeStruct((STEPS, tile_total, 2 * TILE), bf16),
        scratch=(field_shape, field_shape),
        smem=1,
        inputs=5,
        flops=28 * 16 * height * width,
    )(probe_offset, coef, own, low, high)

    def project(part):
        return call(
            project_kernel,
            jax.ShapeDtypeStruct((part.shape[0], groups, 1, GROUP), f32),
            inputs=3,
            flops=part.shape[0] * 2 * actuators * tile_total * 2 * TILE,
        )(index, panel, part)

    last = project(tiles[STEPS - 1 :])
    early = project(tiles[: STEPS - 1])
    parts = summands(last, "state")
    payload = jax.ShapeDtypeStruct((2 * cells - 1, height * columns, TILE), bf16)
    heads = jax.ShapeDtypeStruct((cells, height * columns, TILE), bf16)
    total, forced, rightward, leftward = call(
        lambda *refs: deposit_kernel(len(parts), *refs),
        (
            jax.ShapeDtypeStruct(last.shape, f32),
            jax.ShapeDtypeStruct((cells, height * columns, TILE), f32),
            payload,
            heads,
        ),
        scratch=(pltpu.VMEM((actuators, 2 * TILE), bf16),),
        inputs=2 + len(parts),
        flops=2 * actuators * tile_total * 2 * TILE,
    )(index, panel, *parts)
    from_low = lax.ppermute(rightward, "state", shift_pairs(slabs, 1))
    from_high = lax.ppermute(leftward, "state", shift_pairs(slabs, -1))
    response = call(
        forward_kernel,
        jax.ShapeDtypeStruct((cells, height, width), f32),
        scratch=(field_shape, field_shape),
        inputs=4,
        flops=28 * 16 * height * width,
    )(coef, forced, from_low, from_high)

    early = doubling_sum(early, "state")
    projections = jnp.concatenate([early, total], axis=0).reshape(STEPS, probes, -1)
    back = lax.rem(place - jnp.arange(probes, dtype=jnp.int32) + probes, probes)
    projections = jnp.take(projections, back, axis=1).reshape(STEPS, 1, actuators)
    return projections, response[None]


def solution(mesh):
    return jax.shard_map(
        local,
        mesh=mesh,
        in_specs=(
            P("probe", "state", None, None),
            P(),
            P(),
            P("probe"),
            P("state", None),
            P("state", "probe", None),
        ),
        out_specs=(P(None, "probe", None), P("probe", "state", None, None)),
        check_vma=False,
    )
```

```python
import jax
import jax.numpy as jnp
import numpy as np
from jax import lax
from jax.experimental import pallas as pl
from jax.experimental.pallas import tpu as pltpu
from jax.sharding import PartitionSpec as P

TILE = 128
STEPS = 4
PAD = 8
GROUP = 256
VMEM_LIMIT = 48 * 1024 * 1024


def shift_pairs(count, by):
    return [(i, (i + by) % count) for i in range(count)]


def coefficients(courant, diffusivity):
    zero = jnp.zeros((1,), diffusivity.dtype)
    rows = jnp.stack(
        [
            1.0 - courant - 6.0 * diffusivity,
            courant + diffusivity,
            diffusivity,
            jnp.concatenate([diffusivity[1:], zero]),
            jnp.concatenate([zero, diffusivity[:-1]]),
        ]
    )
    return jnp.broadcast_to(rows[:, :, None], rows.shape + (TILE,))


def clear_pads(buffer):
    planes, columns, rows, lanes = buffer.shape
    edge = jnp.zeros((columns, PAD, lanes), buffer.dtype)

    def body(plane, carry):
        buffer[plane, :, :PAD, :] = edge
        buffer[plane, :, rows - PAD :, :] = edge
        return carry

    lax.fori_loop(0, planes, body, 0)


def stencil_block(source, coef, plane, row, height, adjoint):
    centre = source[plane, :, pl.ds(PAD + row, height), :]
    above = source[plane, :, pl.ds(PAD + row + 1, height), :]
    below = source[plane, :, pl.ds(PAD + row - 1, height), :]
    upper_x = source[plane + 1, :, pl.ds(PAD + row, height), :]
    lower_x = source[plane - 1, :, pl.ds(PAD + row, height), :]
    columns = centre.shape[0]
    lane = lax.broadcasted_iota(jnp.int32, (height, TILE), 1)
    left = [pltpu.roll(centre[c], TILE - 1, 1) for c in range(columns)]
    right = [pltpu.roll(centre[c], 1, 1) for c in range(columns)]
    block = pl.ds(row, height)
    w_centre, w_up, w_diff = coef[0, block, :], coef[1, block, :], coef[2, block, :]
    out = []
    for c in range(columns):
        upper_z = jnp.where(lane == TILE - 1, left[(c + 1) % columns], left[c])
        lower_z = jnp.where(lane == 0, right[(c - 1) % columns], right[c])
        if adjoint:
            total = w_centre * centre[c] + w_up * upper_x[c]
            total = total + w_diff * (lower_x[c] + (upper_z + lower_z))
            total = total + coef[3, block, :] * above[c] + coef[4, block, :] * below[c]
        else:
            total = w_centre * centre[c] + w_up * lower_x[c]
            total = total + w_diff * ((upper_x[c] + (upper_z + lower_z)) + (above[c] + below[c]))
        out.append(total)
    return out


def split(value):
    high = value.astype(jnp.bfloat16)
    low = (value - high.astype(jnp.float32)).astype(jnp.bfloat16)
    return high, low


def adjoint_kernel(offset, coef, own, low, high, tiles, first, second):
    cells, height, width = own.shape
    columns = width // TILE
    steps = tiles.shape[0]
    clear_pads(first)
    clear_pads(second)
    turn = offset[0] // TILE
    rest = offset[0] % TILE
    lane = lax.broadcasted_iota(jnp.int32, (height, TILE), 1)
    for slab, field in enumerate((low, own, high)):

        def load(plane, carry, slab=slab, field=field):
            rolled = [
                pltpu.roll(field[plane, :, pl.ds(c * TILE, TILE)], rest, 1) for c in range(columns)
            ]
            for c in range(columns):
                value = jnp.where(lane >= rest, rolled[c], rolled[c - 1])
                first[slab * cells + plane, lax.rem(c + turn, columns), pl.ds(PAD, height), :] = value
            return carry

        lax.fori_loop(0, cells, load, 0)
    buffers = (first, second)
    rows = 8
    for step in range(steps):
        source, target = buffers[step % 2], buffers[(step + 1) % 2]

        def outer(plane, carry, source=source, target=target):
            for row in range(0, height, rows):
                block = stencil_block(source, coef, plane, row, rows, True)
                for c in range(columns):
                    target[plane, c, pl.ds(PAD + row, rows), :] = block[c]
            return carry

        def inner(plane, carry, source=source, target=target, step=step):
            for row in range(0, height, 2 * rows):
                block = stencil_block(source, coef, plane, row, rows, True)
                after = stencil_block(source, coef, plane, row + rows, rows, True)
                for c in range(columns):
                    target[plane, c, pl.ds(PAD + row, rows), :] = block[c]
                    target[plane, c, pl.ds(PAD + row + rows, rows), :] = after[c]
                    start = (plane - cells) * columns * height + c * height + row
                    where = pl.ds(pl.multiple_of(start, 2 * rows), 2 * rows)
                    head, tail = split(jnp.concatenate([block[c], after[c]], axis=0))
                    tiles[step, where, pl.ds(0, TILE)] = head
                    tiles[step, where, pl.ds(TILE, TILE)] = tail
            return carry

        lax.fori_loop(step + 1, cells, outer, 0)
        lax.fori_loop(cells, 2 * cells, inner, 0)
        lax.fori_loop(2 * cells, 3 * cells - step - 1, outer, 0)


def forward_kernel(coef, own, low, high, out, first, second):
    cells, height, width = out.shape
    columns = width // TILE
    steps = STEPS
    clear_pads(first)
    clear_pads(second)
    for plane in range(cells):
        for c in range(columns):
            where = pl.ds(c * height, height)
            inside = pl.ds(PAD, height)
            first[cells + plane, c, inside, :] = own[plane, where, :]
            first[2 * cells + plane, c, inside, :] = high[plane, where, :].astype(jnp.float32)
            value = low[plane, where, :].astype(jnp.float32)
            if plane > 0:
                value = value + low[cells + plane - 1, where, :].astype(jnp.float32)
            first[plane, c, inside, :] = value
    buffers = (first, second)
    rows = 8
    for step in range(steps):
        source, target = buffers[step % 2], buffers[(step + 1) % 2]
        last = step == steps - 1

        def body(plane, carry, source=source, target=target, last=last):
            for row in range(0, height, rows):
                block = stencil_block(source, coef, plane, row, rows, False)
                for c in range(columns):
                    if last:
                        out[plane - cells, pl.ds(row, rows), pl.ds(c * TILE, TILE)] = block[c]
                    else:
                        target[plane, c, pl.ds(PAD + row, rows), :] = block[c]
            return carry

        lax.fori_loop(step + 1, 3 * cells - step - 1, body, 0)


def transposed(rows):
    return rows.astype(jnp.float32).T.astype(jnp.bfloat16)


def wanted_tile(index, group, columns, height):
    tile = index[group]
    inside = tile & (columns * height - 1)
    return (tile - inside) + (inside & (columns - 1)) * height + inside // columns


def kept_sum(tiles, step, weights, wanted):
    chunk = 256
    partial = jnp.zeros((8, GROUP), jnp.float32)
    for start in range(0, tiles.shape[1], chunk):
        gram = jnp.dot(
            tiles[step, pl.ds(start, chunk), :], weights, preferred_element_type=jnp.float32
        )
        number = lax.broadcasted_iota(jnp.int32, (chunk, GROUP), 0) + start
        kept = jnp.where(number == wanted, gram, 0.0)
        partial = partial + jnp.sum(kept.reshape(chunk // 8, 8, GROUP), axis=0)
    return jnp.sum(partial, axis=0, keepdims=True)


def last_kernel(columns, height, chunks, source, index, tiles, before, *refs):
    panels, (out, turned) = refs[: len(chunks)], refs[len(chunks) :]
    shard = panels[0].shape[0] // GROUP
    if before is not None:
        out[...] = before[...]
    for place, (chunk, panel) in enumerate(zip(chunks, panels)):

        def body(group, carry, place=place, chunk=chunk, panel=panel):
            rows = panel[pl.ds(pl.multiple_of(group * GROUP, GROUP), GROUP), :]
            across = transposed(rows)
            turned[place * shard + group] = across
            number = source[chunk] * shard + group
            weights = jnp.concatenate([across, across], axis=0)
            wanted = wanted_tile(index, number, columns, height)
            out[number] = kept_sum(tiles, tiles.shape[0] - 1, weights, wanted)
            return carry

        lax.fori_loop(0, shard, body, 0)


def early_kernel(columns, height, source, index, tiles, head, tail, out):
    shard = tail.shape[0]
    for turned, first in ((head, 0), (tail, head.shape[0])):

        def body(group, carry, turned=turned, first=first):
            chunk = first + group
            number = source[chunk // shard] * shard + lax.rem(chunk, shard)
            across = turned[group]
            weights = jnp.concatenate([across, across], axis=0)
            wanted = wanted_tile(index, number, columns, height)
            for step in range(out.shape[0]):
                out[step, number] = kept_sum(tiles, step, weights, wanted)
            return carry

        lax.fori_loop(0, turned.shape[0], body, 0)


def deposit_kernel(columns, height, source, index, parts, *refs):
    panels, (total, field, rightward, leftward, scaled, wanted) = refs[:-6], refs[-6:]
    groups = index.shape[0]
    shard = groups // len(panels)
    cells, per_plane = field.shape[0], field.shape[1]
    summed = parts[0]
    for part in range(1, parts.shape[0]):
        summed = summed + parts[part]
    total[...] = summed
    numbers = [source[g // shard] * shard + g % shard for g in range(groups)]
    drive = jnp.concatenate([total[number] for number in numbers], axis=0).T
    for group in range(groups):
        rows = panels[group // shard][pl.ds((group % shard) * GROUP, GROUP), :]
        head, tail = split(drive[:, group : group + 1] * rows.astype(jnp.float32))
        where = pl.ds(group * GROUP, GROUP)
        scaled[where, pl.ds(0, TILE)] = head
        scaled[where, pl.ds(TILE, TILE)] = tail
        wanted[group] = wanted_tile(index, numbers[group], columns, height)

    def body(plane, carry):
        number = lax.broadcasted_iota(jnp.int32, (per_plane, GROUP), 0) + plane * per_plane
        sums = jnp.zeros((per_plane, 2 * TILE), jnp.float32)
        for group in range(groups):
            chosen = jnp.where(number == wanted[group], 1.0, 0.0).astype(jnp.bfloat16)
            sums = sums + jnp.dot(
                chosen,
                scaled[pl.ds(group * GROUP, GROUP), :],
                preferred_element_type=jnp.float32,
            )
        value = sums[:, :TILE] + sums[:, TILE:]
        field[plane] = value
        head, tail = split(value)
        leftward[plane] = head
        rightward[plane] = head

        @pl.when(plane > 0)
        def _():
            rightward[cells + plane - 1] = tail

        return carry

    lax.fori_loop(0, cells, body, 0)


def call(kernel, out_shape, scratch=(), smem=0, inputs=0, flops=0):
    in_specs = [pl.BlockSpec(memory_space=pltpu.SMEM)] * smem
    in_specs += [pl.BlockSpec(memory_space=pltpu.VMEM)] * (inputs - smem)
    out_specs = jax.tree.map(lambda _: pl.BlockSpec(memory_space=pltpu.VMEM), out_shape)
    return pl.pallas_call(
        kernel,
        out_shape=out_shape,
        in_specs=in_specs,
        out_specs=out_specs,
        scratch_shapes=list(scratch),
        compiler_params=pltpu.CompilerParams(vmem_limit_bytes=VMEM_LIMIT),
        cost_estimate=pl.CostEstimate(flops=flops, bytes_accessed=4 * 1024 * 1024, transcendentals=0),
    )


def ring_order(count):
    return list(range(0, count, 2)) + [i for i in range(count - 1, 0, -1) if i % 2]


def tied(value, *others):
    return lax.optimization_barrier((value,) + others)[0]


def gathered(part, axis):
    count = lax.axis_size(axis)
    copies = jnp.broadcast_to(part[None], (count,) + part.shape)
    return lax.all_to_all(copies, axis, 0, 0)


def doubling_sum(part, axis):
    count = lax.axis_size(axis)
    if count & (count - 1):
        return lax.psum(part, axis)
    mask = 1
    while mask < count:
        part = part + lax.ppermute(part, axis, [(i, i ^ mask) for i in range(count)])
        mask *= 2
    return part


def local(sensor_field, courant, diffusivity, probe_offset, tile_index, actuator_panel):
    slabs, probes = lax.axis_size("state"), lax.axis_size("probe")
    own = sensor_field[0]
    cells, height, width = own.shape
    columns = width // TILE
    tile_total = cells * height * columns
    actuators = tile_index.shape[1]
    groups = actuators // GROUP
    shard = groups // probes
    planes = 3 * cells
    f32, bf16 = jnp.float32, jnp.bfloat16

    ring = ring_order(probes)
    hops = [(ring[i], ring[(i + 1) % probes]) for i in range(probes)]
    panels = [actuator_panel[0]]
    for _ in range(probes - 1):
        panels.append(lax.ppermute(panels[-1], "probe", hops))
    origin = np.zeros((probes, probes), np.int32)
    for spot, device in enumerate(ring):
        origin[device] = [ring[(spot - stage) % probes] for stage in range(probes)]
    source = jnp.asarray(origin)[lax.axis_index("probe")]
    low = lax.ppermute(own, "state", shift_pairs(slabs, 1))
    high = lax.ppermute(own, "state", shift_pairs(slabs, -1))

    coef = coefficients(courant, diffusivity)
    index = tile_index.reshape(groups, 1, GROUP)

    field_shape = pltpu.VMEM((planes, columns, height + 2 * PAD, TILE), f32)
    tiles = call(
        adjoint_kernel,
        jax.ShapeDtypeStruct((STEPS, tile_total, 2 * TILE), bf16),
        scratch=(field_shape, field_shape),
        smem=1,
        inputs=5,
        flops=28 * 16 * height * width,
    )(probe_offset, coef, own, low, high)

    row_shape = jax.ShapeDtypeStruct((groups, 1, GROUP), f32)
    step_flops = 2 * GROUP * tile_total * 2 * TILE
    early_chunks, late_chunks = list(range(probes - 1)), [probes - 1]

    def turned_shape(chunks):
        return jax.ShapeDtypeStruct((len(chunks) * shard, TILE, GROUP), bf16)

    before, head = call(
        lambda source, index, tiles, *refs: last_kernel(
            columns, height, early_chunks, source, index, tiles, None, *refs
        ),
        (row_shape, turned_shape(early_chunks)),
        smem=1,
        inputs=3 + len(early_chunks),
        flops=step_flops * shard * len(early_chunks),
    )(source, index, tiles, *panels[:-1])
    last, tail = call(
        lambda source, index, tiles, before, *refs: last_kernel(
            columns, height, late_chunks, source, index, tiles, before, *refs
        ),
        (row_shape, turned_shape(late_chunks)),
        smem=1,
        inputs=4 + len(late_chunks),
        flops=step_flops * shard,
    )(source, index, tiles, before, *panels[-1:])
    parts = gathered(last, "state")
    payload = jax.ShapeDtypeStruct((2 * cells - 1, height * columns, TILE), bf16)
    heads = jax.ShapeDtypeStruct((cells, height * columns, TILE), bf16)
    total, forced, rightward, leftward = call(
        lambda *refs: deposit_kernel(columns, height, *refs),
        (row_shape, jax.ShapeDtypeStruct((cells, height * columns, TILE), f32), payload, heads),
        scratch=(pltpu.VMEM((actuators, 2 * TILE), bf16), pltpu.VMEM((groups, 1, GROUP), jnp.int32)),
        smem=1,
        inputs=3 + probes,
        flops=step_flops * groups,
    )(source, index, parts, *panels)
    from_low = lax.ppermute(rightward, "state", shift_pairs(slabs, 1))
    from_high = lax.ppermute(leftward, "state", shift_pairs(slabs, -1))
    early = call(
        lambda *refs: early_kernel(columns, height, *refs),
        jax.ShapeDtypeStruct((STEPS - 1, groups, 1, GROUP), f32),
        smem=1,
        inputs=5,
        flops=step_flops * groups * (STEPS - 1),
    )(source, tied(index, forced), tiles, head, tail)
    early = doubling_sum(early, "state")
    response = call(
        forward_kernel,
        jax.ShapeDtypeStruct((cells, height, width), f32),
        scratch=(field_shape, field_shape),
        inputs=4,
        flops=28 * 16 * height * width,
    )(coef, forced, from_low, from_high)
    projections = jnp.concatenate([early, total[None]], axis=0)
    return projections.reshape(STEPS, 1, actuators), response[None]


def solution(mesh):
    return jax.shard_map(
        local,
        mesh=mesh,
        in_specs=(
            P("probe", "state", None, None),
            P(),
            P(),
            P("probe"),
            P("state", None),
            P("state", "probe", None),
        ),
        out_specs=(P(None, "probe", None), P("probe", "state", None, None)),
        check_vma=False,
    )
```

```python
import jax
import jax.numpy as jnp
from jax import lax
from jax.experimental import pallas as pl
from jax.experimental.pallas import tpu as pltpu
from jax.sharding import PartitionSpec as P

TILE = 128
STEPS = 4
PAD = 8
GROUP = 256
VMEM_LIMIT = 48 * 1024 * 1024


def shift_pairs(count, by):
    return [(i, (i + by) % count) for i in range(count)]


def clear_pads(buffer):
    planes, columns, rows, lanes = buffer.shape
    edge = jnp.zeros((columns, PAD, lanes), buffer.dtype)

    def body(plane, carry):
        buffer[plane, :, :PAD, :] = edge
        buffer[plane, :, rows - PAD :, :] = edge
        return carry

    lax.fori_loop(0, planes, body, 0)


def stencil_block(source, coef, plane, row, height, adjoint):
    centre = source[plane, :, pl.ds(PAD + row, height), :]
    above = source[plane, :, pl.ds(PAD + row + 1, height), :]
    below = source[plane, :, pl.ds(PAD + row - 1, height), :]
    upper_x = source[plane + 1, :, pl.ds(PAD + row, height), :]
    lower_x = source[plane - 1, :, pl.ds(PAD + row, height), :]
    columns = centre.shape[0]
    lane = lax.broadcasted_iota(jnp.int32, (height, TILE), 1)
    left = [pltpu.roll(centre[c], TILE - 1, 1) for c in range(columns)]
    right = [pltpu.roll(centre[c], 1, 1) for c in range(columns)]
    block = pl.ds(row, height)
    w_centre, w_up, w_diff = coef[0, block, :], coef[1, block, :], coef[2, block, :]
    out = []
    for c in range(columns):
        upper_z = jnp.where(lane == TILE - 1, left[(c + 1) % columns], left[c])
        lower_z = jnp.where(lane == 0, right[(c - 1) % columns], right[c])
        if adjoint:
            total = w_centre * centre[c] + w_up * upper_x[c]
            total = total + w_diff * (lower_x[c] + (upper_z + lower_z))
            total = total + coef[3, block, :] * above[c] + coef[4, block, :] * below[c]
        else:
            total = w_centre * centre[c] + w_up * lower_x[c]
            total = total + w_diff * ((upper_x[c] + (upper_z + lower_z)) + (above[c] + below[c]))
        out.append(total)
    return out


def split(value):
    high = value.astype(jnp.bfloat16)
    low = (value - high.astype(jnp.float32)).astype(jnp.bfloat16)
    return high, low


def shifted_plane(field, plane, offset):
    height, width = field.shape[1:]
    columns = width // TILE
    turn, rest = offset // TILE, offset % TILE
    lane = lax.broadcasted_iota(jnp.int32, (height, TILE), 1)
    rolled = [pltpu.roll(field[plane, :, pl.ds(c * TILE, TILE)], rest, 1) for c in range(columns)]
    return [
        (lax.rem(c + turn, columns), jnp.where(lane >= rest, rolled[c], rolled[c - 1]))
        for c in range(columns)
    ]


def prelude_kernel(columns, height, offset, field, courant, diffusivity, above, below, tile, own, coef, wanted):
    def load(plane, carry):
        for column, value in shifted_plane(field, plane, offset[0]):
            own[plane, column] = value
        return carry

    lax.fori_loop(0, field.shape[0], load, 0)
    rates = (
        1.0 - courant[...] - 6.0 * diffusivity[...],
        courant[...] + diffusivity[...],
        diffusivity[...],
        above[...],
        below[...],
    )
    for place, rate in enumerate(rates):
        coef[place] = jnp.broadcast_to(rate, coef.shape[1:])
    inside = tile[...] & (columns * height - 1)
    wanted[...] = (tile[...] - inside) + (inside & (columns - 1)) * height + inside // columns


def adjoint_kernel(offset, coef, own, low, high, tiles, first, second):
    cells, columns, height = own.shape[:3]
    steps = tiles.shape[0]
    inside = pl.ds(PAD, height)
    clear_pads(first)
    clear_pads(second)

    def load(plane, carry):
        for slab, field in ((0, low), (2, high)):
            for column, value in shifted_plane(field, plane, offset[0]):
                first[slab * cells + plane, column, inside, :] = value
        first[cells + plane, :, inside, :] = own[plane]
        return carry

    lax.fori_loop(0, cells, load, 0)
    buffers = (first, second)
    rows = 8
    for step in range(steps):
        source, target = buffers[step % 2], buffers[(step + 1) % 2]

        def sweep(plane, carry, source=source, target=target, step=step, keep=False):
            blocks = [
                stencil_block(source, coef, plane, row, rows, True)
                for row in range(0, height, rows)
            ]
            for c in range(columns):
                value = jnp.concatenate([block[c] for block in blocks], axis=0)
                target[plane, c, inside, :] = value
                if keep:
                    start = (plane - cells) * columns * height + c * height
                    where = pl.ds(pl.multiple_of(start, height), height)
                    head, tail = split(value)
                    tiles[step, where, pl.ds(0, TILE)] = head
                    tiles[step, where, pl.ds(TILE, TILE)] = tail
            return carry

        def inner(plane, carry, sweep=sweep):
            return sweep(plane, carry, keep=True)

        if step < steps - 1:
            lax.fori_loop(step + 1, cells, sweep, 0)
        lax.fori_loop(cells, 2 * cells, inner, 0)
        if step < steps - 1:
            lax.fori_loop(2 * cells, 3 * cells - step - 1, sweep, 0)


def forward_kernel(coef, own, low, high, out, first, second):
    cells, height, width = out.shape
    columns = width // TILE
    steps = STEPS
    clear_pads(first)
    clear_pads(second)
    for plane in range(cells):
        for c in range(columns):
            where = pl.ds(c * height, height)
            inside = pl.ds(PAD, height)
            first[cells + plane, c, inside, :] = own[plane, where, :]
            first[2 * cells + plane, c, inside, :] = high[plane, where, :].astype(jnp.float32)
            value = low[plane, where, :].astype(jnp.float32)
            if plane > 0:
                value = value + low[cells + plane - 1, where, :].astype(jnp.float32)
            first[plane, c, inside, :] = value
    buffers = (first, second)
    rows = 8
    for step in range(steps):
        source, target = buffers[step % 2], buffers[(step + 1) % 2]
        last = step == steps - 1

        def body(plane, carry, source=source, target=target, last=last):
            blocks = [
                stencil_block(source, coef, plane, row, rows, False)
                for row in range(0, height, rows)
            ]
            for c in range(columns):
                value = jnp.concatenate([block[c] for block in blocks], axis=0)
                if last:
                    out[plane - cells, :, pl.ds(c * TILE, TILE)] = value
                else:
                    target[plane, c, pl.ds(PAD, height), :] = value
            return carry

        lax.fori_loop(step + 1, 3 * cells - step - 1, body, 0)


def kept_sum(tiles, step, weights, wanted):
    chunk = 256
    partial = jnp.zeros((8, GROUP), jnp.float32)
    for start in range(0, tiles.shape[1], chunk):
        gram = lax.dot_general(
            tiles[step, pl.ds(start, chunk), :],
            weights,
            (((1,), (1,)), ((), ())),
            preferred_element_type=jnp.float32,
        )
        number = lax.broadcasted_iota(jnp.int32, (chunk, GROUP), 0) + start
        kept = jnp.where(number == wanted, gram, 0.0)
        partial = partial + jnp.sum(kept.reshape(chunk // 8, 8, GROUP), axis=0)
    return jnp.sum(partial, axis=0, keepdims=True)


def project_kernel(steps, chunks, source, wanted, tiles, *refs):
    panels, (*before, out) = refs[: len(chunks)], refs[len(chunks) :]
    shard = panels[0].shape[0] // GROUP
    for given in before:
        out[...] = given[...]
    for chunk, panel in zip(chunks, panels):

        def body(place, carry, chunk=chunk, panel=panel):
            step = steps[0] + place if len(steps) > 1 else steps[0]
            results = []
            for group in range(shard):
                rows = panel[pl.ds(group * GROUP, GROUP), :]
                number = source[chunk] * shard + group
                weights = jnp.concatenate([rows, rows], axis=1)
                results.append((number, kept_sum(tiles, step, weights, wanted[number])))
            for number, result in results:
                if len(steps) > 1:
                    out[place, number] = result
                else:
                    out[number] = result
            return carry

        if len(steps) > 1:
            lax.fori_loop(0, len(steps), body, 0)
        else:
            body(0, 0)


def deposit_kernel(count, source, wanted, *refs):
    parts, panels, (total, field, rightward, leftward, scaled) = refs[:count], refs[count:-5], refs[-5:]
    groups = wanted.shape[0]
    shard = groups // len(panels)
    cells, per_plane = field.shape[0], field.shape[1]
    total[...] = tree_sum([part[...] for part in parts])
    numbers = [source[g // shard] * shard + g % shard for g in range(groups)]
    drive = jnp.concatenate([total[number] for number in numbers], axis=0).T
    for group in range(groups):
        rows = panels[group // shard][pl.ds((group % shard) * GROUP, GROUP), :]
        head, tail = split(drive[:, group : group + 1] * rows.astype(jnp.float32))
        where = pl.ds(group * GROUP, GROUP)
        scaled[where, pl.ds(0, TILE)] = head
        scaled[where, pl.ds(TILE, TILE)] = tail

    def body(plane, carry):
        number = lax.broadcasted_iota(jnp.int32, (per_plane, GROUP), 0) + plane * per_plane
        sums = jnp.zeros((per_plane, 2 * TILE), jnp.float32)
        for group in range(groups):
            chosen = jnp.where(number == wanted[numbers[group]], 1.0, 0.0).astype(jnp.bfloat16)
            sums = sums + jnp.dot(
                chosen,
                scaled[pl.ds(group * GROUP, GROUP), :],
                preferred_element_type=jnp.float32,
            )
        value = sums[:, :TILE] + sums[:, TILE:]
        field[plane] = value
        head, tail = split(value)
        leftward[plane] = head
        rightward[plane] = head

        @pl.when(plane > 0)
        def _():
            rightward[cells + plane - 1] = tail

        return carry

    lax.fori_loop(0, cells, body, 0)


def call(kernel, out_shape, scratch=(), smem=0, inputs=0, flops=0):
    in_specs = [pl.BlockSpec(memory_space=pltpu.SMEM)] * smem
    in_specs += [pl.BlockSpec(memory_space=pltpu.VMEM)] * (inputs - smem)
    out_specs = jax.tree.map(lambda _: pl.BlockSpec(memory_space=pltpu.VMEM), out_shape)
    return pl.pallas_call(
        kernel,
        out_shape=out_shape,
        in_specs=in_specs,
        out_specs=out_specs,
        scratch_shapes=list(scratch),
        compiler_params=pltpu.CompilerParams(vmem_limit_bytes=VMEM_LIMIT),
        cost_estimate=pl.CostEstimate(
            flops=flops, bytes_accessed=1024 * 1024 if flops else 1024, transcendentals=0
        ),
    )


def gathered_panel(panel, axis):
    count = lax.axis_size(axis)
    shards = {0: panel}
    mask = count // 2
    while mask:
        pairs = [(i, i ^ mask) for i in range(count)]
        for held in sorted(shards):
            shards[held | mask] = lax.ppermute(shards[held], axis, pairs)
        mask //= 2
    return [shards[k] for k in range(count)]


def tied(value, *others):
    return lax.optimization_barrier((value,) + others)[0]


def tree_sum(parts):
    while len(parts) > 1:
        parts = [parts[i] + parts[i + 1] for i in range(0, len(parts), 2)]
    return parts[0]


def summands(part, axis):
    count = lax.axis_size(axis)
    if count & (count - 1):
        return [lax.psum(part, axis)]
    done, parts = 1, [part]
    for span in (2, 4, 4, 4, 4):
        span = min(span, count // done)
        if span > 1:
            part = tree_sum(parts)
            pairs = [[(i, i ^ (k * done)) for i in range(count)] for k in range(1, span)]
            parts = [part] + [lax.ppermute(part, axis, pair) for pair in pairs]
            done *= span
    return parts


def doubling_sum(part, axis):
    count = lax.axis_size(axis)
    if count & (count - 1):
        return lax.psum(part, axis)
    mask = 1
    while mask < count:
        part = part + lax.ppermute(part, axis, [(i, i ^ mask) for i in range(count)])
        mask *= 2
    return part


def local(sensor_field, courant, diffusivity, probe_offset, tile_index, actuator_panel):
    slabs, probes = lax.axis_size("state"), lax.axis_size("probe")
    own = sensor_field[0]
    cells, height, width = own.shape
    columns = width // TILE
    tile_total = cells * height * columns
    actuators = tile_index.shape[1]
    groups = actuators // GROUP
    shard = groups // probes
    planes = 3 * cells
    f32, bf16 = jnp.float32, jnp.bfloat16

    panels = gathered_panel(actuator_panel[0], "probe")
    source = lax.axis_index("probe") ^ jnp.arange(probes, dtype=jnp.int32)
    low = lax.ppermute(own, "state", shift_pairs(slabs, 1))
    high = lax.ppermute(own, "state", shift_pairs(slabs, -1))

    zero = jnp.zeros((1,), f32)
    rates = [
        courant,
        diffusivity,
        jnp.concatenate([diffusivity[1:], zero]),
        jnp.concatenate([zero, diffusivity[:-1]]),
    ]
    shifted, coef, wanted = call(
        lambda *refs: prelude_kernel(columns, height, *refs),
        (
            jax.ShapeDtypeStruct((cells, columns, height, TILE), f32),
            jax.ShapeDtypeStruct((5, height, TILE), f32),
            jax.ShapeDtypeStruct((groups, 1, GROUP), jnp.int32),
        ),
        smem=1,
        inputs=7,
    )(probe_offset, own, *[rate[:, None] for rate in rates], tile_index.reshape(groups, 1, GROUP))

    field_shape = pltpu.VMEM((planes, columns, height + 2 * PAD, TILE), f32)
    tiles = call(
        adjoint_kernel,
        jax.ShapeDtypeStruct((STEPS, tile_total, 2 * TILE), bf16),
        scratch=(field_shape, field_shape),
        smem=1,
        inputs=5,
        flops=28 * 16 * height * width,
    )(probe_offset, coef, shifted, low, high)

    row_shape = jax.ShapeDtypeStruct((groups, 1, GROUP), f32)
    step_flops = 2 * GROUP * tile_total * 2 * TILE
    every = list(range(probes))
    before = call(
        lambda *refs: project_kernel([STEPS - 1], every[:-1], *refs),
        row_shape,
        smem=1,
        inputs=2 + probes,
        flops=step_flops * shard * (probes - 1),
    )(source, wanted, tiles, *panels[:-1])
    last = call(
        lambda *refs: project_kernel([STEPS - 1], every[-1:], *refs),
        row_shape,
        smem=1,
        inputs=5,
        flops=step_flops * shard,
    )(source, wanted, tiles, panels[-1], before)
    parts = summands(last, "state")
    payload = jax.ShapeDtypeStruct((2 * cells - 1, height * columns, TILE), bf16)
    heads = jax.ShapeDtypeStruct((cells, height * columns, TILE), bf16)
    total, forced, rightward, leftward = call(
        lambda *refs: deposit_kernel(len(parts), *refs),
        (row_shape, jax.ShapeDtypeStruct((cells, height * columns, TILE), f32), payload, heads),
        scratch=(pltpu.VMEM((actuators, 2 * TILE), bf16),),
        smem=1,
        inputs=2 + len(parts) + probes,
        flops=step_flops * groups,
    )(source, wanted, *parts, *panels)
    from_low = lax.ppermute(rightward, "state", shift_pairs(slabs, 1))
    from_high = lax.ppermute(leftward, "state", shift_pairs(slabs, -1))
    early = call(
        lambda *refs: project_kernel(list(range(STEPS - 1)), every, *refs),
        jax.ShapeDtypeStruct((STEPS - 1, groups, 1, GROUP), f32),
        smem=1,
        inputs=3 + probes,
    )(source, tied(wanted, forced), tiles, *panels)
    rounds = 1 + jnp.minimum(probe_offset[0], 0)
    early = lax.fori_loop(0, rounds, lambda _, part: doubling_sum(part, "state"), early)
    response = call(
        forward_kernel,
        jax.ShapeDtypeStruct((cells, height, width), f32),
        scratch=(field_shape, field_shape),
        inputs=4,
        flops=28 * 16 * height * width,
    )(coef, forced, from_low, from_high)
    projections = jnp.concatenate([early, total[None]], axis=0)
    return projections.reshape(STEPS, 1, actuators), response[None]


def solution(mesh):
    return jax.shard_map(
        local,
        mesh=mesh,
        in_specs=(
            P("probe", "state", None, None),
            P(),
            P(),
            P("probe"),
            P("state", None),
            P("state", "probe", None),
        ),
        out_specs=(P(None, "probe", None), P("probe", "state", None, None)),
        check_vma=False,
    )
```

```python
import jax
import jax.numpy as jnp
from jax import lax
from jax.experimental import pallas as pl
from jax.experimental.pallas import tpu as pltpu
from jax.sharding import PartitionSpec as P

TILE = 128
STEPS = 4
PAD = 8
GROUP = 256
VMEM_LIMIT = 24 * 1024 * 1024


def shift_pairs(count, by):
    return [(i, (i + by) % count) for i in range(count)]


def clear_pads(buffer):
    planes, columns, rows, lanes = buffer.shape
    edge = jnp.zeros((columns, PAD, lanes), buffer.dtype)

    def body(plane, carry):
        buffer[plane, :, :PAD, :] = edge
        buffer[plane, :, rows - PAD :, :] = edge
        return carry

    lax.fori_loop(0, planes, body, 0)


def sweep_rows(source, coef, planes, row, adjoint):
    here = pl.ds(pl.multiple_of(PAD + row, 8), 8)
    block = pl.ds(pl.multiple_of(row, 8), 8)
    columns = source.shape[1]
    lane = lax.broadcasted_iota(jnp.int32, (8, TILE), 1)
    weights = [coef[place, block, :] for place in range(5)]
    lower, centre = source[planes[0] - 1, :, here, :], source[planes[0], :, here, :]
    out = []
    for plane in planes:
        upper = source[plane + 1, :, here, :]
        above = source[plane, :, pl.ds(PAD + row + 1, 8), :]
        below = source[plane, :, pl.ds(PAD + row - 1, 8), :]
        left = [pltpu.roll(centre[c], TILE - 1, 1) for c in range(columns)]
        right = [pltpu.roll(centre[c], 1, 1) for c in range(columns)]
        results = []
        for c in range(columns):
            upper_z = jnp.where(lane == TILE - 1, left[(c + 1) % columns], left[c])
            lower_z = jnp.where(lane == 0, right[(c - 1) % columns], right[c])
            total = weights[0] * centre[c]
            if adjoint:
                total = total + weights[1] * upper[c]
                total = total + weights[2] * (lower[c] + (upper_z + lower_z))
                total = total + (weights[3] * above[c] + weights[4] * below[c])
            else:
                total = total + weights[1] * lower[c]
                total = total + weights[2] * ((upper[c] + (upper_z + lower_z)) + (above[c] + below[c]))
            results.append(total)
        out.append(results)
        lower, centre = centre, upper
    return out


def split(value):
    high = value.astype(jnp.bfloat16)
    low = (value - high.astype(jnp.float32)).astype(jnp.bfloat16)
    return high, low


def shifted_plane(field, plane, offset):
    height, width = field.shape[1:]
    columns = width // TILE
    turn, rest = offset // TILE, offset % TILE
    lane = lax.broadcasted_iota(jnp.int32, (height, TILE), 1)
    rolled = [pltpu.roll(field[plane, :, pl.ds(c * TILE, TILE)], rest, 1) for c in range(columns)]
    return [
        (lax.rem(c + turn, columns), jnp.where(lane >= rest, rolled[c], rolled[c - 1]))
        for c in range(columns)
    ]


def prelude_kernel(columns, height, offset, field, courant, diffusivity, above, below, tile, panel, own, coef, pick, chosen, kept):
    def load(plane, carry):
        for column, value in shifted_plane(field, plane, offset[0]):
            own[plane, column] = value
        return carry

    lax.fori_loop(0, field.shape[0], load, 0)
    rates = (
        1.0 - courant[...] - 6.0 * diffusivity[...],
        courant[...] + diffusivity[...],
        diffusivity[...],
        above[...],
        below[...],
    )
    for place, rate in enumerate(rates):
        coef[place] = jnp.broadcast_to(rate, coef.shape[1:])
    kept[...] = panel[...]
    numbers = tile[...]
    inside = numbers & (columns * height - 1)
    numbers = (numbers - inside) + (inside & (columns - 1)) * height + inside // columns
    upright = numbers.astype(jnp.float32).T.astype(jnp.int32)
    groups, total = numbers.shape[0], pick.shape[1]
    by_lane = lax.broadcasted_iota(jnp.int32, (GROUP, total), 1)
    by_row = lax.broadcasted_iota(jnp.int32, (total, GROUP), 0)
    for group in range(groups):
        block = pl.ds(group * GROUP, GROUP)
        found = jnp.where(upright[:, group : group + 1] == by_lane, 1.0, 0.0)
        pick[block, :] = found.astype(jnp.bfloat16)
        found = jnp.where(numbers[group : group + 1, :] == by_row, 1.0, 0.0)
        chosen[:, block] = found.astype(jnp.bfloat16)


def adjoint_kernel(offset, coef, own, low, high, tiles, first, second):
    cells, columns, height = own.shape[:3]
    steps = tiles.shape[1] // (2 * TILE)
    inside = pl.ds(PAD, height)
    clear_pads(first)
    clear_pads(second)

    def load(plane, carry):
        for slab, field in ((0, low), (2, high)):
            for column, value in shifted_plane(field, plane, offset[0]):
                first[slab * cells + plane, column, inside, :] = value
        first[cells + plane, :, inside, :] = own[plane]
        return carry

    lax.fori_loop(0, cells, load, 0)
    buffers = (first, second)
    for step in range(steps):
        source, target = buffers[step % 2], buffers[(step + 1) % 2]

        def sweep(place, carry, source=source, target=target, step=step):
            planes = range(step + 1, 3 * cells - step - 1)
            halves = []
            for half in range(2):
                row = place * 16 + half * 8
                blocks = sweep_rows(source, coef, planes, row, True)
                halves.append(blocks)
                if step < steps - 1:
                    for plane, block in zip(planes, blocks):
                        for c in range(columns):
                            where = pl.ds(pl.multiple_of(PAD + row, 8), 8)
                            target[plane, c, where, :] = block[c]
            for plane, upper, lower in zip(planes, *halves):
                if cells <= plane < 2 * cells:
                    for c in range(columns):
                        start = (plane - cells) * columns * height + c * height + place * 16
                        where = pl.ds(pl.multiple_of(start, 16), 16)
                        head, tail = split(jnp.concatenate([upper[c], lower[c]], axis=0))
                        tiles[where, pl.ds(2 * step * TILE, TILE)] = head
                        tiles[where, pl.ds((2 * step + 1) * TILE, TILE)] = tail
            return carry

        lax.fori_loop(0, height // 16, sweep, 0)


def forward_kernel(coef, own, low, high, out, first, second):
    cells, height, width = out.shape
    columns = width // TILE
    steps = STEPS
    clear_pads(first)
    clear_pads(second)
    for plane in range(cells):
        for c in range(columns):
            where = pl.ds(c * height, height)
            inside = pl.ds(PAD, height)
            first[cells + plane, c, inside, :] = own[plane, where, :]
            first[2 * cells + plane, c, inside, :] = high[plane, where, :].astype(jnp.float32)
            value = low[plane, where, :].astype(jnp.float32)
            if plane > 0:
                value = value + low[cells + plane - 1, where, :].astype(jnp.float32)
            first[plane, c, inside, :] = value
    buffers = (first, second)
    for step in range(steps):
        source, target = buffers[step % 2], buffers[(step + 1) % 2]

        def sweep(place, carry, source=source, target=target, step=step):
            planes = range(step + 1, 3 * cells - step - 1)
            row = place * 8
            for plane, block in zip(planes, sweep_rows(source, coef, planes, row, False)):
                for c in range(columns):
                    if step == steps - 1:
                        where = pl.ds(pl.multiple_of(row, 8), 8)
                        out[plane - cells, where, pl.ds(c * TILE, TILE)] = block[c]
                    else:
                        target[plane, c, pl.ds(pl.multiple_of(PAD + row, 8), 8), :] = block[c]
            return carry

        lax.fori_loop(0, height // 8, sweep, 0)


def project_kernel(first, count, chunks, source, pick, tiles, *refs):
    panels, (*before, out) = refs[: len(chunks)], refs[len(chunks) :]
    shard = panels[0].shape[0] // GROUP
    for given in before:
        out[...] = given[...]
    ones = jnp.ones((8, 2 * TILE), jnp.bfloat16)
    weights = tiles[:, pl.ds(2 * first * TILE, 2 * count * TILE)]
    for chunk, panel in zip(chunks, panels):

        def body(group, carry, chunk=chunk, panel=panel):
            number = source[chunk] * shard + group
            chosen = pick[pl.ds(pl.multiple_of(number * GROUP, GROUP), GROUP), :]
            found = jnp.dot(chosen, weights, preferred_element_type=jnp.float32)
            rows = panel[pl.ds(pl.multiple_of(group * GROUP, GROUP), GROUP), :].astype(jnp.float32)
            for step in range(count):
                start = 2 * step * TILE
                cells = found[:, start : start + TILE] + found[:, start + TILE : start + 2 * TILE]
                both = jnp.concatenate(split(cells * rows), axis=1)
                sums = lax.dot_general(
                    ones, both, (((1,), (1,)), ((), ())), preferred_element_type=jnp.float32
                )
                out[step, number] = sums[:1]
            return carry

        lax.fori_loop(0, shard, body, 0, unroll=2 if count > 1 and shard % 2 == 0 else shard)


def deposit_kernel(count, source, chosen, *refs):
    parts, panels, (total, field, rightward, leftward, scaled) = refs[:count], refs[count:-5], refs[-5:]
    groups = total.shape[1]
    shard = groups // len(panels)
    cells, per_plane = field.shape[0], field.shape[1]
    total[...] = tree_sum([part[...] for part in parts])
    numbers = [source[g // shard] * shard + g % shard for g in range(groups)]
    drive = jnp.concatenate([total[0, number] for number in numbers], axis=0).T
    for group, number in enumerate(numbers):
        rows = panels[group // shard][pl.ds((group % shard) * GROUP, GROUP), :]
        head, tail = split(drive[:, group : group + 1] * rows.astype(jnp.float32))
        where = pl.ds(pl.multiple_of(number * GROUP, GROUP), GROUP)
        scaled[where, pl.ds(0, TILE)] = head
        scaled[where, pl.ds(TILE, TILE)] = tail

    for plane in range(cells):
        sums = jnp.dot(
            chosen[pl.ds(plane * per_plane, per_plane), :],
            scaled[...],
            preferred_element_type=jnp.float32,
        )
        value = sums[:, :TILE] + sums[:, TILE:]
        field[plane] = value
        head, tail = split(value)
        leftward[plane] = head
        rightward[plane] = head
        if plane > 0:
            rightward[cells + plane - 1] = tail


def call(kernel, out_shape, scratch=(), smem=0, inputs=0):
    in_specs = [pl.BlockSpec(memory_space=pltpu.SMEM)] * smem
    in_specs += [pl.BlockSpec(memory_space=pltpu.VMEM)] * (inputs - smem)
    out_specs = jax.tree.map(lambda _: pl.BlockSpec(memory_space=pltpu.VMEM), out_shape)
    return pl.pallas_call(
        kernel,
        out_shape=out_shape,
        in_specs=in_specs,
        out_specs=out_specs,
        scratch_shapes=list(scratch),
        compiler_params=pltpu.CompilerParams(vmem_limit_bytes=VMEM_LIMIT),
        cost_estimate=pl.CostEstimate(flops=1024, bytes_accessed=1024, transcendentals=0),
    )


def gathered_panel(panel, axis, ready):
    count = lax.axis_size(axis)
    shards = {0: panel}
    mask = count // 2
    while mask:
        pairs = [(i, i ^ mask) for i in range(count)]
        for held in sorted(shards):
            operand = panel if len(shards) == 1 else tied(shards[held], ready)
            shards[held | mask] = lax.ppermute(operand, axis, pairs)
        mask //= 2
    return [shards[k] for k in range(1, count)]


def tied(value, *others):
    return lax.optimization_barrier((value,) + others)[0]


def tree_sum(parts):
    while len(parts) > 1:
        parts = [parts[i] + parts[i + 1] for i in range(0, len(parts), 2)]
    return parts[0]


def summands(part, axis):
    count = lax.axis_size(axis)
    if count & (count - 1):
        return [lax.psum(part, axis)]
    done, parts = 1, [part]
    for span in (2, 4, 4, 4, 4):
        span = min(span, count // done)
        if span > 1:
            part = tree_sum(parts)
            pairs = [[(i, i ^ (k * done)) for i in range(count)] for k in range(1, span)]
            parts = [part] + [lax.ppermute(part, axis, pair) for pair in pairs]
            done *= span
    return parts


def doubling_sum(part, axis):
    count = lax.axis_size(axis)
    if count & (count - 1):
        return lax.psum(part, axis)
    mask = 1
    while mask < count:
        part = part + lax.ppermute(part, axis, [(i, i ^ mask) for i in range(count)])
        mask *= 2
    return part


def local(sensor_field, courant, diffusivity, probe_offset, tile_index, actuator_panel):
    slabs, probes = lax.axis_size("state"), lax.axis_size("probe")
    own = sensor_field[0]
    cells, height, width = own.shape
    columns = width // TILE
    tile_total = cells * height * columns
    actuators = tile_index.shape[1]
    groups = actuators // GROUP
    shard = groups // probes
    planes = 3 * cells
    f32, bf16 = jnp.float32, jnp.bfloat16

    source = lax.axis_index("probe") ^ jnp.arange(probes, dtype=jnp.int32)
    low = lax.ppermute(own, "state", shift_pairs(slabs, 1))
    high = lax.ppermute(own, "state", shift_pairs(slabs, -1))

    zero = jnp.zeros((1,), f32)
    rates = [
        courant,
        diffusivity,
        jnp.concatenate([diffusivity[1:], zero]),
        jnp.concatenate([zero, diffusivity[:-1]]),
    ]
    shifted, coef, pick, chosen, panel = call(
        lambda *refs: prelude_kernel(columns, height, *refs),
        (
            jax.ShapeDtypeStruct((cells, columns, height, TILE), f32),
            jax.ShapeDtypeStruct((5, height, TILE), f32),
            jax.ShapeDtypeStruct((actuators, tile_total), bf16),
            jax.ShapeDtypeStruct((tile_total, actuators), bf16),
            jax.ShapeDtypeStruct(actuator_panel.shape[1:], bf16),
        ),
        smem=1,
        inputs=8,
    )(
        probe_offset,
        own,
        *[rate[:, None] for rate in rates],
        tile_index.reshape(groups, GROUP),
        actuator_panel[0],
    )
    panels = [panel] + gathered_panel(actuator_panel[0], "probe", coef)

    field_shape = pltpu.VMEM((planes, columns, height + 2 * PAD, TILE), f32)
    tiles = call(
        adjoint_kernel,
        jax.ShapeDtypeStruct((tile_total, 2 * STEPS * TILE), bf16),
        scratch=(field_shape, field_shape),
        smem=1,
        inputs=5,
    )(probe_offset, coef, shifted, low, high)

    every = list(range(probes))

    def project(first, count, chunks, *given):
        return call(
            lambda *refs: project_kernel(first, count, chunks, *refs),
            jax.ShapeDtypeStruct((count, groups, 1, GROUP), f32),
            smem=1,
            inputs=3 + len(chunks) + len(given),
        )

    before = project(STEPS - 1, 1, every[:-1])(source, pick, tiles, *panels[:-1])
    last = project(STEPS - 1, 1, every[-1:], before)(source, pick, tiles, panels[-1], before)
    parts = summands(last, "state")
    payload = jax.ShapeDtypeStruct((2 * cells - 1, height * columns, TILE), bf16)
    heads = jax.ShapeDtypeStruct((cells, height * columns, TILE), bf16)
    total, forced, rightward, leftward = call(
        lambda *refs: deposit_kernel(len(parts), *refs),
        (
            jax.ShapeDtypeStruct(last.shape, f32),
            jax.ShapeDtypeStruct((cells, height * columns, TILE), f32),
            payload,
            heads,
        ),
        scratch=(pltpu.VMEM((actuators, 2 * TILE), bf16),),
        smem=1,
        inputs=2 + len(parts) + probes,
    )(source, chosen, *parts, *panels)
    from_low = lax.ppermute(rightward, "state", shift_pairs(slabs, 1))
    from_high = lax.ppermute(leftward, "state", shift_pairs(slabs, -1))
    early = project(0, STEPS - 1, every)(tied(source, forced), pick, tiles, *panels)
    rounds = 1 + jnp.minimum(probe_offset[0], 0)
    early = lax.fori_loop(0, rounds, lambda _, part: doubling_sum(part, "state"), early)
    response = call(
        forward_kernel,
        jax.ShapeDtypeStruct((cells, height, width), f32),
        scratch=(field_shape, field_shape),
        inputs=4,
    )(coef, forced, from_low, from_high)
    projections = jnp.concatenate([early, total], axis=0)
    return projections.reshape(STEPS, 1, actuators), response[None]


def solution(mesh):
    return jax.shard_map(
        local,
        mesh=mesh,
        in_specs=(
            P("probe", "state", None, None),
            P(),
            P(),
            P("probe"),
            P("state", None),
            P("state", "probe", None),
        ),
        out_specs=(P(None, "probe", None), P("probe", "state", None, None)),
        check_vma=False,
    )
```

```python
import jax
import jax.numpy as jnp
from jax import lax
from jax.experimental import pallas as pl
from jax.experimental.pallas import tpu as pltpu
from jax.sharding import PartitionSpec as P

TILE = 128
STEPS = 4
PAD = 8
GROUP = 256
VMEM_LIMIT = 24 * 1024 * 1024


def shift_pairs(count, by):
    return [(i, (i + by) % count) for i in range(count)]


def clear_pads(buffer):
    planes, columns, rows, lanes = buffer.shape
    edge = jnp.zeros((columns, PAD, lanes), buffer.dtype)

    def body(plane, carry):
        buffer[plane, :, :PAD, :] = edge
        buffer[plane, :, rows - PAD :, :] = edge
        return carry

    lax.fori_loop(0, planes, body, 0)


def sweep_rows(source, coef, planes, row, adjoint):
    here = pl.ds(pl.multiple_of(PAD + row, 8), 8)
    block = pl.ds(pl.multiple_of(row, 8), 8)
    columns = source.shape[1]
    lane = lax.broadcasted_iota(jnp.int32, (8, TILE), 1)
    weights = [coef[place, block, :] for place in range(5)]
    lower, centre = source[planes[0] - 1, :, here, :], source[planes[0], :, here, :]
    out = []
    for plane in planes:
        upper = source[plane + 1, :, here, :]
        above = source[plane, :, pl.ds(PAD + row + 1, 8), :]
        below = source[plane, :, pl.ds(PAD + row - 1, 8), :]
        left = [pltpu.roll(centre[c], TILE - 1, 1) for c in range(columns)]
        right = [pltpu.roll(centre[c], 1, 1) for c in range(columns)]
        results = []
        for c in range(columns):
            upper_z = jnp.where(lane == TILE - 1, left[(c + 1) % columns], left[c])
            lower_z = jnp.where(lane == 0, right[(c - 1) % columns], right[c])
            total = weights[0] * centre[c]
            if adjoint:
                total = total + weights[1] * upper[c]
                total = total + weights[2] * (lower[c] + (upper_z + lower_z))
                total = total + (weights[3] * above[c] + weights[4] * below[c])
            else:
                total = total + weights[1] * lower[c]
                total = total + weights[2] * ((upper[c] + (upper_z + lower_z)) + (above[c] + below[c]))
            results.append(total)
        out.append(results)
        lower, centre = centre, upper
    return out


def split(value):
    high = value.astype(jnp.bfloat16)
    low = (value - high.astype(jnp.float32)).astype(jnp.bfloat16)
    return high, low


def shifted_plane(field, plane, offset):
    height, width = field.shape[1:]
    columns = width // TILE
    turn, rest = offset // TILE, offset % TILE
    lane = lax.broadcasted_iota(jnp.int32, (height, TILE), 1)
    rolled = [pltpu.roll(field[plane, :, pl.ds(c * TILE, TILE)], rest, 1) for c in range(columns)]
    return [
        (lax.rem(c + turn, columns), jnp.where(lane >= rest, rolled[c], rolled[c - 1]))
        for c in range(columns)
    ]


def prelude_kernel(columns, height, offset, field, courant, diffusivity, above, below, tile, panel, own, coef, start, chosen, kept):
    def load(plane, carry):
        for column, value in shifted_plane(field, plane, offset[0]):
            own[plane, column] = value
        return carry

    lax.fori_loop(0, field.shape[0], load, 0)
    rates = (
        1.0 - courant[...] - 6.0 * diffusivity[...],
        courant[...] + diffusivity[...],
        diffusivity[...],
        above[...],
        below[...],
    )
    for place, rate in enumerate(rates):
        coef[place] = jnp.broadcast_to(rate, coef.shape[1:])
    kept[...] = panel[...]
    numbers = tile[...]
    inside = numbers & (columns * height - 1)
    numbers = (numbers - inside) + (inside & (columns - 1)) * height + inside // columns
    start[...] = numbers * STEPS
    by_row = lax.broadcasted_iota(jnp.int32, (chosen.shape[0], GROUP), 0)
    for group in range(numbers.shape[0]):
        found = jnp.where(numbers[group : group + 1, :] == by_row, 1.0, 0.0)
        chosen[:, pl.ds(group * GROUP, GROUP)] = found.astype(jnp.bfloat16)


def adjoint_kernel(offset, coef, own, low, high, tiles, first, second):
    cells, columns, height = own.shape[:3]
    steps = STEPS
    edge = jnp.zeros((PAD, TILE), jnp.float32)
    tiles[:PAD, :] = edge
    tiles[tiles.shape[0] - PAD :, :] = edge
    inside = pl.ds(PAD, height)
    clear_pads(first)
    clear_pads(second)

    def load(plane, carry):
        for slab, field in ((0, low), (2, high)):
            for column, value in shifted_plane(field, plane, offset[0]):
                first[slab * cells + plane, column, inside, :] = value
        first[cells + plane, :, inside, :] = own[plane]
        return carry

    lax.fori_loop(0, cells, load, 0)
    buffers = (first, second)
    for step in range(steps):
        source, target = buffers[step % 2], buffers[(step + 1) % 2]

        def sweep(place, carry, source=source, target=target, step=step):
            planes = range(step + 1, 3 * cells - step - 1)
            row = place * 8
            for plane, block in zip(planes, sweep_rows(source, coef, planes, row, True)):
                for c in range(columns):
                    if step < steps - 1:
                        where = pl.ds(pl.multiple_of(PAD + row, 8), 8)
                        target[plane, c, where, :] = block[c]
                    if cells <= plane < 2 * cells:
                        number = ((plane - cells) * columns + c) * height + row
                        tiles[pl.ds(PAD + number * steps + step, 8, stride=steps), :] = block[c]
            return carry

        lax.fori_loop(0, height // 8, sweep, 0)


def forward_kernel(coef, own, low, high, out, first, second):
    cells, height, width = out.shape
    columns = width // TILE
    steps = STEPS
    clear_pads(first)
    clear_pads(second)
    for plane in range(cells):
        for c in range(columns):
            where = pl.ds(c * height, height)
            inside = pl.ds(PAD, height)
            first[cells + plane, c, inside, :] = own[plane, where, :]
            first[2 * cells + plane, c, inside, :] = high[plane, where, :].astype(jnp.float32)
            value = low[plane, where, :].astype(jnp.float32)
            if plane > 0:
                value = value + low[cells + plane - 1, where, :].astype(jnp.float32)
            first[plane, c, inside, :] = value
    buffers = (first, second)
    for step in range(steps):
        source, target = buffers[step % 2], buffers[(step + 1) % 2]

        def sweep(place, carry, source=source, target=target, step=step):
            planes = range(step + 1, 3 * cells - step - 1)
            row = place * 8
            for plane, block in zip(planes, sweep_rows(source, coef, planes, row, False)):
                for c in range(columns):
                    if step == steps - 1:
                        where = pl.ds(pl.multiple_of(row, 8), 8)
                        out[plane - cells, where, pl.ds(c * TILE, TILE)] = block[c]
                    else:
                        target[plane, c, pl.ds(pl.multiple_of(PAD + row, 8), 8), :] = block[c]
            return carry

        lax.fori_loop(0, height // 8, sweep, 0)


def project_kernel(chunks, source, start, tiles, *refs):
    panels, (*before, out, wide) = refs[: len(chunks)], refs[len(chunks) :]
    shard = panels[0].shape[0] // GROUP
    for given in before:
        out[...] = given[...]
    first = lax.broadcasted_iota(jnp.int32, (8, TILE), 0) < STEPS
    lane = lax.broadcasted_iota(jnp.int32, (8, TILE), 1)
    for chunk, panel in zip(chunks, panels):
        wide[...] = panel[...].astype(jnp.float32)

        def body(group, carry, chunk=chunk):
            number = source[chunk] * shard + group
            sums = jnp.zeros((8, TILE), jnp.float32)
            for place in range(TILE):
                left, right = start[number, place], start[number, TILE + place]
                cells = jnp.where(
                    first, tiles[pl.ds(PAD + left, 8), :], tiles[pl.ds(PAD - STEPS + right, 8), :]
                )
                row = group * GROUP + place
                rows = jnp.where(first, wide[pl.ds(row, 1), :], wide[pl.ds(row + TILE, 1), :])
                total = jnp.sum(cells * rows, axis=1, keepdims=True)
                sums = jnp.where(lane == place, total, sums)
            out[number] = sums
            return carry

        lax.fori_loop(0, shard, body, 0)


def deposit_kernel(count, source, chosen, *refs):
    parts, panels, (total, field, rightward, leftward, scaled) = refs[:count], refs[count:-5], refs[-5:]
    groups = total.shape[0]
    shard = groups // len(panels)
    cells, per_plane = field.shape[0], field.shape[1]
    total[...] = tree_sum([part[...] for part in parts])
    numbers = [source[g // shard] * shard + g % shard for g in range(groups)]
    last = [total[n, pl.ds(half * STEPS + STEPS - 1, 1), :] for n in numbers for half in range(2)]
    drive = jnp.concatenate(last, axis=0).T
    for group, number in enumerate(numbers):
        for half in range(2):
            place = 2 * group + half
            rows = panels[group // shard][pl.ds((group % shard) * GROUP + half * TILE, TILE), :]
            head, tail = split(drive[:, place : place + 1] * rows.astype(jnp.float32))
            where = pl.ds(pl.multiple_of(number * GROUP + half * TILE, TILE), TILE)
            scaled[where, pl.ds(0, TILE)] = head
            scaled[where, pl.ds(TILE, TILE)] = tail

    for plane in range(cells):
        sums = jnp.dot(
            chosen[pl.ds(plane * per_plane, per_plane), :],
            scaled[...],
            preferred_element_type=jnp.float32,
        )
        value = sums[:, :TILE] + sums[:, TILE:]
        field[plane] = value
        head, tail = split(value)
        leftward[plane] = head
        rightward[plane] = head
        if plane > 0:
            rightward[cells + plane - 1] = tail


def call(kernel, out_shape, scratch=(), smem=0, inputs=0):
    in_specs = [pl.BlockSpec(memory_space=pltpu.SMEM)] * smem
    in_specs += [pl.BlockSpec(memory_space=pltpu.VMEM)] * (inputs - smem)
    out_specs = jax.tree.map(lambda _: pl.BlockSpec(memory_space=pltpu.VMEM), out_shape)
    return pl.pallas_call(
        kernel,
        out_shape=out_shape,
        in_specs=in_specs,
        out_specs=out_specs,
        scratch_shapes=list(scratch),
        compiler_params=pltpu.CompilerParams(vmem_limit_bytes=VMEM_LIMIT),
        cost_estimate=pl.CostEstimate(flops=1024, bytes_accessed=1024, transcendentals=0),
    )


def gathered_panel(panel, axis, ready):
    count = lax.axis_size(axis)
    shards = {0: panel}
    mask = count // 2
    while mask:
        pairs = [(i, i ^ mask) for i in range(count)]
        for held in sorted(shards):
            operand = panel if len(shards) == 1 else tied(shards[held], ready)
            shards[held | mask] = lax.ppermute(operand, axis, pairs)
        mask //= 2
    return [shards[k] for k in range(1, count)]


def tied(value, *others):
    return lax.optimization_barrier((value,) + others)[0]


def tree_sum(parts):
    while len(parts) > 1:
        parts = [parts[i] + parts[i + 1] for i in range(0, len(parts), 2)]
    return parts[0]


def summands(part, axis):
    count = lax.axis_size(axis)
    if count & (count - 1):
        return [lax.psum(part, axis)]
    done, parts = 1, [part]
    for span in (2, 4, 4, 4, 4):
        span = min(span, count // done)
        if span > 1:
            part = tree_sum(parts)
            pairs = [[(i, i ^ (k * done)) for i in range(count)] for k in range(1, span)]
            parts = [part] + [lax.ppermute(part, axis, pair) for pair in pairs]
            done *= span
    return parts


def local(sensor_field, courant, diffusivity, probe_offset, tile_index, actuator_panel):
    slabs, probes = lax.axis_size("state"), lax.axis_size("probe")
    own = sensor_field[0]
    cells, height, width = own.shape
    columns = width // TILE
    tile_total = cells * height * columns
    actuators = tile_index.shape[1]
    groups = actuators // GROUP
    shard = groups // probes
    planes = 3 * cells
    f32, bf16 = jnp.float32, jnp.bfloat16

    source = lax.axis_index("probe") ^ jnp.arange(probes, dtype=jnp.int32)
    low = lax.ppermute(own, "state", shift_pairs(slabs, 1))
    high = lax.ppermute(own, "state", shift_pairs(slabs, -1))

    zero = jnp.zeros((1,), f32)
    rates = [
        courant,
        diffusivity,
        jnp.concatenate([diffusivity[1:], zero]),
        jnp.concatenate([zero, diffusivity[:-1]]),
    ]
    shifted, coef, start, chosen, panel = call(
        lambda *refs: prelude_kernel(columns, height, *refs),
        (
            jax.ShapeDtypeStruct((cells, columns, height, TILE), f32),
            jax.ShapeDtypeStruct((5, height, TILE), f32),
            jax.ShapeDtypeStruct((groups, GROUP), jnp.int32),
            jax.ShapeDtypeStruct((tile_total, actuators), bf16),
            jax.ShapeDtypeStruct(actuator_panel.shape[1:], bf16),
        ),
        smem=1,
        inputs=8,
    )(
        probe_offset,
        own,
        *[rate[:, None] for rate in rates],
        tile_index.reshape(groups, GROUP),
        actuator_panel[0],
    )
    panels = [panel] + gathered_panel(actuator_panel[0], "probe", coef)

    field_shape = pltpu.VMEM((planes, columns, height + 2 * PAD, TILE), f32)
    tiles = call(
        adjoint_kernel,
        jax.ShapeDtypeStruct((tile_total * STEPS + 2 * PAD, TILE), f32),
        scratch=(field_shape, field_shape),
        smem=1,
        inputs=5,
    )(probe_offset, coef, shifted, low, high)

    every = list(range(probes))

    def project(chunks, *given):
        return call(
            lambda *refs: project_kernel(chunks, *refs),
            jax.ShapeDtypeStruct((groups, 2 * STEPS, TILE), f32),
            scratch=(pltpu.VMEM((shard * GROUP, TILE), f32),),
            smem=2,
            inputs=3 + len(chunks) + len(given),
        )(source, start, tiles, *[panels[chunk] for chunk in chunks], *given)

    before = project(every[:-1])
    parts = summands(project(every[-1:], before), "state")
    payload = jax.ShapeDtypeStruct((2 * cells - 1, height * columns, TILE), bf16)
    heads = jax.ShapeDtypeStruct((cells, height * columns, TILE), bf16)
    total, forced, rightward, leftward = call(
        lambda *refs: deposit_kernel(len(parts), *refs),
        (
            jax.ShapeDtypeStruct(before.shape, f32),
            jax.ShapeDtypeStruct((cells, height * columns, TILE), f32),
            payload,
            heads,
        ),
        scratch=(pltpu.VMEM((actuators, 2 * TILE), bf16),),
        smem=1,
        inputs=2 + len(parts) + probes,
    )(source, chosen, *parts, *panels)
    from_low = lax.ppermute(rightward, "state", shift_pairs(slabs, 1))
    from_high = lax.ppermute(leftward, "state", shift_pairs(slabs, -1))
    response = call(
        forward_kernel,
        jax.ShapeDtypeStruct((cells, height, width), f32),
        scratch=(field_shape, field_shape),
        inputs=4,
    )(coef, forced, from_low, from_high)
    projections = total.reshape(groups, 2, STEPS, TILE).transpose(2, 0, 1, 3)
    return projections.reshape(STEPS, 1, actuators), response[None]


def solution(mesh):
    return jax.shard_map(
        local,
        mesh=mesh,
        in_specs=(
            P("probe", "state", None, None),
            P(),
            P(),
            P("probe"),
            P("state", None),
            P("state", "probe", None),
        ),
        out_specs=(P(None, "probe", None), P("probe", "state", None, None)),
        check_vma=False,
    )
```

```python
import jax
import jax.numpy as jnp
from jax import lax
from jax.experimental import pallas as pl
from jax.experimental.pallas import tpu as pltpu
from jax.sharding import PartitionSpec as P

TILE = 128
STEPS = 4
PAD = 8
GROUP = 256


def shift_pairs(count, by):
    return [(i, (i + by) % count) for i in range(count)]


def clear_pads(buffer):
    planes, columns, rows, lanes = buffer.shape
    edge = jnp.zeros((columns, PAD, lanes), buffer.dtype)

    def body(plane, carry):
        buffer[plane, :, :PAD, :] = edge
        buffer[plane, :, rows - PAD :, :] = edge
        return carry

    lax.fori_loop(0, planes, body, 0)


def sweep_rows(source, coef, planes, row, adjoint):
    here = pl.ds(pl.multiple_of(PAD + row, 8), 8)
    block = pl.ds(pl.multiple_of(row, 8), 8)
    columns = source.shape[1]
    lane = lax.broadcasted_iota(jnp.int32, (8, TILE), 1)
    weights = [coef[place, block, :] for place in range(5)]
    lower, centre = source[planes[0] - 1, :, here, :], source[planes[0], :, here, :]
    out = []
    for plane in planes:
        upper = source[plane + 1, :, here, :]
        above = source[plane, :, pl.ds(PAD + row + 1, 8), :]
        below = source[plane, :, pl.ds(PAD + row - 1, 8), :]
        left = [pltpu.roll(centre[c], TILE - 1, 1) for c in range(columns)]
        right = [pltpu.roll(centre[c], 1, 1) for c in range(columns)]
        results = []
        for c in range(columns):
            upper_z = jnp.where(lane == TILE - 1, left[(c + 1) % columns], left[c])
            lower_z = jnp.where(lane == 0, right[(c - 1) % columns], right[c])
            total = weights[0] * centre[c]
            if adjoint:
                total = total + weights[1] * upper[c]
                total = total + weights[2] * (lower[c] + (upper_z + lower_z))
                total = total + (weights[3] * above[c] + weights[4] * below[c])
            else:
                total = total + weights[1] * lower[c]
                total = total + weights[2] * ((upper[c] + (upper_z + lower_z)) + (above[c] + below[c]))
            results.append(total)
        out.append(results)
        lower, centre = centre, upper
    return out


def split(value):
    high = value.astype(jnp.bfloat16)
    low = (value - high.astype(jnp.float32)).astype(jnp.bfloat16)
    return high, low


def shifted_plane(field, plane, offset):
    height, width = field.shape[1:]
    columns = width // TILE
    turn, rest = offset // TILE, offset % TILE
    lane = lax.broadcasted_iota(jnp.int32, (height, TILE), 1)
    rolled = [pltpu.roll(field[plane, :, pl.ds(c * TILE, TILE)], rest, 1) for c in range(columns)]
    return [
        (lax.rem(c + turn, columns), jnp.where(lane >= rest, rolled[c], rolled[c - 1]))
        for c in range(columns)
    ]


def prelude_kernel(offset, field, courant, diffusivity, tile, panel, own, coef, start, chosen, kept):
    columns, height = own.shape[1:3]

    def load(plane, carry):
        for column, value in shifted_plane(field, plane, offset[0]):
            own[plane, column] = value
        return carry

    lax.fori_loop(0, field.shape[0], load, 0)
    kept[...] = panel[...]
    padding = jnp.zeros((6, height), jnp.float32)
    upright = jnp.concatenate([courant[...], diffusivity[...], padding], axis=0).T
    speed = jnp.broadcast_to(upright[:, 0:1], (height, TILE))
    rate = jnp.broadcast_to(upright[:, 1:2], (height, TILE))
    edge = jnp.zeros((1, TILE), jnp.float32)
    coef[0] = 1.0 - speed - 6.0 * rate
    coef[1] = speed + rate
    coef[2] = rate
    coef[3] = jnp.concatenate([rate[1:], edge], axis=0)
    coef[4] = jnp.concatenate([edge, rate[:-1]], axis=0)
    numbers = tile[...]
    inside = numbers & (columns * height - 1)
    numbers = (numbers - inside) + (inside & (columns - 1)) * height + inside // columns
    start[...] = numbers * STEPS
    rows = 64

    def choose(place, carry):
        by_row = lax.broadcasted_iota(jnp.int32, (rows, TILE), 0) + place * rows
        where = pl.ds(pl.multiple_of(place * rows, rows), rows)
        for left in range(0, chosen.shape[1], TILE):
            found = jnp.where(numbers[:, left : left + TILE] == by_row, 1.0, 0.0)
            chosen[where, pl.ds(left, TILE)] = found.astype(jnp.bfloat16)
        return carry

    lax.fori_loop(0, chosen.shape[0] // rows, choose, 0)


def adjoint_kernel(offset, coef, own, low, high, tiles, first, second):
    cells, columns, height = own.shape[:3]
    steps = STEPS
    edge = jnp.zeros((PAD, TILE), jnp.float32)
    tiles[:PAD, :] = edge
    tiles[tiles.shape[0] - PAD :, :] = edge
    inside = pl.ds(PAD, height)
    clear_pads(first)
    clear_pads(second)

    def load(plane, carry):
        for slab, field in ((0, low), (2, high)):
            for column, value in shifted_plane(field, plane, offset[0]):
                first[slab * cells + plane, column, inside, :] = value
        first[cells + plane, :, inside, :] = own[plane]
        return carry

    lax.fori_loop(0, cells, load, 0)
    buffers = (first, second)
    for step in range(steps):
        source, target = buffers[step % 2], buffers[(step + 1) % 2]

        def sweep(place, carry, source=source, target=target, step=step):
            planes = range(step + 1, 3 * cells - step - 1)
            row = place * 8
            for plane, block in zip(planes, sweep_rows(source, coef, planes, row, True)):
                for c in range(columns):
                    if step < steps - 1:
                        where = pl.ds(pl.multiple_of(PAD + row, 8), 8)
                        target[plane, c, where, :] = block[c]
                    if cells <= plane < 2 * cells:
                        number = ((plane - cells) * columns + c) * height + row
                        tiles[pl.ds(PAD + number * steps + step, 8, stride=steps), :] = block[c]
            return carry

        lax.fori_loop(0, height // 8, sweep, 0)


def forward_kernel(coef, own, low, high, out, first, second):
    cells, height, width = out.shape
    columns = width // TILE
    steps = STEPS
    clear_pads(first)
    clear_pads(second)
    for plane in range(cells):
        for c in range(columns):
            where = pl.ds(c * height, height)
            inside = pl.ds(PAD, height)
            first[cells + plane, c, inside, :] = own[plane, where, :]
            first[2 * cells + plane, c, inside, :] = high[plane, where, :].astype(jnp.float32)
            value = low[plane, where, :].astype(jnp.float32)
            if plane > 0:
                value = value + low[cells + plane - 1, where, :].astype(jnp.float32)
            first[plane, c, inside, :] = value
    buffers = (first, second)
    for step in range(steps):
        source, target = buffers[step % 2], buffers[(step + 1) % 2]

        def sweep(place, carry, source=source, target=target, step=step):
            planes = range(step + 1, 3 * cells - step - 1)
            row = place * 8
            for plane, block in zip(planes, sweep_rows(source, coef, planes, row, False)):
                for c in range(columns):
                    if step == steps - 1:
                        where = pl.ds(pl.multiple_of(row, 8), 8)
                        out[plane - cells, where, pl.ds(c * TILE, TILE)] = block[c]
                    else:
                        target[plane, c, pl.ds(pl.multiple_of(PAD + row, 8), 8), :] = block[c]
            return carry

        lax.fori_loop(0, height // 8, sweep, 0)


def project_kernel(chunks, source, start, tiles, *refs):
    panels, (*before, out, wide) = refs[: len(chunks)], refs[len(chunks) :]
    shard = panels[0].shape[0] // GROUP
    for given in before:
        out[...] = given[...]
    first = lax.broadcasted_iota(jnp.int32, (8, TILE), 0) < STEPS
    lane = lax.broadcasted_iota(jnp.int32, (8, TILE), 1)
    for chunk, panel in zip(chunks, panels):
        wide[...] = panel[...].astype(jnp.float32)

        def body(group, carry, chunk=chunk):
            number = source[chunk] * shard + group
            sums = jnp.zeros((8, TILE), jnp.float32)
            for place in range(TILE):
                left = start[0, number * GROUP + place]
                right = start[0, number * GROUP + TILE + place]
                cells = jnp.where(
                    first, tiles[pl.ds(PAD + left, 8), :], tiles[pl.ds(PAD - STEPS + right, 8), :]
                )
                row = group * GROUP + place
                rows = jnp.where(first, wide[pl.ds(row, 1), :], wide[pl.ds(row + TILE, 1), :])
                total = jnp.sum(cells * rows, axis=1, keepdims=True)
                sums = jnp.where(lane == place, total, sums)
            out[number] = sums
            return carry

        lax.fori_loop(0, shard, body, 0)


def deposit_kernel(count, source, chosen, *refs):
    parts, panels, (total, field, rightward, leftward, scaled) = refs[:count], refs[count:-5], refs[-5:]
    groups = total.shape[0]
    shard = groups // len(panels)
    cells, per_plane = field.shape[0], field.shape[1]
    total[...] = tree_sum([part[...] for part in parts])
    numbers = [source[g // shard] * shard + g % shard for g in range(groups)]
    last = [total[n, pl.ds(half * STEPS + STEPS - 1, 1), :] for n in numbers for half in range(2)]
    drive = jnp.concatenate(last, axis=0).T
    for group, number in enumerate(numbers):
        for half in range(2):
            place = 2 * group + half
            rows = panels[group // shard][pl.ds((group % shard) * GROUP + half * TILE, TILE), :]
            head, tail = split(drive[:, place : place + 1] * rows.astype(jnp.float32))
            where = pl.ds(pl.multiple_of(number * GROUP + half * TILE, TILE), TILE)
            scaled[where, pl.ds(0, TILE)] = head
            scaled[where, pl.ds(TILE, TILE)] = tail

    for plane in range(cells):
        sums = jnp.dot(
            chosen[pl.ds(plane * per_plane, per_plane), :],
            scaled[...],
            preferred_element_type=jnp.float32,
        )
        value = sums[:, :TILE] + sums[:, TILE:]
        field[plane] = value
        head, tail = split(value)
        leftward[plane] = head
        rightward[plane] = head
        if plane > 0:
            rightward[cells + plane - 1] = tail


def call(kernel, out_shape, vmem, scratch=(), smem=0, inputs=0):
    in_specs = [pl.BlockSpec(memory_space=pltpu.SMEM)] * smem
    in_specs += [pl.BlockSpec(memory_space=pltpu.VMEM)] * (inputs - smem)
    out_specs = jax.tree.map(lambda _: pl.BlockSpec(memory_space=pltpu.VMEM), out_shape)
    return pl.pallas_call(
        kernel,
        out_shape=out_shape,
        in_specs=in_specs,
        out_specs=out_specs,
        scratch_shapes=list(scratch),
        compiler_params=pltpu.CompilerParams(vmem_limit_bytes=vmem * 1024 * 1024),
        cost_estimate=pl.CostEstimate(flops=1024, bytes_accessed=1024, transcendentals=0),
    )


def gathered_panel(panel, axis, ready):
    count = lax.axis_size(axis)
    shards, mask = {0: panel}, count // 2
    while mask:
        pairs = [(i, i ^ mask) for i in range(count)]
        for held in sorted(shards):
            operand = tied(shards[held], ready) if held else panel
            shards[held | mask] = lax.ppermute(operand, axis, pairs)
        mask //= 2
    return [shards[k] for k in range(1, count)]


def tied(value, *others):
    return lax.optimization_barrier((value,) + others)[0]


def tree_sum(parts):
    while len(parts) > 1:
        parts = [parts[i] + parts[i + 1] for i in range(0, len(parts), 2)]
    return parts[0]


def summands(part, axis):
    count = lax.axis_size(axis)
    if count & (count - 1):
        return [lax.psum(part, axis)]
    done, parts = 1, [part]
    for span in (2, 4, 4, 4, 4):
        span = min(span, count // done)
        if span > 1:
            part = tree_sum(parts)
            pairs = [[(i, i ^ (k * done)) for i in range(count)] for k in range(1, span)]
            parts = [part] + [lax.ppermute(part, axis, pair) for pair in pairs]
            done *= span
    return parts


def local(sensor_field, courant, diffusivity, probe_offset, tile_index, actuator_panel):
    slabs, probes = lax.axis_size("state"), lax.axis_size("probe")
    own = sensor_field[0]
    cells, height, width = own.shape
    columns = width // TILE
    tile_total = cells * height * columns
    actuators = tile_index.shape[1]
    groups = actuators // GROUP
    shard = groups // probes
    planes = 3 * cells
    f32, bf16 = jnp.float32, jnp.bfloat16

    source = lax.axis_index("probe") ^ jnp.arange(probes, dtype=jnp.int32)
    low = lax.ppermute(own, "state", shift_pairs(slabs, 1))
    high = lax.ppermute(own, "state", shift_pairs(slabs, -1))

    shifted, coef, start, chosen, panel = call(
        prelude_kernel,
        (
            jax.ShapeDtypeStruct((cells, columns, height, TILE), f32),
            jax.ShapeDtypeStruct((5, height, TILE), f32),
            jax.ShapeDtypeStruct(tile_index.shape, jnp.int32),
            jax.ShapeDtypeStruct((tile_total, actuators), bf16),
            jax.ShapeDtypeStruct(actuator_panel.shape[1:], bf16),
        ),
        vmem=14,
        smem=1,
        inputs=6,
    )(probe_offset, own, courant[None], diffusivity[None], tile_index, actuator_panel[0])

    field_shape = pltpu.VMEM((planes, columns, height + 2 * PAD, TILE), f32)
    tiles = call(
        adjoint_kernel,
        jax.ShapeDtypeStruct((tile_total * STEPS + 2 * PAD, TILE), f32),
        vmem=10,
        scratch=(field_shape, field_shape),
        smem=1,
        inputs=5,
    )(probe_offset, coef, shifted, low, high)

    panels = [panel] + gathered_panel(actuator_panel[0], "probe", tiles)
    every = list(range(probes))

    def project(chunks, *given):
        return call(
            lambda *refs: project_kernel(chunks, *refs),
            jax.ShapeDtypeStruct((groups, 2 * STEPS, TILE), f32),
            vmem=6,
            scratch=(pltpu.VMEM((shard * GROUP, TILE), f32),),
            smem=2,
            inputs=3 + len(chunks) + len(given),
        )(source, start, tiles, *[panels[chunk] for chunk in chunks], *given)

    before = project(every[:-1])
    parts = summands(project(every[-1:], before), "state")
    payload = jax.ShapeDtypeStruct((2 * cells - 1, height * columns, TILE), bf16)
    heads = jax.ShapeDtypeStruct((cells, height * columns, TILE), bf16)
    total, forced, rightward, leftward = call(
        lambda *refs: deposit_kernel(len(parts), *refs),
        (
            jax.ShapeDtypeStruct(before.shape, f32),
            jax.ShapeDtypeStruct((cells, height * columns, TILE), f32),
            payload,
            heads,
        ),
        vmem=18,
        scratch=(pltpu.VMEM((actuators, 2 * TILE), bf16),),
        smem=1,
        inputs=2 + len(parts) + probes,
    )(source, chosen, *parts, *panels)
    from_low = lax.ppermute(rightward, "state", shift_pairs(slabs, 1))
    from_high = lax.ppermute(leftward, "state", shift_pairs(slabs, -1))
    response = call(
        forward_kernel,
        jax.ShapeDtypeStruct((cells, height, width), f32),
        vmem=10,
        scratch=(field_shape, field_shape),
        inputs=4,
    )(coef, forced, from_low, from_high)
    projections = total.reshape(groups, 2, STEPS, TILE).transpose(2, 0, 1, 3)
    return projections.reshape(STEPS, 1, actuators), response[None]


def solution(mesh):
    return jax.shard_map(
        local,
        mesh=mesh,
        in_specs=(
            P("probe", "state", None, None),
            P(),
            P(),
            P("probe"),
            P("state", None),
            P("state", "probe", None),
        ),
        out_specs=(P(None, "probe", None), P("probe", "state", None, None)),
        check_vma=False,
    )
```

```python
import jax
import jax.numpy as jnp
from jax import lax
from jax.experimental import pallas as pl
from jax.experimental.pallas import tpu as pltpu
from jax.sharding import PartitionSpec as P

TILE = 128
STEPS = 4
PAD = 8
GROUP = 256


def shift_pairs(count, by):
    return [(i, (i + by) % count) for i in range(count)]


def clear_pads(buffer):
    planes, columns, rows, lanes = buffer.shape
    edge = jnp.zeros((columns, PAD, lanes), buffer.dtype)

    def body(plane, carry):
        buffer[plane, :, :PAD, :] = edge
        buffer[plane, :, rows - PAD :, :] = edge
        return carry

    lax.fori_loop(0, planes, body, 0)


def sweep_rows(source, coef, planes, row, adjoint):
    here = pl.ds(pl.multiple_of(PAD + row, 8), 8)
    block = pl.ds(pl.multiple_of(row, 8), 8)
    columns = source.shape[1]
    lane = lax.broadcasted_iota(jnp.int32, (8, TILE), 1)
    weights = [coef[place, block, :] for place in range(5)]
    lower, centre = source[planes[0] - 1, :, here, :], source[planes[0], :, here, :]
    out = []
    for plane in planes:
        upper = source[plane + 1, :, here, :]
        above = source[plane, :, pl.ds(PAD + row + 1, 8), :]
        below = source[plane, :, pl.ds(PAD + row - 1, 8), :]
        left = [pltpu.roll(centre[c], TILE - 1, 1) for c in range(columns)]
        right = [pltpu.roll(centre[c], 1, 1) for c in range(columns)]
        results = []
        for c in range(columns):
            upper_z = jnp.where(lane == TILE - 1, left[(c + 1) % columns], left[c])
            lower_z = jnp.where(lane == 0, right[(c - 1) % columns], right[c])
            total = weights[0] * centre[c]
            if adjoint:
                total = total + weights[1] * upper[c]
                total = total + weights[2] * (lower[c] + (upper_z + lower_z))
                total = total + (weights[3] * above[c] + weights[4] * below[c])
            else:
                total = total + weights[1] * lower[c]
                total = total + weights[2] * ((upper[c] + (upper_z + lower_z)) + (above[c] + below[c]))
            results.append(total)
        out.append(results)
        lower, centre = centre, upper
    return out


def split(value):
    high = value.astype(jnp.bfloat16)
    low = (value - high.astype(jnp.float32)).astype(jnp.bfloat16)
    return high, low


def shifted_plane(field, plane, offset):
    height, width = field.shape[1:]
    columns = width // TILE
    turn, rest = offset // TILE, offset % TILE
    lane = lax.broadcasted_iota(jnp.int32, (height, TILE), 1)
    parts = [field[plane, :, pl.ds(c * TILE, TILE)].astype(jnp.float32) for c in range(columns)]
    rolled = [pltpu.roll(part, rest, 1) for part in parts]
    return [
        (lax.rem(c + turn, columns), jnp.where(lane >= rest, rolled[c], rolled[c - 1]))
        for c in range(columns)
    ]


def prelude_kernel(offset, field, courant, diffusivity, tile, panel, own, coef, start, kept, chosen, built, sems):
    columns, height = own.shape[1:3]

    def load(plane, carry):
        for column, value in shifted_plane(field, plane, offset[0]):
            own[plane, column] = value
        return carry

    lax.fori_loop(0, field.shape[0], load, 0)
    kept[...] = panel[...]
    padding = jnp.zeros((6, height), jnp.float32)
    upright = jnp.concatenate([courant[...], diffusivity[...], padding], axis=0).T
    speed = jnp.broadcast_to(upright[:, 0:1], (height, TILE))
    rate = jnp.broadcast_to(upright[:, 1:2], (height, TILE))
    edge = jnp.zeros((1, TILE), jnp.float32)
    coef[0] = 1.0 - speed - 6.0 * rate
    coef[1] = speed + rate
    coef[2] = rate
    coef[3] = jnp.concatenate([rate[1:], edge], axis=0)
    coef[4] = jnp.concatenate([edge, rate[:-1]], axis=0)
    numbers = tile[...]
    inside = numbers & (columns * height - 1)
    numbers = (numbers - inside) + (inside & (columns - 1)) * height + inside // columns
    start[...] = numbers * STEPS
    rows = built.shape[0] // sems.shape[0]

    def block(place):
        where = pl.ds(pl.multiple_of(place * rows, rows), rows)
        return pltpu.make_async_copy(built.at[where], chosen.at[where], sems.at[place])

    def choose(place, carry):
        by_row = lax.broadcasted_iota(jnp.int32, (rows, TILE), 0) + place * rows
        where = pl.ds(pl.multiple_of(place * rows, rows), rows)
        for left in range(0, built.shape[1], TILE):
            found = jnp.where(numbers[:, left : left + TILE] == by_row, 1.0, 0.0)
            built[where, pl.ds(left, TILE)] = found.astype(jnp.bfloat16)
        block(place).start()
        return carry

    def finish(place, carry):
        block(place).wait()
        return carry

    lax.fori_loop(0, sems.shape[0], choose, 0)
    lax.fori_loop(0, sems.shape[0], finish, 0)


def adjoint_kernel(offset, coef, own, low, high, tiles, first, second):
    cells, columns, height = own.shape[:3]
    steps = STEPS
    edge = jnp.zeros((PAD, TILE), jnp.float32)
    tiles[:PAD, :] = edge
    tiles[tiles.shape[0] - PAD :, :] = edge
    inside = pl.ds(PAD, height)
    clear_pads(first)
    clear_pads(second)

    def load(plane, carry):
        for slab, field in ((0, low), (2, high)):
            for column, value in shifted_plane(field, plane, offset[0]):
                first[slab * cells + plane, column, inside, :] = value
        first[cells + plane, :, inside, :] = own[plane]
        return carry

    lax.fori_loop(0, cells, load, 0)
    buffers = (first, second)
    for step in range(steps):
        source, target = buffers[step % 2], buffers[(step + 1) % 2]

        def sweep(place, carry, source=source, target=target, step=step):
            planes = range(step + 1, 3 * cells - step - 1)
            row = place * 8
            for plane, block in zip(planes, sweep_rows(source, coef, planes, row, True)):
                for c in range(columns):
                    if step < steps - 1:
                        where = pl.ds(pl.multiple_of(PAD + row, 8), 8)
                        target[plane, c, where, :] = block[c]
                    if cells <= plane < 2 * cells:
                        number = ((plane - cells) * columns + c) * height + row
                        tiles[pl.ds(PAD + number * steps + step, 8, stride=steps), :] = block[c]
            return carry

        lax.fori_loop(0, height // 8, sweep, 0)


def forward_kernel(coef, own, low, high, out, first, second):
    cells, height, width = out.shape
    columns = width // TILE
    steps = STEPS
    clear_pads(first)
    clear_pads(second)
    for plane in range(cells):
        for c in range(columns):
            where = pl.ds(c * height, height)
            inside = pl.ds(PAD, height)
            first[cells + plane, c, inside, :] = own[plane, where, :]
            first[2 * cells + plane, c, inside, :] = high[plane, where, :].astype(jnp.float32)
            value = low[plane, where, :].astype(jnp.float32)
            if plane > 0:
                value = value + low[cells + plane - 1, where, :].astype(jnp.float32)
            first[plane, c, inside, :] = value
    buffers = (first, second)
    for step in range(steps):
        source, target = buffers[step % 2], buffers[(step + 1) % 2]

        def sweep(place, carry, source=source, target=target, step=step):
            planes = range(step + 1, 3 * cells - step - 1)
            row = place * 8
            for plane, block in zip(planes, sweep_rows(source, coef, planes, row, False)):
                for c in range(columns):
                    if step == steps - 1:
                        where = pl.ds(pl.multiple_of(row, 8), 8)
                        out[plane - cells, where, pl.ds(c * TILE, TILE)] = block[c]
                    else:
                        target[plane, c, pl.ds(pl.multiple_of(PAD + row, 8), 8), :] = block[c]
            return carry

        lax.fori_loop(0, height // 8, sweep, 0)


def project_kernel(chunks, source, start, tiles, *refs):
    count = len(chunks)
    panels, (*before, early, last, wide) = refs[:count], refs[count:]
    shard = panels[0].shape[0] // GROUP
    if before:
        early[...] = before[0][...]
        last[...] = before[1][...]
    first = lax.broadcasted_iota(jnp.int32, (8, TILE), 0) < STEPS
    lane = lax.broadcasted_iota(jnp.int32, (8, TILE), 1)
    for chunk, panel in zip(chunks, panels):
        wide[...] = panel[...].astype(jnp.float32)

        def body(group, carry, chunk=chunk):
            number = source[chunk] * shard + group
            sums = jnp.zeros((8, TILE), jnp.float32)
            for place in range(TILE):
                left = start[0, number * GROUP + place]
                right = start[0, number * GROUP + TILE + place]
                cells = jnp.where(
                    first, tiles[pl.ds(PAD + left, 8), :], tiles[pl.ds(PAD - STEPS + right, 8), :]
                )
                row = group * GROUP + place
                rows = jnp.where(first, wide[pl.ds(row, 1), :], wide[pl.ds(row + TILE, 1), :])
                total = jnp.sum(cells * rows, axis=1, keepdims=True)
                sums = jnp.where(lane == place, total, sums)
            for half in range(2):
                row = 2 * number + half
                for step in range(STEPS):
                    value = sums[half * STEPS + step : half * STEPS + step + 1]
                    if step < STEPS - 1:
                        early[step, pl.ds(row, 1), :] = value
                    else:
                        last[pl.ds(row, 1), :] = value
            return carry

        lax.fori_loop(0, shard, body, 0)


def deposit_kernel(count, source, chosen, *refs):
    parts, panels = refs[:count], refs[count:-7]
    total, field, rightward, leftward, scaled, held, sems = refs[-7:]
    groups = total.shape[0] // 2
    shard = groups // len(panels)
    cells, per_plane = field.shape[0], field.shape[1]
    copies = []
    for plane in range(cells):
        where = pl.ds(plane * per_plane, per_plane)
        copies.append(pltpu.make_async_copy(chosen.at[where], held.at[where], sems.at[plane]))
        copies[plane].start()
    total[...] = tree_sum([part[...] for part in parts])
    numbers = [source[g // shard] * shard + g % shard for g in range(groups)]
    last = [total[pl.ds(2 * number + half, 1), :] for number in numbers for half in range(2)]
    drive = jnp.concatenate(last, axis=0).T
    for group, number in enumerate(numbers):
        for half in range(2):
            place = 2 * group + half
            rows = panels[group // shard][pl.ds((group % shard) * GROUP + half * TILE, TILE), :]
            head, tail = split(drive[:, place : place + 1] * rows.astype(jnp.float32))
            where = pl.ds(pl.multiple_of(number * GROUP + half * TILE, TILE), TILE)
            scaled[where, pl.ds(0, TILE)] = head
            scaled[where, pl.ds(TILE, TILE)] = tail

    for plane in range(cells):
        copies[plane].wait()
        sums = jnp.dot(
            held[pl.ds(plane * per_plane, per_plane), :],
            scaled[...],
            preferred_element_type=jnp.float32,
        )
        value = sums[:, :TILE] + sums[:, TILE:]
        field[plane] = value
        head, tail = split(value)
        leftward[plane] = head
        rightward[plane] = head
        if plane > 0:
            rightward[cells + plane - 1] = tail


def call(kernel, out_shape, vmem, scratch=(), smem=0, inputs=0, hbm_in=(), hbm_out=()):
    in_specs = [pl.BlockSpec(memory_space=pltpu.SMEM)] * smem
    in_specs += [pl.BlockSpec(memory_space=pltpu.VMEM)] * (inputs - smem)
    for place in hbm_in:
        in_specs[place] = pl.BlockSpec(memory_space=pltpu.HBM)
    out_specs = jax.tree.map(lambda _: pl.BlockSpec(memory_space=pltpu.VMEM), out_shape)
    if hbm_out:
        out_specs = list(out_specs)
        for place in hbm_out:
            out_specs[place] = pl.BlockSpec(memory_space=pltpu.HBM)
        out_specs = tuple(out_specs)
    return pl.pallas_call(
        kernel,
        out_shape=out_shape,
        in_specs=in_specs,
        out_specs=out_specs,
        scratch_shapes=list(scratch),
        compiler_params=pltpu.CompilerParams(vmem_limit_bytes=vmem * 1024 * 1024),
        cost_estimate=pl.CostEstimate(flops=1024, bytes_accessed=1024, transcendentals=0),
    )


def gathered_panel(panel, axis, ready):
    count = lax.axis_size(axis)
    shards, mask = {0: panel}, count // 2
    while mask:
        pairs = [(i, i ^ mask) for i in range(count)]
        for held in sorted(shards):
            operand = tied(shards[held], ready) if held else panel
            shards[held | mask] = lax.ppermute(operand, axis, pairs)
        mask //= 2
    return [shards[k] for k in range(1, count)]


def tied(value, *others):
    return lax.optimization_barrier((value,) + others)[0]


def tree_sum(parts):
    while len(parts) > 1:
        parts = [parts[i] + parts[i + 1] for i in range(0, len(parts), 2)]
    return parts[0]


def summands(part, axis):
    count = lax.axis_size(axis)
    if count & (count - 1):
        return [lax.psum(part, axis)]
    done, parts = 1, [part]
    for span in (2, 4, 4, 4, 4):
        span = min(span, count // done)
        if span > 1:
            part = tree_sum(parts)
            pairs = [[(i, i ^ (k * done)) for i in range(count)] for k in range(1, span)]
            parts = [part] + [lax.ppermute(part, axis, pair) for pair in pairs]
            done *= span
    return parts


def local(sensor_field, courant, diffusivity, probe_offset, tile_index, actuator_panel):
    slabs, probes = lax.axis_size("state"), lax.axis_size("probe")
    own = sensor_field[0]
    cells, height, width = own.shape
    columns = width // TILE
    tile_total = cells * height * columns
    actuators = tile_index.shape[1]
    groups = actuators // GROUP
    shard = groups // probes
    planes = 3 * cells
    f32, bf16 = jnp.float32, jnp.bfloat16

    source = lax.axis_index("probe") ^ jnp.arange(probes, dtype=jnp.int32)
    low = lax.ppermute(own.astype(bf16), "state", shift_pairs(slabs, 1))
    high = lax.ppermute(own, "state", shift_pairs(slabs, -1))

    shifted, coef, start, panel, chosen = call(
        prelude_kernel,
        (
            jax.ShapeDtypeStruct((cells, columns, height, TILE), f32),
            jax.ShapeDtypeStruct((5, height, TILE), f32),
            jax.ShapeDtypeStruct(tile_index.shape, jnp.int32),
            jax.ShapeDtypeStruct(actuator_panel.shape[1:], bf16),
            jax.ShapeDtypeStruct((tile_total, actuators), bf16),
        ),
        vmem=14,
        scratch=(pltpu.VMEM((tile_total, actuators), bf16), pltpu.SemaphoreType.DMA((16,))),
        hbm_out=(4,),
        smem=1,
        inputs=6,
    )(probe_offset, own, courant[None], diffusivity[None], tile_index, actuator_panel[0])

    field_shape = pltpu.VMEM((planes, columns, height + 2 * PAD, TILE), f32)
    tiles = call(
        adjoint_kernel,
        jax.ShapeDtypeStruct((tile_total * STEPS + 2 * PAD, TILE), f32),
        vmem=10,
        scratch=(field_shape, field_shape),
        smem=1,
        inputs=5,
    )(probe_offset, coef, shifted, low, high)

    panels = [panel] + gathered_panel(actuator_panel[0], "probe", tiles)
    every = list(range(probes))

    def project(chunks, *given):
        return call(
            lambda *refs: project_kernel(chunks, *refs),
            (
                jax.ShapeDtypeStruct((STEPS - 1, 2 * groups, TILE), f32),
                jax.ShapeDtypeStruct((2 * groups, TILE), f32),
            ),
            vmem=6,
            scratch=(pltpu.VMEM((shard * GROUP, TILE), f32),),
            smem=2,
            inputs=3 + len(chunks) + len(given),
        )(source, start, tiles, *[panels[chunk] for chunk in chunks], *given)

    early, last = project(every[-1:], *project(every[:-1]))
    parts = summands(last, "state")
    payload = jax.ShapeDtypeStruct((2 * cells - 1, height * columns, TILE), bf16)
    heads = jax.ShapeDtypeStruct((cells, height * columns, TILE), bf16)
    total, forced, rightward, leftward = call(
        lambda *refs: deposit_kernel(len(parts), *refs),
        (
            jax.ShapeDtypeStruct(last.shape, f32),
            jax.ShapeDtypeStruct((cells, height * columns, TILE), f32),
            payload,
            heads,
        ),
        vmem=16,
        scratch=(
            pltpu.VMEM((actuators, 2 * TILE), bf16),
            pltpu.VMEM((tile_total, actuators), bf16),
            pltpu.SemaphoreType.DMA((cells,)),
        ),
        smem=1,
        hbm_in=(1,),
        inputs=2 + len(parts) + probes,
    )(source, chosen, *parts, *panels)
    from_low = lax.ppermute(rightward, "state", shift_pairs(slabs, 1))
    from_high = lax.ppermute(leftward, "state", shift_pairs(slabs, -1))
    response = call(
        forward_kernel,
        jax.ShapeDtypeStruct((cells, height, width), f32),
        vmem=10,
        scratch=(field_shape, field_shape),
        inputs=4,
    )(coef, forced, from_low, from_high)
    rounds = 1 + jnp.minimum(probe_offset[0], 0)
    early = lax.fori_loop(0, rounds, lambda _, part: tree_sum(summands(part, "state")), early)
    projections = jnp.concatenate([early, total[None]], axis=0)
    return projections.reshape(STEPS, 1, actuators), response[None]


def solution(mesh):
    return jax.shard_map(
        local,
        mesh=mesh,
        in_specs=(
            P("probe", "state", None, None),
            P(),
            P(),
            P("probe"),
            P("state", None),
            P("state", "probe", None),
        ),
        out_specs=(P(None, "probe", None), P("probe", "state", None, None)),
        check_vma=False,
    )
```

```python
import jax
import jax.numpy as jnp
from jax import lax
from jax.experimental import pallas as pl
from jax.experimental.pallas import tpu as pltpu
from jax.sharding import PartitionSpec as P

TILE = 128
STEPS = 4
PAD = 8
GROUP = 256
ROOM = 6


def shift_pairs(count, by):
    return [(i, (i + by) % count) for i in range(count)]


def clear_pads(buffer):
    planes, columns, rows, lanes = buffer.shape
    edge = jnp.zeros((columns, PAD, lanes), buffer.dtype)

    def body(plane, carry):
        buffer[plane, :, :PAD, :] = edge
        buffer[plane, :, rows - PAD :, :] = edge
        return carry

    lax.fori_loop(0, planes, body, 0)


def sweep_rows(source, coef, planes, row, adjoint):
    here = pl.ds(pl.multiple_of(PAD + row, 8), 8)
    block = pl.ds(pl.multiple_of(row, 8), 8)
    columns = source.shape[1]
    lane = lax.broadcasted_iota(jnp.int32, (8, TILE), 1)
    weights = [coef[place, block, :] for place in range(5)]
    lower, centre = source[planes[0] - 1, :, here, :], source[planes[0], :, here, :]
    out = []
    for plane in planes:
        upper = source[plane + 1, :, here, :]
        above = source[plane, :, pl.ds(PAD + row + 1, 8), :]
        below = source[plane, :, pl.ds(PAD + row - 1, 8), :]
        left = [pltpu.roll(centre[c], TILE - 1, 1) for c in range(columns)]
        right = [pltpu.roll(centre[c], 1, 1) for c in range(columns)]
        results = []
        for c in range(columns):
            upper_z = jnp.where(lane == TILE - 1, left[(c + 1) % columns], left[c])
            lower_z = jnp.where(lane == 0, right[(c - 1) % columns], right[c])
            total = weights[0] * centre[c]
            if adjoint:
                total = total + weights[1] * upper[c]
                total = total + weights[2] * (lower[c] + (upper_z + lower_z))
                total = total + (weights[3] * above[c] + weights[4] * below[c])
            else:
                total = total + weights[1] * lower[c]
                total = total + weights[2] * ((upper[c] + (upper_z + lower_z)) + (above[c] + below[c]))
            results.append(total)
        out.append(results)
        lower, centre = centre, upper
    return out


def split(value):
    high = value.astype(jnp.bfloat16)
    low = (value - high.astype(jnp.float32)).astype(jnp.bfloat16)
    return high, low


def shifted_plane(field, plane, offset):
    height, width = field.shape[1:]
    columns = width // TILE
    turn, rest = offset // TILE, offset % TILE
    lane = lax.broadcasted_iota(jnp.int32, (height, TILE), 1)
    parts = [field[plane, :, pl.ds(c * TILE, TILE)].astype(jnp.float32) for c in range(columns)]
    rolled = [pltpu.roll(part, rest, 1) for part in parts]
    return [
        (lax.rem(c + turn, columns), jnp.where(lane >= rest, rolled[c], rolled[c - 1]))
        for c in range(columns)
    ]


def prelude_kernel(offset, field, courant, diffusivity, tile, panel, own, coef, start, kept, chosen, built, sems):
    columns, height = own.shape[1:3]

    def load(plane, carry):
        for column, value in shifted_plane(field, plane, offset[0]):
            own[plane, column] = value
        return carry

    lax.fori_loop(0, field.shape[0], load, 0)
    kept[...] = panel[...]
    padding = jnp.zeros((6, height), jnp.float32)
    upright = jnp.concatenate([courant[...], diffusivity[...], padding], axis=0).T
    speed = jnp.broadcast_to(upright[:, 0:1], (height, TILE))
    rate = jnp.broadcast_to(upright[:, 1:2], (height, TILE))
    edge = jnp.zeros((1, TILE), jnp.float32)
    coef[0] = 1.0 - speed - 6.0 * rate
    coef[1] = speed + rate
    coef[2] = rate
    coef[3] = jnp.concatenate([rate[1:], edge], axis=0)
    coef[4] = jnp.concatenate([edge, rate[:-1]], axis=0)
    numbers = tile[...]
    inside = numbers & (columns * height - 1)
    numbers = (numbers - inside) + (inside & (columns - 1)) * height + inside // columns
    start[...] = numbers * STEPS
    rows = built.shape[0] // sems.shape[0]

    def block(place):
        where = pl.ds(pl.multiple_of(place * rows, rows), rows)
        return pltpu.make_async_copy(built.at[where], chosen.at[0, where], sems.at[place])

    def choose(place, carry):
        by_row = lax.broadcasted_iota(jnp.int32, (rows, TILE), 0) + place * rows
        where = pl.ds(pl.multiple_of(place * rows, rows), rows)
        for left in range(0, built.shape[1], TILE):
            found = jnp.where(numbers[:, left : left + TILE] == by_row, 1.0, 0.0)
            built[where, pl.ds(left, TILE)] = found.astype(jnp.bfloat16)
        block(place).start()
        return carry

    def finish(place, carry):
        block(place).wait()
        return carry

    lax.fori_loop(0, sems.shape[0], choose, 0)
    lax.fori_loop(0, sems.shape[0], finish, 0)


def adjoint_kernel(offset, coef, own, low, high, tiles, first, second):
    cells, columns, height = own.shape[:3]
    steps = STEPS
    edge = jnp.zeros((PAD, TILE), jnp.float32)
    tiles[:PAD, :] = edge
    tiles[tiles.shape[0] - PAD :, :] = edge
    inside = pl.ds(PAD, height)
    clear_pads(first)
    clear_pads(second)

    def load(plane, carry):
        for slab, field in ((0, low), (2, high)):
            for column, value in shifted_plane(field, plane, offset[0]):
                first[slab * cells + plane, column, inside, :] = value
        first[cells + plane, :, inside, :] = own[plane]
        return carry

    lax.fori_loop(0, cells, load, 0)
    buffers = (first, second)
    for step in range(steps):
        source, target = buffers[step % 2], buffers[(step + 1) % 2]

        def sweep(place, carry, source=source, target=target, step=step):
            planes = range(step + 1, 3 * cells - step - 1)
            row = place * 8
            for plane, block in zip(planes, sweep_rows(source, coef, planes, row, True)):
                for c in range(columns):
                    if step < steps - 1:
                        where = pl.ds(pl.multiple_of(PAD + row, 8), 8)
                        target[plane, c, where, :] = block[c]
                    if cells <= plane < 2 * cells:
                        number = ((plane - cells) * columns + c) * height + row
                        tiles[pl.ds(PAD + number * steps + step, 8, stride=steps), :] = block[c]
            return carry

        lax.fori_loop(0, height // 8, sweep, 0)


def forward_kernel(coef, own, low, high, out, first, second):
    cells, height, width = out.shape
    columns = width // TILE
    steps = STEPS
    clear_pads(first)
    clear_pads(second)
    for plane in range(cells):
        for c in range(columns):
            where = pl.ds(c * height, height)
            inside = pl.ds(PAD, height)
            first[cells + plane, c, inside, :] = own[plane, where, :]
            first[2 * cells + plane, c, inside, :] = high[plane, where, :].astype(jnp.float32)
            value = low[plane, where, :].astype(jnp.float32)
            if plane > 0:
                value = value + low[cells + plane - 1, where, :].astype(jnp.float32)
            first[plane, c, inside, :] = value
    buffers = (first, second)
    for step in range(steps):
        source, target = buffers[step % 2], buffers[(step + 1) % 2]

        def sweep(place, carry, source=source, target=target, step=step):
            planes = range(step + 1, 3 * cells - step - 1)
            row = place * 8
            for plane, block in zip(planes, sweep_rows(source, coef, planes, row, False)):
                for c in range(columns):
                    if step == steps - 1:
                        where = pl.ds(pl.multiple_of(row, 8), 8)
                        out[plane - cells, where, pl.ds(c * TILE, TILE)] = block[c]
                    else:
                        target[plane, c, pl.ds(pl.multiple_of(PAD + row, 8), 8), :] = block[c]
            return carry

        lax.fori_loop(0, height // 8, sweep, 0)


def project_kernel(chunks, source, start, tiles, *refs):
    panels, (*before, out, wide) = refs[: len(chunks)], refs[len(chunks) :]
    shard = panels[0].shape[0] // GROUP
    for given in before:
        out[...] = given[...]
    first = lax.broadcasted_iota(jnp.int32, (8, TILE), 0) < STEPS
    lane = lax.broadcasted_iota(jnp.int32, (8, TILE), 1)
    for chunk, panel in zip(chunks, panels):
        wide[...] = panel[...].astype(jnp.float32)

        def body(group, carry, chunk=chunk):
            number = source[chunk] * shard + group
            sums = jnp.zeros((8, TILE), jnp.float32)
            for place in range(TILE):
                left = start[0, number * GROUP + place]
                right = start[0, number * GROUP + TILE + place]
                cells = jnp.where(
                    first, tiles[pl.ds(PAD + left, 8), :], tiles[pl.ds(PAD - STEPS + right, 8), :]
                )
                row = group * GROUP + place
                rows = jnp.where(first, wide[pl.ds(row, 1), :], wide[pl.ds(row + TILE, 1), :])
                total = jnp.sum(cells * rows, axis=1, keepdims=True)
                sums = jnp.where(lane == place, total, sums)
            out[number] = sums
            return carry

        lax.fori_loop(0, shard, body, 0)


def deposit_kernel(count, source, chosen, *refs):
    parts, panels = refs[:count], refs[count:-7]
    total, field, rightward, leftward, scaled, held, sems = refs[-7:]
    groups = total.shape[0]
    shard = groups // len(panels)
    cells, per_plane = field.shape[0], field.shape[1]
    copies = []
    for plane in range(cells):
        where = pl.ds(plane * per_plane, per_plane)
        copies.append(pltpu.make_async_copy(chosen.at[0, where], held.at[where], sems.at[plane]))
        copies[plane].start()
    total[...] = tree_sum([part[...] for part in parts])
    numbers = [source[g // shard] * shard + g % shard for g in range(groups)]
    last = [total[n, pl.ds(half * STEPS + STEPS - 1, 1), :] for n in numbers for half in range(2)]
    drive = jnp.concatenate(last, axis=0).T
    for group, number in enumerate(numbers):
        for half in range(2):
            place = 2 * group + half
            rows = panels[group // shard][pl.ds((group % shard) * GROUP + half * TILE, TILE), :]
            head, tail = split(drive[:, place : place + 1] * rows.astype(jnp.float32))
            where = pl.ds(pl.multiple_of(number * GROUP + half * TILE, TILE), TILE)
            scaled[where, pl.ds(0, TILE)] = head
            scaled[where, pl.ds(TILE, TILE)] = tail

    for plane in range(cells):
        copies[plane].wait()
        sums = jnp.dot(
            held[pl.ds(plane * per_plane, per_plane), :],
            scaled[...],
            preferred_element_type=jnp.float32,
        )
        value = sums[:, :TILE] + sums[:, TILE:]
        field[plane] = value
        head, tail = split(value)
        leftward[plane] = head
        rightward[plane] = head
        if plane > 0:
            rightward[cells + plane - 1] = tail


def call(kernel, out_shape, vmem, scratch=(), smem=0, inputs=0, hbm_in=(), hbm_out=()):
    in_specs = [pl.BlockSpec(memory_space=pltpu.SMEM)] * smem
    in_specs += [pl.BlockSpec(memory_space=pltpu.VMEM)] * (inputs - smem)
    for place in hbm_in:
        in_specs[place] = pl.BlockSpec(memory_space=pltpu.HBM)
    out_specs = jax.tree.map(lambda _: pl.BlockSpec(memory_space=pltpu.VMEM), out_shape)
    if hbm_out:
        out_specs = list(out_specs)
        for place in hbm_out:
            out_specs[place] = pl.BlockSpec(memory_space=pltpu.HBM)
        out_specs = tuple(out_specs)
    return pl.pallas_call(
        kernel,
        out_shape=out_shape,
        in_specs=in_specs,
        out_specs=out_specs,
        scratch_shapes=list(scratch),
        compiler_params=pltpu.CompilerParams(vmem_limit_bytes=vmem * 1024 * 1024),
        cost_estimate=pl.CostEstimate(flops=1024, bytes_accessed=1024, transcendentals=0),
    )


def gathered_panel(panel, axis, ready):
    count = lax.axis_size(axis)
    shards, mask = {0: panel}, count // 2
    while mask:
        pairs = [(i, i ^ mask) for i in range(count)]
        for held in sorted(shards):
            operand = tied(shards[held], ready) if held else panel
            shards[held | mask] = lax.ppermute(operand, axis, pairs)
        mask //= 2
    return [shards[k] for k in range(1, count)]


def tied(value, *others):
    return lax.optimization_barrier((value,) + others)[0]


def tree_sum(parts):
    while len(parts) > 1:
        parts = [parts[i] + parts[i + 1] for i in range(0, len(parts), 2)]
    return parts[0]


def summands(part, axis):
    count = lax.axis_size(axis)
    if count & (count - 1):
        return [lax.psum(part, axis)]
    done, parts = 1, [part]
    for span in (2, 4, 4, 4, 4):
        span = min(span, count // done)
        if span > 1:
            part = tree_sum(parts)
            pairs = [[(i, i ^ (k * done)) for i in range(count)] for k in range(1, span)]
            parts = [part] + [lax.ppermute(part, axis, pair) for pair in pairs]
            done *= span
    return parts


def local(sensor_field, courant, diffusivity, probe_offset, tile_index, actuator_panel):
    slabs, probes = lax.axis_size("state"), lax.axis_size("probe")
    own = sensor_field[0]
    cells, height, width = own.shape
    columns = width // TILE
    tile_total = cells * height * columns
    actuators = tile_index.shape[1]
    groups = actuators // GROUP
    shard = groups // probes
    planes = 3 * cells
    f32, bf16 = jnp.float32, jnp.bfloat16

    source = lax.axis_index("probe") ^ jnp.arange(probes, dtype=jnp.int32)
    rounded = own.astype(bf16)
    low = lax.ppermute(rounded, "state", shift_pairs(slabs, 1))
    high = lax.ppermute(tied(own, rounded), "state", shift_pairs(slabs, -1))

    shifted, coef, start, panel, chosen = call(
        prelude_kernel,
        (
            jax.ShapeDtypeStruct((cells, columns, height, TILE), f32),
            jax.ShapeDtypeStruct((5, height, TILE), f32),
            jax.ShapeDtypeStruct(tile_index.shape, jnp.int32),
            jax.ShapeDtypeStruct(actuator_panel.shape[1:], bf16),
            jax.ShapeDtypeStruct((ROOM, tile_total, actuators), bf16),
        ),
        vmem=16,
        scratch=(pltpu.VMEM((tile_total, actuators), bf16), pltpu.SemaphoreType.DMA((16,))),
        hbm_out=(4,),
        smem=1,
        inputs=6,
    )(probe_offset, own, courant[None], diffusivity[None], tile_index, actuator_panel[0])

    field_shape = pltpu.VMEM((planes, columns, height + 2 * PAD, TILE), f32)
    tiles = call(
        adjoint_kernel,
        jax.ShapeDtypeStruct((tile_total * STEPS + 2 * PAD, TILE), f32),
        vmem=10,
        scratch=(field_shape, field_shape),
        smem=1,
        inputs=5,
    )(probe_offset, coef, shifted, low, high)

    panels = [panel] + gathered_panel(actuator_panel[0], "probe", coef)
    every = list(range(probes))

    def project(chunks, *given):
        return call(
            lambda *refs: project_kernel(chunks, *refs),
            jax.ShapeDtypeStruct((groups, 2 * STEPS, TILE), f32),
            vmem=6,
            scratch=(pltpu.VMEM((shard * GROUP, TILE), f32),),
            smem=2,
            inputs=3 + len(chunks) + len(given),
        )(source, start, tiles, *[panels[chunk] for chunk in chunks], *given)

    before = project(every[:-1])
    parts = summands(project(every[-1:], before), "state")
    payload = jax.ShapeDtypeStruct((2 * cells - 1, height * columns, TILE), bf16)
    heads = jax.ShapeDtypeStruct((cells, height * columns, TILE), bf16)
    total, forced, rightward, leftward = call(
        lambda *refs: deposit_kernel(len(parts), *refs),
        (
            jax.ShapeDtypeStruct(before.shape, f32),
            jax.ShapeDtypeStruct((cells, height * columns, TILE), f32),
            payload,
            heads,
        ),
        vmem=16,
        scratch=(
            pltpu.VMEM((actuators, 2 * TILE), bf16),
            pltpu.VMEM((tile_total, actuators), bf16),
            pltpu.SemaphoreType.DMA((cells,)),
        ),
        smem=1,
        hbm_in=(1,),
        inputs=2 + len(parts) + probes,
    )(source, chosen, *parts, *panels)
    from_low = lax.ppermute(rightward, "state", shift_pairs(slabs, 1))
    from_high = lax.ppermute(leftward, "state", shift_pairs(slabs, -1))
    response = call(
        forward_kernel,
        jax.ShapeDtypeStruct((cells, height, width), f32),
        vmem=10,
        scratch=(field_shape, field_shape),
        inputs=4,
    )(coef, forced, from_low, from_high)
    projections = total.reshape(groups, 2, STEPS, TILE).transpose(2, 0, 1, 3)
    return projections.reshape(STEPS, 1, actuators), response[None]


def solution(mesh):
    return jax.shard_map(
        local,
        mesh=mesh,
        in_specs=(
            P("probe", "state", None, None),
            P(),
            P(),
            P("probe"),
            P("state", None),
            P("state", "probe", None),
        ),
        out_specs=(P(None, "probe", None), P("probe", "state", None, None)),
        check_vma=False,
    )
```

```python
import jax
import jax.numpy as jnp
from jax import lax
from jax.experimental import pallas as pl
from jax.experimental.pallas import tpu as pltpu
from jax.sharding import PartitionSpec as P

TILE = 128
STEPS = 4
PAD = 8
GROUP = 256


def shift_pairs(count, by):
    return [(i, (i + by) % count) for i in range(count)]


def clear_pads(buffer):
    planes, columns, rows, lanes = buffer.shape
    edge = jnp.zeros((columns, PAD, lanes), buffer.dtype)

    def body(plane, carry):
        buffer[plane, :, :PAD, :] = edge
        buffer[plane, :, rows - PAD :, :] = edge
        return carry

    lax.fori_loop(0, planes, body, 0)


def sweep_rows(source, coef, planes, row, adjoint):
    here = pl.ds(pl.multiple_of(PAD + row, 8), 8)
    block = pl.ds(pl.multiple_of(row, 8), 8)
    columns = source.shape[1]
    lane = lax.broadcasted_iota(jnp.int32, (8, TILE), 1)
    weights = [coef[place, block, :] for place in range(5)]
    lower, centre = source[planes[0] - 1, :, here, :], source[planes[0], :, here, :]
    out = []
    for plane in planes:
        upper = source[plane + 1, :, here, :]
        above = source[plane, :, pl.ds(PAD + row + 1, 8), :]
        below = source[plane, :, pl.ds(PAD + row - 1, 8), :]
        left = [pltpu.roll(centre[c], TILE - 1, 1) for c in range(columns)]
        right = [pltpu.roll(centre[c], 1, 1) for c in range(columns)]
        results = []
        for c in range(columns):
            upper_z = jnp.where(lane == TILE - 1, left[(c + 1) % columns], left[c])
            lower_z = jnp.where(lane == 0, right[(c - 1) % columns], right[c])
            total = weights[0] * centre[c]
            if adjoint:
                total = total + weights[1] * upper[c]
                total = total + weights[2] * (lower[c] + (upper_z + lower_z))
                total = total + (weights[3] * above[c] + weights[4] * below[c])
            else:
                total = total + weights[1] * lower[c]
                total = total + weights[2] * ((upper[c] + (upper_z + lower_z)) + (above[c] + below[c]))
            results.append(total)
        out.append(results)
        lower, centre = centre, upper
    return out


def split(value):
    high = value.astype(jnp.bfloat16)
    low = (value - high.astype(jnp.float32)).astype(jnp.bfloat16)
    return high, low


def shifted_plane(field, plane, offset, tail=None):
    height, width = field.shape[1:]
    columns = width // TILE
    turn, rest = offset // TILE, offset % TILE
    lane = lax.broadcasted_iota(jnp.int32, (height, TILE), 1)
    parts = [field[plane, :, pl.ds(c * TILE, TILE)].astype(jnp.float32) for c in range(columns)]
    if tail is not None:
        parts = [
            part + field[tail, :, pl.ds(c * TILE, TILE)].astype(jnp.float32)
            for c, part in enumerate(parts)
        ]
    rolled = [pltpu.roll(part, rest, 1) for part in parts]
    return [
        (lax.rem(c + turn, columns), jnp.where(lane >= rest, rolled[c], rolled[c - 1]))
        for c in range(columns)
    ]


def prelude_kernel(offset, field, courant, diffusivity, tile, panel, own, coef, start, kept):
    columns, height = own.shape[1:3]

    def load(plane, carry):
        for column, value in shifted_plane(field, plane, offset[0]):
            own[plane, column] = value
        return carry

    lax.fori_loop(0, field.shape[0], load, 0)
    kept[...] = panel[...]
    padding = jnp.zeros((6, height), jnp.float32)
    upright = jnp.concatenate([courant[...], diffusivity[...], padding], axis=0).T
    speed = jnp.broadcast_to(upright[:, 0:1], (height, TILE))
    rate = jnp.broadcast_to(upright[:, 1:2], (height, TILE))
    edge = jnp.zeros((1, TILE), jnp.float32)
    coef[0] = 1.0 - speed - 6.0 * rate
    coef[1] = speed + rate
    coef[2] = rate
    coef[3] = jnp.concatenate([rate[1:], edge], axis=0)
    coef[4] = jnp.concatenate([edge, rate[:-1]], axis=0)
    numbers = tile[...]
    inside = numbers & (columns * height - 1)
    numbers = (numbers - inside) + (inside & (columns - 1)) * height + inside // columns
    start[...] = numbers * STEPS


def adjoint_kernel(offset, coef, own, low, high, tiles, first, second):
    cells, columns, height = own.shape[:3]
    steps = STEPS
    edge = jnp.zeros((PAD, TILE), jnp.float32)
    tiles[:PAD, :] = edge
    tiles[tiles.shape[0] - PAD :, :] = edge
    inside = pl.ds(PAD, height)
    clear_pads(first)
    clear_pads(second)

    for plane in range(cells):
        for column, value in shifted_plane(low, plane, offset[0]):
            first[plane, column, inside, :] = value
        near = cells + plane if plane < cells - 1 else None
        for column, value in shifted_plane(high, plane, offset[0], near):
            first[2 * cells + plane, column, inside, :] = value
        first[cells + plane, :, inside, :] = own[plane]
    buffers = (first, second)
    for step in range(steps):
        source, target = buffers[step % 2], buffers[(step + 1) % 2]

        def sweep(place, carry, source=source, target=target, step=step):
            planes = range(step + 1, 3 * cells - step - 1)
            row = place * 8
            for plane, block in zip(planes, sweep_rows(source, coef, planes, row, True)):
                for c in range(columns):
                    if step < steps - 1:
                        where = pl.ds(pl.multiple_of(PAD + row, 8), 8)
                        target[plane, c, where, :] = block[c]
                    if cells <= plane < 2 * cells:
                        number = ((plane - cells) * columns + c) * height + row
                        tiles[pl.ds(PAD + number * steps + step, 8, stride=steps), :] = block[c]
            return carry

        lax.fori_loop(0, height // 8, sweep, 0)


def forward_kernel(coef, own, low, high, out, first, second):
    cells, height, width = out.shape
    columns = width // TILE
    steps = STEPS
    clear_pads(first)
    clear_pads(second)
    for plane in range(cells):
        for c in range(columns):
            where = pl.ds(c * height, height)
            inside = pl.ds(PAD, height)
            first[cells + plane, c, inside, :] = own[plane, where, :]
            first[2 * cells + plane, c, inside, :] = high[plane, where, :].astype(jnp.float32)
            value = low[plane, where, :].astype(jnp.float32)
            if plane > 0:
                value = value + low[cells + plane - 1, where, :].astype(jnp.float32)
            first[plane, c, inside, :] = value
    buffers = (first, second)
    for step in range(steps):
        source, target = buffers[step % 2], buffers[(step + 1) % 2]

        def sweep(place, carry, source=source, target=target, step=step):
            planes = range(step + 1, 3 * cells - step - 1)
            row = place * 8
            for plane, block in zip(planes, sweep_rows(source, coef, planes, row, False)):
                for c in range(columns):
                    if step == steps - 1:
                        where = pl.ds(pl.multiple_of(row, 8), 8)
                        out[plane - cells, where, pl.ds(c * TILE, TILE)] = block[c]
                    else:
                        target[plane, c, pl.ds(pl.multiple_of(PAD + row, 8), 8), :] = block[c]
            return carry

        lax.fori_loop(0, height // 8, sweep, 0)


def project_kernel(chunks, source, start, tiles, *refs):
    panels, (*before, out, wide) = refs[: len(chunks)], refs[len(chunks) :]
    shard = panels[0].shape[0] // GROUP
    for given in before:
        out[...] = given[...]
    first = lax.broadcasted_iota(jnp.int32, (8, TILE), 0) < STEPS
    lane = lax.broadcasted_iota(jnp.int32, (8, TILE), 1)
    for chunk, panel in zip(chunks, panels):
        wide[...] = panel[...].astype(jnp.float32)

        def body(group, carry, chunk=chunk):
            number = source[chunk] * shard + group
            sums = jnp.zeros((8, TILE), jnp.float32)
            for place in range(TILE):
                left = start[0, number * GROUP + place]
                right = start[0, number * GROUP + TILE + place]
                cells = jnp.where(
                    first, tiles[pl.ds(PAD + left, 8), :], tiles[pl.ds(PAD - STEPS + right, 8), :]
                )
                row = group * GROUP + place
                rows = jnp.where(first, wide[pl.ds(row, 1), :], wide[pl.ds(row + TILE, 1), :])
                total = jnp.sum(cells * rows, axis=1, keepdims=True)
                sums = jnp.where(lane == place, total, sums)
            out[number] = sums
            return carry

        lax.fori_loop(0, shard, body, 0)


def deposit_kernel(count, source, start, *refs):
    parts, panels = refs[:count], refs[count:-7]
    total, field, rightward, leftward, scaled, *chosen = refs[-7:]
    groups = total.shape[0]
    shard = groups // len(panels)
    cells, per_plane = field.shape[0], field.shape[1]
    tile = start[...]

    def choose(plane):
        target = chosen[plane % 2]
        rows = 64
        for top in range(0, per_plane, rows):
            first = (plane * per_plane + top) * STEPS
            by_row = lax.broadcasted_iota(jnp.int32, (rows, TILE), 0) * STEPS + first
            for left in range(0, tile.shape[1], TILE):
                found = jnp.where(tile[:, left : left + TILE] == by_row, 1.0, 0.0)
                target[pl.ds(top, rows), pl.ds(left, TILE)] = found.astype(jnp.bfloat16)

    choose(0)
    total[...] = tree_sum([part[...] for part in parts])
    numbers = [source[g // shard] * shard + g % shard for g in range(groups)]
    last = [total[n, pl.ds(half * STEPS + STEPS - 1, 1), :] for n in numbers for half in range(2)]
    drive = jnp.concatenate(last, axis=0).T
    for group, number in enumerate(numbers):
        for half in range(2):
            place = 2 * group + half
            rows = panels[group // shard][pl.ds((group % shard) * GROUP + half * TILE, TILE), :]
            head, tail = split(drive[:, place : place + 1] * rows.astype(jnp.float32))
            where = pl.ds(pl.multiple_of(number * GROUP + half * TILE, TILE), TILE)
            scaled[where, pl.ds(0, TILE)] = head
            scaled[where, pl.ds(TILE, TILE)] = tail

    for plane in range(cells):
        if plane < cells - 1:
            choose(plane + 1)
        sums = jnp.dot(chosen[plane % 2][...], scaled[...], preferred_element_type=jnp.float32)
        value = sums[:, :TILE] + sums[:, TILE:]
        field[plane] = value
        head, tail = split(value)
        leftward[plane] = head
        rightward[plane] = head
        if plane > 0:
            rightward[cells + plane - 1] = tail


def call(kernel, out_shape, vmem, scratch=(), smem=0, inputs=0):
    in_specs = [pl.BlockSpec(memory_space=pltpu.SMEM)] * smem
    in_specs += [pl.BlockSpec(memory_space=pltpu.VMEM)] * (inputs - smem)
    out_specs = jax.tree.map(lambda _: pl.BlockSpec(memory_space=pltpu.VMEM), out_shape)
    return pl.pallas_call(
        kernel,
        out_shape=out_shape,
        in_specs=in_specs,
        out_specs=out_specs,
        scratch_shapes=list(scratch),
        compiler_params=pltpu.CompilerParams(vmem_limit_bytes=vmem * 1024 * 1024),
        cost_estimate=pl.CostEstimate(flops=1024, bytes_accessed=1024, transcendentals=0),
    )


def gathered_panel(panel, axis, ready):
    count = lax.axis_size(axis)
    shards, mask = {0: panel}, count // 2
    while mask:
        pairs = [(i, i ^ mask) for i in range(count)]
        for held in sorted(shards):
            operand = tied(shards[held], ready) if held else panel
            shards[held | mask] = lax.ppermute(operand, axis, pairs)
        mask //= 2
    return [shards[k] for k in range(1, count)]


def tied(value, *others):
    return lax.optimization_barrier((value,) + others)[0]


def tree_sum(parts):
    while len(parts) > 1:
        parts = [parts[i] + parts[i + 1] for i in range(0, len(parts), 2)]
    return parts[0]


def summands(part, axis):
    count = lax.axis_size(axis)
    if count & (count - 1):
        return [lax.psum(part, axis)]
    done, parts = 1, [part]
    for span in (2, 4, 4, 4, 4):
        span = min(span, count // done)
        if span > 1:
            part = tree_sum(parts)
            pairs = [[(i, i ^ (k * done)) for i in range(count)] for k in range(1, span)]
            parts = [part] + [lax.ppermute(part, axis, pair) for pair in pairs]
            done *= span
    return parts


def local(sensor_field, courant, diffusivity, probe_offset, tile_index, actuator_panel):
    slabs, probes = lax.axis_size("state"), lax.axis_size("probe")
    own = sensor_field[0]
    cells, height, width = own.shape
    columns = width // TILE
    tile_total = cells * height * columns
    actuators = tile_index.shape[1]
    groups = actuators // GROUP
    shard = groups // probes
    planes = 3 * cells
    f32, bf16 = jnp.float32, jnp.bfloat16

    source = lax.axis_index("probe") ^ jnp.arange(probes, dtype=jnp.int32)
    head = own.astype(bf16)
    tail = (own - head.astype(f32)).astype(bf16)[: cells - 1]
    low = lax.ppermute(head, "state", shift_pairs(slabs, 1))
    both = jnp.concatenate([head, tail], axis=0)
    high = lax.ppermute(both, "state", shift_pairs(slabs, -1))

    shifted, coef, start, panel = call(
        prelude_kernel,
        (
            jax.ShapeDtypeStruct((cells, columns, height, TILE), f32),
            jax.ShapeDtypeStruct((5, height, TILE), f32),
            jax.ShapeDtypeStruct(tile_index.shape, jnp.int32),
            jax.ShapeDtypeStruct(actuator_panel.shape[1:], bf16),
        ),
        vmem=8,
        smem=1,
        inputs=6,
    )(probe_offset, own, courant[None], diffusivity[None], tile_index, actuator_panel[0])

    field_shape = pltpu.VMEM((planes, columns, height + 2 * PAD, TILE), f32)
    tiles = call(
        adjoint_kernel,
        jax.ShapeDtypeStruct((tile_total * STEPS + 2 * PAD, TILE), f32),
        vmem=10,
        scratch=(field_shape, field_shape),
        smem=1,
        inputs=5,
    )(probe_offset, coef, shifted, low, high)

    panels = [panel] + gathered_panel(actuator_panel[0], "probe", coef)
    every = list(range(probes))

    def project(chunks, *given):
        return call(
            lambda *refs: project_kernel(chunks, *refs),
            jax.ShapeDtypeStruct((groups, 2 * STEPS, TILE), f32),
            vmem=6,
            scratch=(pltpu.VMEM((shard * GROUP, TILE), f32),),
            smem=2,
            inputs=3 + len(chunks) + len(given),
        )(source, start, tiles, *[panels[chunk] for chunk in chunks], *given)

    before = project(every[:-1])
    parts = summands(project(every[-1:], before), "state")
    payload = jax.ShapeDtypeStruct((2 * cells - 1, height * columns, TILE), bf16)
    heads = jax.ShapeDtypeStruct((cells, height * columns, TILE), bf16)
    total, forced, rightward, leftward = call(
        lambda *refs: deposit_kernel(len(parts), *refs),
        (
            jax.ShapeDtypeStruct(before.shape, f32),
            jax.ShapeDtypeStruct((cells, height * columns, TILE), f32),
            payload,
            heads,
        ),
        vmem=16,
        scratch=(
            pltpu.VMEM((actuators, 2 * TILE), bf16),
            pltpu.VMEM((height * columns, actuators), bf16),
            pltpu.VMEM((height * columns, actuators), bf16),
        ),
        smem=1,
        inputs=2 + len(parts) + probes,
    )(source, start, *parts, *panels)
    from_low = lax.ppermute(rightward, "state", shift_pairs(slabs, 1))
    from_high = lax.ppermute(leftward, "state", shift_pairs(slabs, -1))
    response = call(
        forward_kernel,
        jax.ShapeDtypeStruct((cells, height, width), f32),
        vmem=10,
        scratch=(field_shape, field_shape),
        inputs=4,
    )(coef, forced, from_low, from_high)
    projections = total.reshape(groups, 2, STEPS, TILE).transpose(2, 0, 1, 3)
    return projections.reshape(STEPS, 1, actuators), response[None]


def solution(mesh):
    return jax.shard_map(
        local,
        mesh=mesh,
        in_specs=(
            P("probe", "state", None, None),
            P(),
            P(),
            P("probe"),
            P("state", None),
            P("state", "probe", None),
        ),
        out_specs=(P(None, "probe", None), P("probe", "state", None, None)),
        check_vma=False,
    )
```

```python
import jax
import jax.numpy as jnp
from jax import lax
from jax.experimental import pallas as pl
from jax.experimental.pallas import tpu as pltpu
from jax.sharding import PartitionSpec as P

TILE = 128
STEPS = 4
PAD = 8
GROUP = 256


def shift_pairs(count, by):
    return [(i, (i + by) % count) for i in range(count)]


def clear_pads(buffer):
    planes, columns, rows, lanes = buffer.shape
    edge = jnp.zeros((columns, PAD, lanes), buffer.dtype)

    def body(plane, carry):
        buffer[plane, :, :PAD, :] = edge
        buffer[plane, :, rows - PAD :, :] = edge
        return carry

    lax.fori_loop(0, planes, body, 0)


def sweep_rows(source, coef, planes, row, adjoint):
    here = pl.ds(pl.multiple_of(PAD + row, 8), 8)
    block = pl.ds(pl.multiple_of(row, 8), 8)
    columns = source.shape[1]
    lane = lax.broadcasted_iota(jnp.int32, (8, TILE), 1)
    weights = [coef[place, block, :] for place in range(5)]
    lower, centre = source[planes[0] - 1, :, here, :], source[planes[0], :, here, :]
    out = []
    for plane in planes:
        upper = source[plane + 1, :, here, :]
        above = source[plane, :, pl.ds(PAD + row + 1, 8), :]
        below = source[plane, :, pl.ds(PAD + row - 1, 8), :]
        left = [pltpu.roll(centre[c], TILE - 1, 1) for c in range(columns)]
        right = [pltpu.roll(centre[c], 1, 1) for c in range(columns)]
        results = []
        for c in range(columns):
            upper_z = jnp.where(lane == TILE - 1, left[(c + 1) % columns], left[c])
            lower_z = jnp.where(lane == 0, right[(c - 1) % columns], right[c])
            total = weights[0] * centre[c]
            if adjoint:
                total = total + weights[1] * upper[c]
                total = total + weights[2] * (lower[c] + (upper_z + lower_z))
                total = total + (weights[3] * above[c] + weights[4] * below[c])
            else:
                total = total + weights[1] * lower[c]
                total = total + weights[2] * ((upper[c] + (upper_z + lower_z)) + (above[c] + below[c]))
            results.append(total)
        out.append(results)
        lower, centre = centre, upper
    return out


def split(value):
    high = value.astype(jnp.bfloat16)
    low = (value - high.astype(jnp.float32)).astype(jnp.bfloat16)
    return high, low


def shifted_plane(field, plane, offset):
    height, width = field.shape[1:]
    columns = width // TILE
    turn, rest = offset // TILE, offset % TILE
    lane = lax.broadcasted_iota(jnp.int32, (height, TILE), 1)
    parts = [field[plane, :, pl.ds(c * TILE, TILE)].astype(jnp.float32) for c in range(columns)]
    rolled = [pltpu.roll(part, rest, 1) for part in parts]
    return [
        (lax.rem(c + turn, columns), jnp.where(lane >= rest, rolled[c], rolled[c - 1]))
        for c in range(columns)
    ]


def prelude_kernel(offset, field, courant, diffusivity, tile, panel, own, coef, start, kept):
    columns, height = own.shape[1:3]

    def load(plane, carry):
        for column, value in shifted_plane(field, plane, offset[0]):
            own[plane, column] = value
        return carry

    lax.fori_loop(0, field.shape[0], load, 0)
    kept[...] = panel[...]
    padding = jnp.zeros((6, height), jnp.float32)
    upright = jnp.concatenate([courant[...], diffusivity[...], padding], axis=0).T
    speed = jnp.broadcast_to(upright[:, 0:1], (height, TILE))
    rate = jnp.broadcast_to(upright[:, 1:2], (height, TILE))
    edge = jnp.zeros((1, TILE), jnp.float32)
    coef[0] = 1.0 - speed - 6.0 * rate
    coef[1] = speed + rate
    coef[2] = rate
    coef[3] = jnp.concatenate([rate[1:], edge], axis=0)
    coef[4] = jnp.concatenate([edge, rate[:-1]], axis=0)
    numbers = tile[...]
    inside = numbers & (columns * height - 1)
    numbers = (numbers - inside) + (inside & (columns - 1)) * height + inside // columns
    start[...] = numbers * STEPS


def adjoint_kernel(offset, coef, own, low, high, tiles, first, second):
    cells, columns, height = own.shape[:3]
    steps = STEPS
    edge = jnp.zeros((PAD, TILE), jnp.float32)
    tiles[:PAD, :] = edge
    tiles[tiles.shape[0] - PAD :, :] = edge
    inside = pl.ds(PAD, height)
    clear_pads(first)
    clear_pads(second)

    def load(plane, carry):
        for slab, field in ((0, low), (2, high)):
            for column, value in shifted_plane(field, plane, offset[0]):
                first[slab * cells + plane, column, inside, :] = value
        first[cells + plane, :, inside, :] = own[plane]
        return carry

    lax.fori_loop(0, cells, load, 0)
    buffers = (first, second)
    for step in range(steps):
        source, target = buffers[step % 2], buffers[(step + 1) % 2]

        def sweep(place, carry, source=source, target=target, step=step):
            planes = range(step + 1, 3 * cells - step - 1)
            row = place * 8
            for plane, block in zip(planes, sweep_rows(source, coef, planes, row, True)):
                for c in range(columns):
                    if step < steps - 1:
                        where = pl.ds(pl.multiple_of(PAD + row, 8), 8)
                        target[plane, c, where, :] = block[c]
                    if cells <= plane < 2 * cells:
                        number = ((plane - cells) * columns + c) * height + row
                        tiles[pl.ds(PAD + number * steps + step, 8, stride=steps), :] = block[c]
            return carry

        lax.fori_loop(0, height // 8, sweep, 0, unroll=4)


def forward_kernel(coef, own, low, high, out, first, second):
    cells, height, width = out.shape
    columns = width // TILE
    steps = STEPS
    clear_pads(first)
    clear_pads(second)
    for plane in range(cells):
        for c in range(columns):
            where = pl.ds(c * height, height)
            inside = pl.ds(PAD, height)
            first[cells + plane, c, inside, :] = own[plane, where, :]
            first[2 * cells + plane, c, inside, :] = high[plane, where, :].astype(jnp.float32)
            value = low[plane, where, :].astype(jnp.float32)
            if plane > 0:
                value = value + low[cells + plane - 1, where, :].astype(jnp.float32)
            first[plane, c, inside, :] = value
    buffers = (first, second)
    for step in range(steps):
        source, target = buffers[step % 2], buffers[(step + 1) % 2]

        def sweep(place, carry, source=source, target=target, step=step):
            planes = range(step + 1, 3 * cells - step - 1)
            row = place * 8
            for plane, block in zip(planes, sweep_rows(source, coef, planes, row, False)):
                for c in range(columns):
                    if step == steps - 1:
                        where = pl.ds(pl.multiple_of(row, 8), 8)
                        out[plane - cells, where, pl.ds(c * TILE, TILE)] = block[c]
                    else:
                        target[plane, c, pl.ds(pl.multiple_of(PAD + row, 8), 8), :] = block[c]
            return carry

        lax.fori_loop(0, height // 8, sweep, 0, unroll=4)


def project_kernel(chunks, source, start, tiles, *refs):
    panels, (*before, out, wide) = refs[: len(chunks)], refs[len(chunks) :]
    shard = panels[0].shape[0] // GROUP
    for given in before:
        out[...] = given[...]
    first = lax.broadcasted_iota(jnp.int32, (8, TILE), 0) < STEPS
    lane = lax.broadcasted_iota(jnp.int32, (8, TILE), 1)
    for chunk, panel in zip(chunks, panels):
        wide[...] = panel[...].astype(jnp.float32)

        def body(group, carry, chunk=chunk):
            number = source[chunk] * shard + group
            sums = jnp.zeros((8, TILE), jnp.float32)
            for place in range(TILE):
                left = start[0, number * GROUP + place]
                right = start[0, number * GROUP + TILE + place]
                cells = jnp.where(
                    first, tiles[pl.ds(PAD + left, 8), :], tiles[pl.ds(PAD - STEPS + right, 8), :]
                )
                row = group * GROUP + place
                rows = jnp.where(first, wide[pl.ds(row, 1), :], wide[pl.ds(row + TILE, 1), :])
                total = jnp.sum(cells * rows, axis=1, keepdims=True)
                sums = jnp.where(lane == place, total, sums)
            out[number] = sums
            return carry

        lax.fori_loop(0, shard, body, 0)


def deposit_kernel(count, source, start, *refs):
    parts, panels = refs[:count], refs[count:-7]
    total, field, rightward, leftward, scaled, *chosen = refs[-7:]
    groups = total.shape[0]
    shard = groups // len(panels)
    cells, per_plane = field.shape[0], field.shape[1]
    tile = start[...].astype(jnp.int16)
    one, none = jnp.ones((), jnp.bfloat16), jnp.zeros((), jnp.bfloat16)

    def choose(plane):
        target = chosen[plane % 2]
        rows = 64
        for top in range(0, per_plane, rows):
            first = (plane * per_plane + top) * STEPS
            by_row = lax.broadcasted_iota(jnp.int32, (rows, TILE), 0) * STEPS + first
            by_row = by_row.astype(jnp.int16)
            for left in range(0, tile.shape[1], TILE):
                found = jnp.where(tile[:, left : left + TILE] == by_row, one, none)
                target[pl.ds(top, rows), pl.ds(left, TILE)] = found

    choose(0)
    total[...] = tree_sum([part[...] for part in parts])
    numbers = [source[g // shard] * shard + g % shard for g in range(groups)]
    last = [total[n, pl.ds(half * STEPS + STEPS - 1, 1), :] for n in numbers for half in range(2)]
    drive = jnp.concatenate(last, axis=0).T
    for group, number in enumerate(numbers):
        for half in range(2):
            place = 2 * group + half
            rows = panels[group // shard][pl.ds((group % shard) * GROUP + half * TILE, TILE), :]
            head, tail = split(drive[:, place : place + 1] * rows.astype(jnp.float32))
            where = pl.ds(pl.multiple_of(number * GROUP + half * TILE, TILE), TILE)
            scaled[where, pl.ds(0, TILE)] = head
            scaled[where, pl.ds(TILE, TILE)] = tail

    for plane in range(cells):
        if plane < cells - 1:
            choose(plane + 1)
        sums = jnp.dot(chosen[plane % 2][...], scaled[...], preferred_element_type=jnp.float32)
        value = sums[:, :TILE] + sums[:, TILE:]
        field[plane] = value
        head, tail = split(value)
        leftward[plane] = head
        rightward[plane] = head
        if plane > 0:
            rightward[cells + plane - 1] = tail


def call(kernel, out_shape, vmem, scratch=(), smem=0, inputs=0):
    in_specs = [pl.BlockSpec(memory_space=pltpu.SMEM)] * smem
    in_specs += [pl.BlockSpec(memory_space=pltpu.VMEM)] * (inputs - smem)
    out_specs = jax.tree.map(lambda _: pl.BlockSpec(memory_space=pltpu.VMEM), out_shape)
    return pl.pallas_call(
        kernel,
        out_shape=out_shape,
        in_specs=in_specs,
        out_specs=out_specs,
        scratch_shapes=list(scratch),
        compiler_params=pltpu.CompilerParams(vmem_limit_bytes=vmem * 1024 * 1024),
        cost_estimate=pl.CostEstimate(flops=1024, bytes_accessed=1024, transcendentals=0),
    )


def gathered_panel(panel, axis, ready):
    count = lax.axis_size(axis)
    shards, mask = {0: panel}, count // 2
    while mask:
        pairs = [(i, i ^ mask) for i in range(count)]
        for held in sorted(shards):
            operand = tied(shards[held], ready) if held else panel
            shards[held | mask] = lax.ppermute(operand, axis, pairs)
        mask //= 2
    return [shards[k] for k in range(1, count)]


def tied(value, *others):
    return lax.optimization_barrier((value,) + others)[0]


def tree_sum(parts):
    while len(parts) > 1:
        parts = [parts[i] + parts[i + 1] for i in range(0, len(parts), 2)]
    return parts[0]


def summands(part, axis):
    count = lax.axis_size(axis)
    if count & (count - 1):
        return [lax.psum(part, axis)]
    done, parts = 1, [part]
    for span in [2] * count.bit_length():
        span = min(span, count // done)
        if span > 1:
            part = tree_sum(parts)
            pairs = [[(i, i ^ (k * done)) for i in range(count)] for k in range(1, span)]
            parts = [part] + [lax.ppermute(part, axis, pair) for pair in pairs]
            done *= span
    return parts


def local(sensor_field, courant, diffusivity, probe_offset, tile_index, actuator_panel):
    slabs, probes = lax.axis_size("state"), lax.axis_size("probe")
    own = sensor_field[0]
    cells, height, width = own.shape
    columns = width // TILE
    tile_total = cells * height * columns
    actuators = tile_index.shape[1]
    groups = actuators // GROUP
    shard = groups // probes
    planes = 3 * cells
    f32, bf16 = jnp.float32, jnp.bfloat16

    source = lax.axis_index("probe") ^ jnp.arange(probes, dtype=jnp.int32)
    high = lax.ppermute(own, "state", shift_pairs(slabs, -1))
    low = lax.ppermute(own.astype(bf16), "state", shift_pairs(slabs, 1))

    shifted, coef, start, panel = call(
        prelude_kernel,
        (
            jax.ShapeDtypeStruct((cells, columns, height, TILE), f32),
            jax.ShapeDtypeStruct((5, height, TILE), f32),
            jax.ShapeDtypeStruct(tile_index.shape, jnp.int32),
            jax.ShapeDtypeStruct(actuator_panel.shape[1:], bf16),
        ),
        vmem=8,
        smem=1,
        inputs=6,
    )(probe_offset, own, courant[None], diffusivity[None], tile_index, actuator_panel[0])

    field_shape = pltpu.VMEM((planes, columns, height + 2 * PAD, TILE), f32)
    tiles = call(
        adjoint_kernel,
        jax.ShapeDtypeStruct((tile_total * STEPS + 2 * PAD, TILE), f32),
        vmem=10,
        scratch=(field_shape, field_shape),
        smem=1,
        inputs=5,
    )(probe_offset, coef, shifted, low, high)

    panels = [panel] + gathered_panel(actuator_panel[0], "probe", tiles)
    every = list(range(probes))

    def project(chunks, *given):
        return call(
            lambda *refs: project_kernel(chunks, *refs),
            jax.ShapeDtypeStruct((groups, 2 * STEPS, TILE), f32),
            vmem=6,
            scratch=(pltpu.VMEM((shard * GROUP, TILE), f32),),
            smem=2,
            inputs=3 + len(chunks) + len(given),
        )(source, start, tiles, *[panels[chunk] for chunk in chunks], *given)

    before = project(every[:-1])
    parts = summands(project(every[-1:], before), "state")
    payload = jax.ShapeDtypeStruct((2 * cells - 1, height * columns, TILE), bf16)
    heads = jax.ShapeDtypeStruct((cells, height * columns, TILE), bf16)
    total, forced, rightward, leftward = call(
        lambda *refs: deposit_kernel(len(parts), *refs),
        (
            jax.ShapeDtypeStruct(before.shape, f32),
            jax.ShapeDtypeStruct((cells, height * columns, TILE), f32),
            payload,
            heads,
        ),
        vmem=16,
        scratch=(
            pltpu.VMEM((actuators, 2 * TILE), bf16),
            pltpu.VMEM((height * columns, actuators), bf16),
            pltpu.VMEM((height * columns, actuators), bf16),
        ),
        smem=1,
        inputs=2 + len(parts) + probes,
    )(source, start, *parts, *panels)
    from_low = lax.ppermute(rightward, "state", shift_pairs(slabs, 1))
    from_high = lax.ppermute(leftward, "state", shift_pairs(slabs, -1))
    response = call(
        forward_kernel,
        jax.ShapeDtypeStruct((cells, height, width), f32),
        vmem=10,
        scratch=(field_shape, field_shape),
        inputs=4,
    )(coef, forced, from_low, from_high)
    projections = total.reshape(groups, 2, STEPS, TILE).transpose(2, 0, 1, 3)
    return projections.reshape(STEPS, 1, actuators), response[None]


def solution(mesh):
    return jax.shard_map(
        local,
        mesh=mesh,
        in_specs=(
            P("probe", "state", None, None),
            P(),
            P(),
            P("probe"),
            P("state", None),
            P("state", "probe", None),
        ),
        out_specs=(P(None, "probe", None), P("probe", "state", None, None)),
        check_vma=False,
    )
```

```python
import jax
import jax.numpy as jnp
from jax import lax
from jax.experimental import pallas as pl
from jax.experimental.pallas import tpu as pltpu
from jax.sharding import PartitionSpec as P

TILE = 128
STEPS = 4
PAD = 8
GROUP = 256


def shift_pairs(count, by):
    return [(i, (i + by) % count) for i in range(count)]


def clear_pads(buffer):
    planes, columns, rows, lanes = buffer.shape
    edge = jnp.zeros((columns, PAD, lanes), buffer.dtype)

    def body(plane, carry):
        buffer[plane, :, :PAD, :] = edge
        buffer[plane, :, rows - PAD :, :] = edge
        return carry

    lax.fori_loop(0, planes, body, 0)


def sweep_rows(source, coef, planes, row, adjoint):
    here = pl.ds(pl.multiple_of(PAD + row, 8), 8)
    block = pl.ds(pl.multiple_of(row, 8), 8)
    columns = source.shape[1]
    lane = lax.broadcasted_iota(jnp.int32, (8, TILE), 1)
    weights = [coef[place, block, :] for place in range(5)]
    lower, centre = source[planes[0] - 1, :, here, :], source[planes[0], :, here, :]
    out = []
    for plane in planes:
        upper = source[plane + 1, :, here, :]
        above = source[plane, :, pl.ds(PAD + row + 1, 8), :]
        below = source[plane, :, pl.ds(PAD + row - 1, 8), :]
        left = [pltpu.roll(centre[c], TILE - 1, 1) for c in range(columns)]
        right = [pltpu.roll(centre[c], 1, 1) for c in range(columns)]
        results = []
        for c in range(columns):
            upper_z = jnp.where(lane == TILE - 1, left[(c + 1) % columns], left[c])
            lower_z = jnp.where(lane == 0, right[(c - 1) % columns], right[c])
            total = weights[0] * centre[c]
            if adjoint:
                total = total + weights[1] * upper[c]
                total = total + weights[2] * (lower[c] + (upper_z + lower_z))
                total = total + (weights[3] * above[c] + weights[4] * below[c])
            else:
                total = total + weights[1] * lower[c]
                total = total + weights[2] * ((upper[c] + (upper_z + lower_z)) + (above[c] + below[c]))
            results.append(total)
        out.append(results)
        lower, centre = centre, upper
    return out


def split(value):
    high = value.astype(jnp.bfloat16)
    low = (value - high.astype(jnp.float32)).astype(jnp.bfloat16)
    return high, low


def shifted_plane(field, plane, offset):
    height, width = field.shape[1:]
    columns = width // TILE
    turn, rest = offset // TILE, offset % TILE
    lane = lax.broadcasted_iota(jnp.int32, (height, TILE), 1)
    parts = [field[plane, :, pl.ds(c * TILE, TILE)].astype(jnp.float32) for c in range(columns)]
    rolled = [pltpu.roll(part, rest, 1) for part in parts]
    return [
        (lax.rem(c + turn, columns), jnp.where(lane >= rest, rolled[c], rolled[c - 1]))
        for c in range(columns)
    ]


def prelude_kernel(offset, field, courant, diffusivity, tile, panel, own, coef, start, kept):
    columns, height = own.shape[1:3]

    def load(plane, carry):
        for column, value in shifted_plane(field, plane, offset[0]):
            own[plane, column] = value
        return carry

    lax.fori_loop(0, field.shape[0], load, 0)
    kept[...] = panel[...]
    padding = jnp.zeros((6, height), jnp.float32)
    upright = jnp.concatenate([courant[...], diffusivity[...], padding], axis=0).T
    speed = jnp.broadcast_to(upright[:, 0:1], (height, TILE))
    rate = jnp.broadcast_to(upright[:, 1:2], (height, TILE))
    edge = jnp.zeros((1, TILE), jnp.float32)
    coef[0] = 1.0 - speed - 6.0 * rate
    coef[1] = speed + rate
    coef[2] = rate
    coef[3] = jnp.concatenate([rate[1:], edge], axis=0)
    coef[4] = jnp.concatenate([edge, rate[:-1]], axis=0)
    numbers = tile[...]
    inside = numbers & (columns * height - 1)
    numbers = (numbers - inside) + (inside & (columns - 1)) * height + inside // columns
    start[...] = numbers * STEPS


def adjoint_kernel(offset, coef, own, low, high, tiles, first, second):
    cells, columns, height = own.shape[:3]
    steps = STEPS
    edge = jnp.zeros((PAD, TILE), jnp.float32)
    tiles[:PAD, :] = edge
    tiles[tiles.shape[0] - PAD :, :] = edge
    inside = pl.ds(PAD, height)
    clear_pads(first)
    clear_pads(second)

    def load(plane, carry):
        for slab, field in ((0, low), (2, high)):
            for column, value in shifted_plane(field, plane, offset[0]):
                first[slab * cells + plane, column, inside, :] = value
        first[cells + plane, :, inside, :] = own[plane]
        return carry

    lax.fori_loop(0, cells, load, 0)
    buffers = (first, second)
    for step in range(steps):
        source, target = buffers[step % 2], buffers[(step + 1) % 2]

        def sweep(place, carry, source=source, target=target, step=step):
            planes = range(step + 1, 3 * cells - step - 1)
            row = place * 8
            for plane, block in zip(planes, sweep_rows(source, coef, planes, row, True)):
                for c in range(columns):
                    if step < steps - 1:
                        where = pl.ds(pl.multiple_of(PAD + row, 8), 8)
                        target[plane, c, where, :] = block[c]
                    if cells <= plane < 2 * cells:
                        number = ((plane - cells) * columns + c) * height + row
                        tiles[pl.ds(PAD + number * steps + step, 8, stride=steps), :] = block[c]
            return carry

        lax.fori_loop(0, height // 8, sweep, 0, unroll=8)


def forward_kernel(coef, own, low, high, out, first, second):
    cells, height, width = out.shape
    columns = width // TILE
    steps = STEPS
    clear_pads(first)
    clear_pads(second)
    for plane in range(cells):
        for c in range(columns):
            where = pl.ds(c * height, height)
            inside = pl.ds(PAD, height)
            first[cells + plane, c, inside, :] = own[plane, where, :]
            first[2 * cells + plane, c, inside, :] = high[plane, where, :].astype(jnp.float32)
            value = low[plane, where, :].astype(jnp.float32)
            if plane > 0:
                value = value + low[cells + plane - 1, where, :].astype(jnp.float32)
            first[plane, c, inside, :] = value
    buffers = (first, second)
    for step in range(steps):
        source, target = buffers[step % 2], buffers[(step + 1) % 2]

        def sweep(place, carry, source=source, target=target, step=step):
            planes = range(step + 1, 3 * cells - step - 1)
            row = place * 8
            for plane, block in zip(planes, sweep_rows(source, coef, planes, row, False)):
                for c in range(columns):
                    if step == steps - 1:
                        where = pl.ds(pl.multiple_of(row, 8), 8)
                        out[plane - cells, where, pl.ds(c * TILE, TILE)] = block[c]
                    else:
                        target[plane, c, pl.ds(pl.multiple_of(PAD + row, 8), 8), :] = block[c]
            return carry

        lax.fori_loop(0, height // 8, sweep, 0, unroll=8)


def project_kernel(places, shard, source, start, tiles, *refs):
    panels, (*before, out, wide) = refs[: len(places)], refs[len(places) :]
    for given in before:
        out[...] = given[...]
    first = lax.broadcasted_iota(jnp.int32, (8, TILE), 0) < STEPS
    lane = lax.broadcasted_iota(jnp.int32, (8, TILE), 1)
    for (chunk, offset), panel in zip(places, panels):
        wide[: panel.shape[0], :] = panel[...].astype(jnp.float32)

        def body(group, carry, chunk=chunk, offset=offset):
            number = source[chunk] * shard + offset + group
            sums = jnp.zeros((8, TILE), jnp.float32)
            for place in range(TILE):
                left = start[0, number * GROUP + place]
                right = start[0, number * GROUP + TILE + place]
                cells = jnp.where(
                    first, tiles[pl.ds(PAD + left, 8), :], tiles[pl.ds(PAD - STEPS + right, 8), :]
                )
                row = group * GROUP + place
                rows = jnp.where(first, wide[pl.ds(row, 1), :], wide[pl.ds(row + TILE, 1), :])
                total = jnp.sum(cells * rows, axis=1, keepdims=True)
                sums = jnp.where(lane == place, total, sums)
            out[number] = sums
            return carry

        lax.fori_loop(0, panel.shape[0] // GROUP, body, 0)


def deposit_kernel(count, places, shard, source, start, *refs):
    parts, panels = refs[:count], refs[count:-7]
    total, field, rightward, leftward, scaled, *chosen = refs[-7:]
    cells, per_plane = field.shape[0], field.shape[1]
    tile = start[...].astype(jnp.int16)
    one, none = jnp.ones((), jnp.bfloat16), jnp.zeros((), jnp.bfloat16)

    def choose(plane):
        target = chosen[plane % 2]
        rows = 64
        for top in range(0, per_plane, rows):
            first = (plane * per_plane + top) * STEPS
            by_row = lax.broadcasted_iota(jnp.int32, (rows, TILE), 0) * STEPS + first
            by_row = by_row.astype(jnp.int16)
            for left in range(0, tile.shape[1], TILE):
                found = jnp.where(tile[:, left : left + TILE] == by_row, one, none)
                target[pl.ds(top, rows), pl.ds(left, TILE)] = found

    choose(0)
    total[...] = tree_sum([part[...] for part in parts])
    blocks = []
    for (chunk, offset), panel in zip(places, panels):
        for group in range(panel.shape[0] // GROUP):
            number = source[chunk] * shard + offset + group
            blocks += [(number, half, panel, group * GROUP + half * TILE) for half in range(2)]
    last = [total[number, pl.ds(half * STEPS + STEPS - 1, 1), :] for number, half, _, _ in blocks]
    drive = jnp.concatenate(last, axis=0).T
    for place, (number, half, panel, row) in enumerate(blocks):
        rows = panel[pl.ds(row, TILE), :].astype(jnp.float32)
        head, tail = split(drive[:, place : place + 1] * rows)
        where = pl.ds(pl.multiple_of(number * GROUP + half * TILE, TILE), TILE)
        scaled[where, pl.ds(0, TILE)] = head
        scaled[where, pl.ds(TILE, TILE)] = tail

    for plane in range(cells):
        if plane < cells - 1:
            choose(plane + 1)
        sums = jnp.dot(chosen[plane % 2][...], scaled[...], preferred_element_type=jnp.float32)
        value = sums[:, :TILE] + sums[:, TILE:]
        field[plane] = value
        head, tail = split(value)
        leftward[plane] = head
        rightward[plane] = head
        if plane > 0:
            rightward[cells + plane - 1] = tail


def call(kernel, out_shape, vmem, scratch=(), smem=0, inputs=0):
    in_specs = [pl.BlockSpec(memory_space=pltpu.SMEM)] * smem
    in_specs += [pl.BlockSpec(memory_space=pltpu.VMEM)] * (inputs - smem)
    out_specs = jax.tree.map(lambda _: pl.BlockSpec(memory_space=pltpu.VMEM), out_shape)
    return pl.pallas_call(
        kernel,
        out_shape=out_shape,
        in_specs=in_specs,
        out_specs=out_specs,
        scratch_shapes=list(scratch),
        compiler_params=pltpu.CompilerParams(vmem_limit_bytes=vmem * 1024 * 1024),
        cost_estimate=pl.CostEstimate(flops=1024, bytes_accessed=1024, transcendentals=0),
    )


def gathered_panel(panel, axis, soon, late):
    count, rows = lax.axis_size(axis), panel.shape[0]
    shards, mask = {0: [panel]}, count // 2
    while mask:
        pairs = [(i, i ^ mask) for i in range(count)]
        for held in sorted(shards):
            pieces = shards[held]
            if held:
                ready = (soon, late) if len(pieces) > 1 else (late,)
                pieces = [tied(piece, after) for piece, after in zip(pieces, ready)]
            elif len(shards) == 1 and rows >= 2 * GROUP:
                pieces = [panel[: rows // 2], panel[rows // 2 :]]
            shards[held | mask] = [lax.ppermute(piece, axis, pairs) for piece in pieces]
        mask //= 2
    return [shards[k] for k in range(1, count)]


def layout(panels):
    places = []
    for chunk, pieces in panels:
        first = 0
        for piece in pieces:
            places.append((chunk, first))
            first += piece.shape[0] // GROUP
    return places


def tied(value, *others):
    return lax.optimization_barrier((value,) + others)[0]


def tree_sum(parts):
    while len(parts) > 1:
        parts = [parts[i] + parts[i + 1] for i in range(0, len(parts), 2)]
    return parts[0]


def summands(part, axis):
    count = lax.axis_size(axis)
    if count & (count - 1):
        return [lax.psum(part, axis)]
    done, parts = 1, [part]
    for span in (2, 4, 4, 4, 4):
        span = min(span, count // done)
        if span > 1:
            part = tree_sum(parts)
            pairs = [[(i, i ^ (k * done)) for i in range(count)] for k in range(1, span)]
            parts = [part] + [lax.ppermute(part, axis, pair) for pair in pairs]
            done *= span
    return parts


def local(sensor_field, courant, diffusivity, probe_offset, tile_index, actuator_panel):
    slabs, probes = lax.axis_size("state"), lax.axis_size("probe")
    own = sensor_field[0]
    cells, height, width = own.shape
    columns = width // TILE
    tile_total = cells * height * columns
    actuators = tile_index.shape[1]
    groups = actuators // GROUP
    shard = groups // probes
    planes = 3 * cells
    f32, bf16 = jnp.float32, jnp.bfloat16

    source = lax.axis_index("probe") ^ jnp.arange(probes, dtype=jnp.int32)
    high = lax.ppermute(own, "state", shift_pairs(slabs, -1))
    low = lax.ppermute(own.astype(bf16), "state", shift_pairs(slabs, 1))

    shifted, coef, start, panel = call(
        prelude_kernel,
        (
            jax.ShapeDtypeStruct((cells, columns, height, TILE), f32),
            jax.ShapeDtypeStruct((5, height, TILE), f32),
            jax.ShapeDtypeStruct(tile_index.shape, jnp.int32),
            jax.ShapeDtypeStruct(actuator_panel.shape[1:], bf16),
        ),
        vmem=8,
        smem=1,
        inputs=6,
    )(probe_offset, own, courant[None], diffusivity[None], tile_index, actuator_panel[0])

    field_shape = pltpu.VMEM((planes, columns, height + 2 * PAD, TILE), f32)
    tiles = call(
        adjoint_kernel,
        jax.ShapeDtypeStruct((tile_total * STEPS + 2 * PAD, TILE), f32),
        vmem=10,
        scratch=(field_shape, field_shape),
        smem=1,
        inputs=5,
    )(probe_offset, coef, shifted, low, high)

    panels = list(enumerate([[panel]] + gathered_panel(actuator_panel[0], "probe", coef, tiles)))

    def project(shards, *given):
        pieces = [piece for _, pieces in shards for piece in pieces]
        return call(
            lambda *refs: project_kernel(layout(shards), shard, *refs),
            jax.ShapeDtypeStruct((groups, 2 * STEPS, TILE), f32),
            vmem=6,
            scratch=(pltpu.VMEM((shard * GROUP, TILE), f32),),
            smem=2,
            inputs=3 + len(pieces) + len(given),
        )(source, start, tiles, *pieces, *given)

    before = project(panels[:-1])
    parts = summands(project(panels[-1:], before), "state")
    pieces = [piece for _, pieces in panels for piece in pieces]
    payload = jax.ShapeDtypeStruct((2 * cells - 1, height * columns, TILE), bf16)
    heads = jax.ShapeDtypeStruct((cells, height * columns, TILE), bf16)
    total, forced, rightward, leftward = call(
        lambda *refs: deposit_kernel(len(parts), layout(panels), shard, *refs),
        (
            jax.ShapeDtypeStruct(before.shape, f32),
            jax.ShapeDtypeStruct((cells, height * columns, TILE), f32),
            payload,
            heads,
        ),
        vmem=16,
        scratch=(
            pltpu.VMEM((actuators, 2 * TILE), bf16),
            pltpu.VMEM((height * columns, actuators), bf16),
            pltpu.VMEM((height * columns, actuators), bf16),
        ),
        smem=1,
        inputs=2 + len(parts) + len(pieces),
    )(source, start, *parts, *pieces)
    from_low = lax.ppermute(rightward, "state", shift_pairs(slabs, 1))
    from_high = lax.ppermute(leftward, "state", shift_pairs(slabs, -1))
    response = call(
        forward_kernel,
        jax.ShapeDtypeStruct((cells, height, width), f32),
        vmem=10,
        scratch=(field_shape, field_shape),
        inputs=4,
    )(coef, forced, from_low, from_high)
    projections = total.reshape(groups, 2, STEPS, TILE).transpose(2, 0, 1, 3)
    return projections.reshape(STEPS, 1, actuators), response[None]


def solution(mesh):
    return jax.shard_map(
        local,
        mesh=mesh,
        in_specs=(
            P("probe", "state", None, None),
            P(),
            P(),
            P("probe"),
            P("state", None),
            P("state", "probe", None),
        ),
        out_specs=(P(None, "probe", None), P("probe", "state", None, None)),
        check_vma=False,
    )
```

```python
import jax
import jax.numpy as jnp
from jax import lax
from jax.experimental import pallas as pl
from jax.experimental.pallas import tpu as pltpu
from jax.sharding import PartitionSpec as P

TILE = 128
STEPS = 4
PAD = 8
GROUP = 256


def shift_pairs(count, by):
    return [(i, (i + by) % count) for i in range(count)]


def clear_pads(buffer):
    planes, columns, rows, lanes = buffer.shape
    edge = jnp.zeros((columns, PAD, lanes), buffer.dtype)

    def body(plane, carry):
        buffer[plane, :, :PAD, :] = edge
        buffer[plane, :, rows - PAD :, :] = edge
        return carry

    lax.fori_loop(0, planes, body, 0)


def sweep_rows(source, coef, planes, row, adjoint):
    here = pl.ds(pl.multiple_of(PAD + row, 8), 8)
    block = pl.ds(pl.multiple_of(row, 8), 8)
    columns = source.shape[1]
    lane = lax.broadcasted_iota(jnp.int32, (8, TILE), 1)
    weights = [coef[place, block, :] for place in range(5)]
    lower, centre = source[planes[0] - 1, :, here, :], source[planes[0], :, here, :]
    out = []
    for plane in planes:
        upper = source[plane + 1, :, here, :]
        above = source[plane, :, pl.ds(PAD + row + 1, 8), :]
        below = source[plane, :, pl.ds(PAD + row - 1, 8), :]
        left = [pltpu.roll(centre[c], TILE - 1, 1) for c in range(columns)]
        right = [pltpu.roll(centre[c], 1, 1) for c in range(columns)]
        results = []
        for c in range(columns):
            upper_z = jnp.where(lane == TILE - 1, left[(c + 1) % columns], left[c])
            lower_z = jnp.where(lane == 0, right[(c - 1) % columns], right[c])
            total = weights[0] * centre[c]
            if adjoint:
                total = total + weights[1] * upper[c]
                total = total + weights[2] * (lower[c] + (upper_z + lower_z))
                total = total + (weights[3] * above[c] + weights[4] * below[c])
            else:
                total = total + weights[1] * lower[c]
                total = total + weights[2] * ((upper[c] + (upper_z + lower_z)) + (above[c] + below[c]))
            results.append(total)
        out.append(results)
        lower, centre = centre, upper
    return out


def split(value):
    high = value.astype(jnp.bfloat16)
    low = (value - high.astype(jnp.float32)).astype(jnp.bfloat16)
    return high, low


def shifted_plane(field, plane, offset):
    height, width = field.shape[1:]
    columns = width // TILE
    turn, rest = offset // TILE, offset % TILE
    lane = lax.broadcasted_iota(jnp.int32, (height, TILE), 1)
    parts = [field[plane, :, pl.ds(c * TILE, TILE)].astype(jnp.float32) for c in range(columns)]
    rolled = [pltpu.roll(part, rest, 1) for part in parts]
    return [
        (lax.rem(c + turn, columns), jnp.where(lane >= rest, rolled[c], rolled[c - 1]))
        for c in range(columns)
    ]


def prelude_kernel(offset, field, courant, diffusivity, tile, panel, own, coef, start, kept):
    columns, height = own.shape[1:3]

    def load(plane, carry):
        for column, value in shifted_plane(field, plane, offset[0]):
            own[plane, column] = value
        return carry

    lax.fori_loop(0, field.shape[0], load, 0)
    kept[...] = panel[...]
    padding = jnp.zeros((6, height), jnp.float32)
    upright = jnp.concatenate([courant[...], diffusivity[...], padding], axis=0).T
    speed = jnp.broadcast_to(upright[:, 0:1], (height, TILE))
    rate = jnp.broadcast_to(upright[:, 1:2], (height, TILE))
    edge = jnp.zeros((1, TILE), jnp.float32)
    coef[0] = 1.0 - speed - 6.0 * rate
    coef[1] = speed + rate
    coef[2] = rate
    coef[3] = jnp.concatenate([rate[1:], edge], axis=0)
    coef[4] = jnp.concatenate([edge, rate[:-1]], axis=0)
    numbers = tile[...]
    inside = numbers & (columns * height - 1)
    numbers = (numbers - inside) + (inside & (columns - 1)) * height + inside // columns
    start[...] = numbers * STEPS


def adjoint_kernel(offset, coef, own, low, high, tiles, first, second):
    cells, columns, height = own.shape[:3]
    steps = STEPS
    edge = jnp.zeros((PAD, TILE), jnp.float32)
    tiles[:PAD, :] = edge
    tiles[tiles.shape[0] - PAD :, :] = edge
    inside = pl.ds(PAD, height)
    clear_pads(first)
    clear_pads(second)

    def load(plane, carry):
        for slab, field in ((0, low), (2, high)):
            for column, value in shifted_plane(field, plane, offset[0]):
                first[slab * cells + plane, column, inside, :] = value
        first[cells + plane, :, inside, :] = own[plane]
        return carry

    lax.fori_loop(0, cells, load, 0)
    buffers = (first, second)
    for step in range(steps):
        source, target = buffers[step % 2], buffers[(step + 1) % 2]

        def sweep(place, carry, source=source, target=target, step=step):
            planes = range(step + 1, 3 * cells - step - 1)
            row = place * 8
            for plane, block in zip(planes, sweep_rows(source, coef, planes, row, True)):
                for c in range(columns):
                    if step < steps - 1:
                        where = pl.ds(pl.multiple_of(PAD + row, 8), 8)
                        target[plane, c, where, :] = block[c]
                    if cells <= plane < 2 * cells:
                        number = ((plane - cells) * columns + c) * height + row
                        tiles[pl.ds(PAD + number * steps + step, 8, stride=steps), :] = block[c]
            return carry

        lax.fori_loop(0, height // 8, sweep, 0, unroll=8)


def forward_kernel(coef, own, low, high, out, first, second):
    cells, height, width = out.shape
    columns = width // TILE
    steps = STEPS
    clear_pads(first)
    clear_pads(second)
    for plane in range(cells):
        for c in range(columns):
            where = pl.ds(c * height, height)
            inside = pl.ds(PAD, height)
            first[cells + plane, c, inside, :] = own[plane, where, :]
            first[2 * cells + plane, c, inside, :] = high[plane, where, :].astype(jnp.float32)
            value = low[plane, where, :].astype(jnp.float32)
            if plane > 0:
                value = value + low[cells + plane - 1, where, :].astype(jnp.float32)
            first[plane, c, inside, :] = value
    buffers = (first, second)
    for step in range(steps):
        source, target = buffers[step % 2], buffers[(step + 1) % 2]

        def sweep(place, carry, source=source, target=target, step=step):
            planes = range(step + 1, 3 * cells - step - 1)
            row = place * 8
            for plane, block in zip(planes, sweep_rows(source, coef, planes, row, False)):
                for c in range(columns):
                    if step == steps - 1:
                        where = pl.ds(pl.multiple_of(row, 8), 8)
                        out[plane - cells, where, pl.ds(c * TILE, TILE)] = block[c]
                    else:
                        target[plane, c, pl.ds(pl.multiple_of(PAD + row, 8), 8), :] = block[c]
            return carry

        lax.fori_loop(0, height // 8, sweep, 0, unroll=8)


def project_kernel(places, shard, source, start, tiles, *refs):
    panels, (*before, out, wide) = refs[: len(places)], refs[len(places) :]
    for given in before:
        out[...] = given[...]
    first = lax.broadcasted_iota(jnp.int32, (8, TILE), 0) < STEPS
    lane = lax.broadcasted_iota(jnp.int32, (8, TILE), 1)
    for (chunk, offset), panel in zip(places, panels):
        wide[: panel.shape[0], :] = panel[...].astype(jnp.float32)

        def body(group, carry, chunk=chunk, offset=offset):
            number = source[chunk] * shard + offset + group
            sums = jnp.zeros((8, TILE), jnp.float32)
            for place in range(TILE):
                left = start[0, number * GROUP + place]
                right = start[0, number * GROUP + TILE + place]
                cells = jnp.where(
                    first, tiles[pl.ds(PAD + left, 8), :], tiles[pl.ds(PAD - STEPS + right, 8), :]
                )
                row = group * GROUP + place
                rows = jnp.where(first, wide[pl.ds(row, 1), :], wide[pl.ds(row + TILE, 1), :])
                total = jnp.sum(cells * rows, axis=1, keepdims=True)
                sums = jnp.where(lane == place, total, sums)
            out[number] = sums
            return carry

        lax.fori_loop(0, panel.shape[0] // GROUP, body, 0)


def deposit_kernel(count, places, shard, source, start, *refs):
    parts, panels = refs[:count], refs[count:-7]
    total, field, rightward, leftward, scaled, *chosen = refs[-7:]
    cells, per_plane = field.shape[0], field.shape[1]
    tile = start[...].astype(jnp.int16)
    one, none = jnp.ones((), jnp.bfloat16), jnp.zeros((), jnp.bfloat16)

    def choose(plane):
        target = chosen[plane % 2]
        rows = 64
        for top in range(0, per_plane, rows):
            first = (plane * per_plane + top) * STEPS
            by_row = lax.broadcasted_iota(jnp.int32, (rows, TILE), 0) * STEPS + first
            by_row = by_row.astype(jnp.int16)
            for left in range(0, tile.shape[1], TILE):
                found = jnp.where(tile[:, left : left + TILE] == by_row, one, none)
                target[pl.ds(top, rows), pl.ds(left, TILE)] = found

    choose(0)
    total[...] = tree_sum([part[...] for part in parts])
    blocks = []
    for (chunk, offset), panel in zip(places, panels):
        for group in range(panel.shape[0] // GROUP):
            number = source[chunk] * shard + offset + group
            blocks += [(number, half, panel, group * GROUP + half * TILE) for half in range(2)]
    last = [total[number, pl.ds(half * STEPS + STEPS - 1, 1), :] for number, half, _, _ in blocks]
    drive = jnp.concatenate(last, axis=0).T
    for place, (number, half, panel, row) in enumerate(blocks):
        rows = panel[pl.ds(row, TILE), :].astype(jnp.float32)
        head, tail = split(drive[:, place : place + 1] * rows)
        where = pl.ds(pl.multiple_of(number * GROUP + half * TILE, TILE), TILE)
        scaled[where, pl.ds(0, TILE)] = head
        scaled[where, pl.ds(TILE, TILE)] = tail

    for plane in range(cells):
        if plane < cells - 1:
            choose(plane + 1)
        sums = jnp.dot(chosen[plane % 2][...], scaled[...], preferred_element_type=jnp.float32)
        value = sums[:, :TILE] + sums[:, TILE:]
        field[plane] = value
        head, tail = split(value)
        leftward[plane] = head
        rightward[plane] = head
        if plane > 0:
            rightward[cells + plane - 1] = tail


def call(kernel, out_shape, vmem, scratch=(), smem=0, inputs=0):
    in_specs = [pl.BlockSpec(memory_space=pltpu.SMEM)] * smem
    in_specs += [pl.BlockSpec(memory_space=pltpu.VMEM)] * (inputs - smem)
    out_specs = jax.tree.map(lambda _: pl.BlockSpec(memory_space=pltpu.VMEM), out_shape)
    return pl.pallas_call(
        kernel,
        out_shape=out_shape,
        in_specs=in_specs,
        out_specs=out_specs,
        scratch_shapes=list(scratch),
        compiler_params=pltpu.CompilerParams(vmem_limit_bytes=vmem * 1024 * 1024),
        cost_estimate=pl.CostEstimate(flops=1024, bytes_accessed=1024, transcendentals=0),
    )


def gathered_panel(panel, axis, late, first):
    count = lax.axis_size(axis)
    shards, mask = {0: [panel]}, count // 2
    while mask:
        pairs = [(i, i ^ mask) for i in range(count)]
        for held in sorted(shards):
            pieces = shards[held]
            if held:
                pieces = [tied(piece, late) for piece in pieces]
            if len(shards) == 1:
                shards[mask] = [first]
                continue
            shards[held | mask] = [lax.ppermute(piece, axis, pairs) for piece in pieces]
        mask //= 2
    return [shards[k] for k in range(1, count)]


def layout(panels):
    places = []
    for chunk, pieces in panels:
        first = 0
        for piece in pieces:
            places.append((chunk, first))
            first += piece.shape[0] // GROUP
    return places


def tied(value, *others):
    return lax.optimization_barrier((value,) + others)[0]


def tree_sum(parts):
    while len(parts) > 1:
        parts = [parts[i] + parts[i + 1] for i in range(0, len(parts), 2)]
    return parts[0]


def summands(part, axis):
    count = lax.axis_size(axis)
    if count & (count - 1):
        return [lax.psum(part, axis)]
    done, parts = 1, [part]
    for span in (2, 4, 4, 4, 4):
        span = min(span, count // done)
        if span > 1:
            part = tree_sum(parts)
            pairs = [[(i, i ^ (k * done)) for i in range(count)] for k in range(1, span)]
            parts = [part] + [lax.ppermute(part, axis, pair) for pair in pairs]
            done *= span
    return parts


def local(sensor_field, courant, diffusivity, probe_offset, tile_index, actuator_panel):
    slabs, probes = lax.axis_size("state"), lax.axis_size("probe")
    own = sensor_field[0]
    cells, height, width = own.shape
    columns = width // TILE
    tile_total = cells * height * columns
    actuators = tile_index.shape[1]
    groups = actuators // GROUP
    shard = groups // probes
    planes = 3 * cells
    f32, bf16 = jnp.float32, jnp.bfloat16

    source = lax.axis_index("probe") ^ jnp.arange(probes, dtype=jnp.int32)
    high = lax.ppermute(own, "state", shift_pairs(slabs, -1))
    low = lax.ppermute(own.astype(bf16), "state", shift_pairs(slabs, 1))

    shifted, coef, start, panel = call(
        prelude_kernel,
        (
            jax.ShapeDtypeStruct((cells, columns, height, TILE), f32),
            jax.ShapeDtypeStruct((5, height, TILE), f32),
            jax.ShapeDtypeStruct(tile_index.shape, jnp.int32),
            jax.ShapeDtypeStruct(actuator_panel.shape[1:], bf16),
        ),
        vmem=8,
        smem=1,
        inputs=6,
    )(probe_offset, own, courant[None], diffusivity[None], tile_index, actuator_panel[0])

    half = probes // 2
    far = lax.ppermute(actuator_panel[0], "probe", [(i, i ^ half) for i in range(probes)])
    coef = tied(coef, far)
    field_shape = pltpu.VMEM((planes, columns, height + 2 * PAD, TILE), f32)
    tiles = call(
        adjoint_kernel,
        jax.ShapeDtypeStruct((tile_total * STEPS + 2 * PAD, TILE), f32),
        vmem=10,
        scratch=(field_shape, field_shape),
        smem=1,
        inputs=5,
    )(probe_offset, coef, shifted, low, high)

    panels = list(enumerate([[panel]] + gathered_panel(actuator_panel[0], "probe", coef, far)))

    def project(shards, *given):
        pieces = [piece for _, pieces in shards for piece in pieces]
        return call(
            lambda *refs: project_kernel(layout(shards), shard, *refs),
            jax.ShapeDtypeStruct((groups, 2 * STEPS, TILE), f32),
            vmem=6,
            scratch=(pltpu.VMEM((shard * GROUP, TILE), f32),),
            smem=2,
            inputs=3 + len(pieces) + len(given),
        )(source, start, tiles, *pieces, *given)

    before = project(panels[:-1])
    parts = summands(project(panels[-1:], before), "state")
    pieces = [piece for _, pieces in panels for piece in pieces]
    payload = jax.ShapeDtypeStruct((2 * cells - 1, height * columns, TILE), bf16)
    heads = jax.ShapeDtypeStruct((cells, height * columns, TILE), bf16)
    total, forced, rightward, leftward = call(
        lambda *refs: deposit_kernel(len(parts), layout(panels), shard, *refs),
        (
            jax.ShapeDtypeStruct(before.shape, f32),
            jax.ShapeDtypeStruct((cells, height * columns, TILE), f32),
            payload,
            heads,
        ),
        vmem=16,
        scratch=(
            pltpu.VMEM((actuators, 2 * TILE), bf16),
            pltpu.VMEM((height * columns, actuators), bf16),
            pltpu.VMEM((height * columns, actuators), bf16),
        ),
        smem=1,
        inputs=2 + len(parts) + len(pieces),
    )(source, start, *parts, *pieces)
    from_low = lax.ppermute(rightward, "state", shift_pairs(slabs, 1))
    from_high = lax.ppermute(leftward, "state", shift_pairs(slabs, -1))
    response = call(
        forward_kernel,
        jax.ShapeDtypeStruct((cells, height, width), f32),
        vmem=10,
        scratch=(field_shape, field_shape),
        inputs=4,
    )(coef, forced, from_low, from_high)
    projections = total.reshape(groups, 2, STEPS, TILE).transpose(2, 0, 1, 3)
    return projections.reshape(STEPS, 1, actuators), response[None]


def solution(mesh):
    return jax.shard_map(
        local,
        mesh=mesh,
        in_specs=(
            P("probe", "state", None, None),
            P(),
            P(),
            P("probe"),
            P("state", None),
            P("state", "probe", None),
        ),
        out_specs=(P(None, "probe", None), P("probe", "state", None, None)),
        check_vma=False,
    )
```

```python
import jax
import jax.numpy as jnp
from jax import lax
from jax.experimental import pallas as pl
from jax.experimental.pallas import tpu as pltpu
from jax.sharding import PartitionSpec as P

TILE = 128
STEPS = 4
PAD = 8
GROUP = 256


def shift_pairs(count, by):
    return [(i, (i + by) % count) for i in range(count)]


def clear_pads(buffer):
    planes, columns, rows, lanes = buffer.shape
    edge = jnp.zeros((columns, PAD, lanes), buffer.dtype)

    def body(plane, carry):
        buffer[plane, :, :PAD, :] = edge
        buffer[plane, :, rows - PAD :, :] = edge
        return carry

    lax.fori_loop(0, planes, body, 0)


def sweep_rows(source, coef, planes, row, adjoint):
    here = pl.ds(pl.multiple_of(PAD + row, 8), 8)
    block = pl.ds(pl.multiple_of(row, 8), 8)
    columns = source.shape[1]
    lane = lax.broadcasted_iota(jnp.int32, (8, TILE), 1)
    weights = [coef[place, block, :] for place in range(5)]
    lower, centre = source[planes[0] - 1, :, here, :], source[planes[0], :, here, :]
    out = []
    for plane in planes:
        upper = source[plane + 1, :, here, :]
        above = source[plane, :, pl.ds(PAD + row + 1, 8), :]
        below = source[plane, :, pl.ds(PAD + row - 1, 8), :]
        left = [pltpu.roll(centre[c], TILE - 1, 1) for c in range(columns)]
        right = [pltpu.roll(centre[c], 1, 1) for c in range(columns)]
        results = []
        for c in range(columns):
            upper_z = jnp.where(lane == TILE - 1, left[(c + 1) % columns], left[c])
            lower_z = jnp.where(lane == 0, right[(c - 1) % columns], right[c])
            total = weights[0] * centre[c]
            if adjoint:
                total = total + weights[1] * upper[c]
                total = total + weights[2] * (lower[c] + (upper_z + lower_z))
                total = total + (weights[3] * above[c] + weights[4] * below[c])
            else:
                total = total + weights[1] * lower[c]
                total = total + weights[2] * ((upper[c] + (upper_z + lower_z)) + (above[c] + below[c]))
            results.append(total)
        out.append(results)
        lower, centre = centre, upper
    return out


def split(value):
    high = value.astype(jnp.bfloat16)
    low = (value - high.astype(jnp.float32)).astype(jnp.bfloat16)
    return high, low


def shifted_plane(field, plane, offset):
    height, width = field.shape[1:]
    columns = width // TILE
    turn, rest = offset // TILE, offset % TILE
    lane = lax.broadcasted_iota(jnp.int32, (height, TILE), 1)
    parts = [field[plane, :, pl.ds(c * TILE, TILE)].astype(jnp.float32) for c in range(columns)]
    rolled = [pltpu.roll(part, rest, 1) for part in parts]
    return [
        (lax.rem(c + turn, columns), jnp.where(lane >= rest, rolled[c], rolled[c - 1]))
        for c in range(columns)
    ]


def prelude_kernel(offset, field, courant, diffusivity, tile, panel, own, coef, start, kept):
    columns, height = own.shape[1:3]

    def load(plane, carry):
        for column, value in shifted_plane(field, plane, offset[0]):
            own[plane, column] = value
        return carry

    lax.fori_loop(0, field.shape[0], load, 0)
    kept[...] = panel[...]
    padding = jnp.zeros((6, height), jnp.float32)
    upright = jnp.concatenate([courant[...], diffusivity[...], padding], axis=0).T
    speed = jnp.broadcast_to(upright[:, 0:1], (height, TILE))
    rate = jnp.broadcast_to(upright[:, 1:2], (height, TILE))
    edge = jnp.zeros((1, TILE), jnp.float32)
    coef[0] = 1.0 - speed - 6.0 * rate
    coef[1] = speed + rate
    coef[2] = rate
    coef[3] = jnp.concatenate([rate[1:], edge], axis=0)
    coef[4] = jnp.concatenate([edge, rate[:-1]], axis=0)
    numbers = tile[...]
    inside = numbers & (columns * height - 1)
    numbers = (numbers - inside) + (inside & (columns - 1)) * height + inside // columns
    start[...] = numbers * STEPS


def adjoint_kernel(offset, coef, own, low, high, tiles, first, second):
    cells, columns, height = own.shape[:3]
    steps = STEPS
    edge = jnp.zeros((PAD, TILE), jnp.float32)
    tiles[:PAD, :] = edge
    tiles[tiles.shape[0] - PAD :, :] = edge
    inside = pl.ds(PAD, height)
    clear_pads(first)
    clear_pads(second)

    def load(plane, carry):
        for slab, field in ((0, low), (2, high)):
            for column, value in shifted_plane(field, plane, offset[0]):
                first[slab * cells + plane, column, inside, :] = value
        first[cells + plane, :, inside, :] = own[plane]
        return carry

    lax.fori_loop(0, cells, load, 0)
    buffers = (first, second)
    for step in range(steps):
        source, target = buffers[step % 2], buffers[(step + 1) % 2]

        def sweep(place, carry, source=source, target=target, step=step):
            planes = range(step + 1, 3 * cells - step - 1)
            row = place * 8
            for plane, block in zip(planes, sweep_rows(source, coef, planes, row, True)):
                for c in range(columns):
                    if step < steps - 1:
                        where = pl.ds(pl.multiple_of(PAD + row, 8), 8)
                        target[plane, c, where, :] = block[c]
                    if cells <= plane < 2 * cells:
                        number = ((plane - cells) * columns + c) * height + row
                        tiles[pl.ds(PAD + number * steps + step, 8, stride=steps), :] = block[c]
            return carry

        lax.fori_loop(0, height // 8, sweep, 0, unroll=8)


def forward_kernel(coef, own, low, high, out, first, second):
    cells, height, width = out.shape
    columns = width // TILE
    steps = STEPS
    clear_pads(first)
    clear_pads(second)
    for plane in range(cells):
        for c in range(columns):
            where = pl.ds(c * height, height)
            inside = pl.ds(PAD, height)
            first[cells + plane, c, inside, :] = own[plane, where, :]
            first[2 * cells + plane, c, inside, :] = high[plane, where, :].astype(jnp.float32)
            value = low[plane, where, :].astype(jnp.float32)
            if plane > 0:
                value = value + low[cells + plane - 1, where, :].astype(jnp.float32)
            first[plane, c, inside, :] = value
    buffers = (first, second)
    for step in range(steps):
        source, target = buffers[step % 2], buffers[(step + 1) % 2]

        def sweep(place, carry, source=source, target=target, step=step):
            planes = range(step + 1, 3 * cells - step - 1)
            row = place * 8
            for plane, block in zip(planes, sweep_rows(source, coef, planes, row, False)):
                for c in range(columns):
                    if step == steps - 1:
                        where = pl.ds(pl.multiple_of(row, 8), 8)
                        out[plane - cells, where, pl.ds(c * TILE, TILE)] = block[c]
                    else:
                        target[plane, c, pl.ds(pl.multiple_of(PAD + row, 8), 8), :] = block[c]
            return carry

        lax.fori_loop(0, height // 8, sweep, 0, unroll=8)


def project_kernel(places, shard, source, start, tiles, *refs):
    panels, (*before, out, wide) = refs[: len(places)], refs[len(places) :]
    for given in before:
        out[...] = given[...]
    first = lax.broadcasted_iota(jnp.int32, (8, TILE), 0) < STEPS
    lane = lax.broadcasted_iota(jnp.int32, (8, TILE), 1)
    for (chunk, offset), panel in zip(places, panels):
        wide[: panel.shape[0], :] = panel[...].astype(jnp.float32)

        def body(group, carry, chunk=chunk, offset=offset):
            number = source[chunk] * shard + offset + group
            sums = jnp.zeros((8, TILE), jnp.float32)
            for place in range(TILE):
                left = start[0, number * GROUP + place]
                right = start[0, number * GROUP + TILE + place]
                cells = jnp.where(
                    first, tiles[pl.ds(PAD + left, 8), :], tiles[pl.ds(PAD - STEPS + right, 8), :]
                )
                row = group * GROUP + place
                rows = jnp.where(first, wide[pl.ds(row, 1), :], wide[pl.ds(row + TILE, 1), :])
                total = jnp.sum(cells * rows, axis=1, keepdims=True)
                sums = jnp.where(lane == place, total, sums)
            out[number] = sums
            return carry

        groups = panel.shape[0] // GROUP
        lax.fori_loop(0, groups, body, 0, unroll=2 if groups % 2 == 0 else 1)


def deposit_kernel(count, places, shard, source, start, *refs):
    parts, panels = refs[:count], refs[count:-7]
    total, field, rightward, leftward, scaled, *chosen = refs[-7:]
    cells, per_plane = field.shape[0], field.shape[1]
    tile = start[...].astype(jnp.int16)
    one, none = jnp.ones((), jnp.bfloat16), jnp.zeros((), jnp.bfloat16)

    def choose(plane):
        target = chosen[plane % 2]
        rows = 64
        for top in range(0, per_plane, rows):
            first = (plane * per_plane + top) * STEPS
            by_row = lax.broadcasted_iota(jnp.int32, (rows, TILE), 0) * STEPS + first
            by_row = by_row.astype(jnp.int16)
            for left in range(0, tile.shape[1], TILE):
                found = jnp.where(tile[:, left : left + TILE] == by_row, one, none)
                target[pl.ds(top, rows), pl.ds(left, TILE)] = found

    choose(0)
    total[...] = tree_sum([part[...] for part in parts[::-1]])
    blocks = []
    for (chunk, offset), panel in zip(places, panels):
        for group in range(panel.shape[0] // GROUP):
            number = source[chunk] * shard + offset + group
            blocks += [(number, half, panel, group * GROUP + half * TILE) for half in range(2)]
    last = [total[number, pl.ds(half * STEPS + STEPS - 1, 1), :] for number, half, _, _ in blocks]
    drive = jnp.concatenate(last, axis=0).T
    for place, (number, half, panel, row) in enumerate(blocks):
        rows = panel[pl.ds(row, TILE), :].astype(jnp.float32)
        head, tail = split(drive[:, place : place + 1] * rows)
        where = pl.ds(pl.multiple_of(number * GROUP + half * TILE, TILE), TILE)
        scaled[where, pl.ds(0, TILE)] = head
        scaled[where, pl.ds(TILE, TILE)] = tail

    for plane in range(cells):
        if plane < cells - 1:
            choose(plane + 1)
        sums = jnp.dot(chosen[plane % 2][...], scaled[...], preferred_element_type=jnp.float32)
        value = sums[:, :TILE] + sums[:, TILE:]
        field[plane] = value
        head, tail = split(value)
        leftward[plane] = head
        rightward[plane] = head
        if plane > 0:
            rightward[cells + plane - 1] = tail


def call(kernel, out_shape, vmem, scratch=(), smem=0, inputs=0):
    in_specs = [pl.BlockSpec(memory_space=pltpu.SMEM)] * smem
    in_specs += [pl.BlockSpec(memory_space=pltpu.VMEM)] * (inputs - smem)
    out_specs = jax.tree.map(lambda _: pl.BlockSpec(memory_space=pltpu.VMEM), out_shape)
    return pl.pallas_call(
        kernel,
        out_shape=out_shape,
        in_specs=in_specs,
        out_specs=out_specs,
        scratch_shapes=list(scratch),
        compiler_params=pltpu.CompilerParams(vmem_limit_bytes=vmem * 1024 * 1024),
        cost_estimate=pl.CostEstimate(flops=1024, bytes_accessed=1024, transcendentals=0),
    )


def gathered_panel(panel, axis, late, first):
    count = lax.axis_size(axis)
    shards, mask = {0: [panel]}, count // 2
    while mask:
        pairs = [(i, i ^ mask) for i in range(count)]
        for held in sorted(shards):
            pieces = shards[held]
            if held:
                pieces = [tied(piece, late) for piece in pieces]
            if len(shards) == 1:
                shards[mask] = [first]
                continue
            shards[held | mask] = [lax.ppermute(piece, axis, pairs) for piece in pieces]
        mask //= 2
    return [shards[k] for k in range(1, count)]


def layout(panels):
    places = []
    for chunk, pieces in panels:
        first = 0
        for piece in pieces:
            places.append((chunk, first))
            first += piece.shape[0] // GROUP
    return places


def tied(value, *others):
    return lax.optimization_barrier((value,) + others)[0]


def tree_sum(parts):
    while len(parts) > 1:
        parts = [parts[i] + parts[i + 1] for i in range(0, len(parts), 2)]
    return parts[0]


def summands(part, axis):
    count = lax.axis_size(axis)
    if count & (count - 1):
        return [lax.psum(part, axis)]
    done, parts = 1, [part]
    for span in (2, 4, 4, 4, 4):
        span = min(span, count // done)
        if span > 1:
            part = tree_sum(parts)
            came = {0: part}
            for k in range(span - 1, 0, -1):
                came[k] = lax.ppermute(part, axis, [(i, i ^ (k * done)) for i in range(count)])
            parts = [came[k] for k in range(span)]
            done *= span
    return parts


def local(sensor_field, courant, diffusivity, probe_offset, tile_index, actuator_panel):
    slabs, probes = lax.axis_size("state"), lax.axis_size("probe")
    own = sensor_field[0]
    cells, height, width = own.shape
    columns = width // TILE
    tile_total = cells * height * columns
    actuators = tile_index.shape[1]
    groups = actuators // GROUP
    shard = groups // probes
    planes = 3 * cells
    f32, bf16 = jnp.float32, jnp.bfloat16

    source = lax.axis_index("probe") ^ jnp.arange(probes, dtype=jnp.int32)
    high = lax.ppermute(own, "state", shift_pairs(slabs, -1))
    low = lax.ppermute(own.astype(bf16), "state", shift_pairs(slabs, 1))

    shifted, coef, start, panel = call(
        prelude_kernel,
        (
            jax.ShapeDtypeStruct((cells, columns, height, TILE), f32),
            jax.ShapeDtypeStruct((5, height, TILE), f32),
            jax.ShapeDtypeStruct(tile_index.shape, jnp.int32),
            jax.ShapeDtypeStruct(actuator_panel.shape[1:], bf16),
        ),
        vmem=8,
        smem=1,
        inputs=6,
    )(probe_offset, own, courant[None], diffusivity[None], tile_index, actuator_panel[0])

    half = probes // 2
    far = lax.ppermute(actuator_panel[0], "probe", [(i, i ^ half) for i in range(probes)])
    coef = tied(coef, far)
    field_shape = pltpu.VMEM((planes, columns, height + 2 * PAD, TILE), f32)
    tiles = call(
        adjoint_kernel,
        jax.ShapeDtypeStruct((tile_total * STEPS + 2 * PAD, TILE), f32),
        vmem=10,
        scratch=(field_shape, field_shape),
        smem=1,
        inputs=5,
    )(probe_offset, coef, shifted, low, high)

    panels = list(enumerate([[panel]] + gathered_panel(actuator_panel[0], "probe", coef, far)))

    def project(shards, *given):
        pieces = [piece for _, pieces in shards for piece in pieces]
        return call(
            lambda *refs: project_kernel(layout(shards), shard, *refs),
            jax.ShapeDtypeStruct((groups, 2 * STEPS, TILE), f32),
            vmem=6,
            scratch=(pltpu.VMEM((shard * GROUP, TILE), f32),),
            smem=2,
            inputs=3 + len(pieces) + len(given),
        )(source, start, tiles, *pieces, *given)

    before = project(panels[:-1])
    parts = summands(project(panels[-1:], before), "state")
    pieces = [piece for _, pieces in panels for piece in pieces]
    payload = jax.ShapeDtypeStruct((2 * cells - 1, height * columns, TILE), bf16)
    heads = jax.ShapeDtypeStruct((cells, height * columns, TILE), bf16)
    total, forced, rightward, leftward = call(
        lambda *refs: deposit_kernel(len(parts), layout(panels), shard, *refs),
        (
            jax.ShapeDtypeStruct(before.shape, f32),
            jax.ShapeDtypeStruct((cells, height * columns, TILE), f32),
            payload,
            heads,
        ),
        vmem=16,
        scratch=(
            pltpu.VMEM((actuators, 2 * TILE), bf16),
            pltpu.VMEM((height * columns, actuators), bf16),
            pltpu.VMEM((height * columns, actuators), bf16),
        ),
        smem=1,
        inputs=2 + len(parts) + len(pieces),
    )(source, start, *parts[::-1], *pieces)
    from_low = lax.ppermute(rightward, "state", shift_pairs(slabs, 1))
    from_high = lax.ppermute(leftward, "state", shift_pairs(slabs, -1))
    response = call(
        forward_kernel,
        jax.ShapeDtypeStruct((cells, height, width), f32),
        vmem=10,
        scratch=(field_shape, field_shape),
        inputs=4,
    )(coef, forced, from_low, from_high)
    projections = total.reshape(groups, 2, STEPS, TILE).transpose(2, 0, 1, 3)
    return projections.reshape(STEPS, 1, actuators), response[None]


def solution(mesh):
    return jax.shard_map(
        local,
        mesh=mesh,
        in_specs=(
            P("probe", "state", None, None),
            P(),
            P(),
            P("probe"),
            P("state", None),
            P("state", "probe", None),
        ),
        out_specs=(P(None, "probe", None), P("probe", "state", None, None)),
        check_vma=False,
    )
```

```python
import jax
import jax.numpy as jnp
from jax import lax
from jax.experimental import pallas as pl
from jax.experimental.pallas import tpu as pltpu
from jax.sharding import PartitionSpec as P

TILE = 128
STEPS = 4
PAD = 8
GROUP = 256


def shift_pairs(count, by):
    return [(i, (i + by) % count) for i in range(count)]


def clear_pads(buffer):
    planes, columns, rows, lanes = buffer.shape
    edge = jnp.zeros((columns, PAD, lanes), buffer.dtype)

    def body(plane, carry):
        buffer[plane, :, :PAD, :] = edge
        buffer[plane, :, rows - PAD :, :] = edge
        return carry

    lax.fori_loop(0, planes, body, 0)


def sweep_rows(source, coef, planes, row, adjoint):
    here = pl.ds(pl.multiple_of(PAD + row, 8), 8)
    block = pl.ds(pl.multiple_of(row, 8), 8)
    columns = source.shape[1]
    lane = lax.broadcasted_iota(jnp.int32, (8, TILE), 1)
    weights = [coef[place, block, :] for place in range(5)]
    lower, centre = source[planes[0] - 1, :, here, :], source[planes[0], :, here, :]
    out = []
    for plane in planes:
        upper = source[plane + 1, :, here, :]
        above = source[plane, :, pl.ds(PAD + row + 1, 8), :]
        below = source[plane, :, pl.ds(PAD + row - 1, 8), :]
        left = [pltpu.roll(centre[c], TILE - 1, 1) for c in range(columns)]
        right = [pltpu.roll(centre[c], 1, 1) for c in range(columns)]
        results = []
        for c in range(columns):
            upper_z = jnp.where(lane == TILE - 1, left[(c + 1) % columns], left[c])
            lower_z = jnp.where(lane == 0, right[(c - 1) % columns], right[c])
            total = weights[0] * centre[c]
            if adjoint:
                total = total + weights[1] * upper[c]
                total = total + weights[2] * (lower[c] + (upper_z + lower_z))
                total = total + (weights[3] * above[c] + weights[4] * below[c])
            else:
                total = total + weights[1] * lower[c]
                total = total + weights[2] * ((upper[c] + (upper_z + lower_z)) + (above[c] + below[c]))
            results.append(total)
        out.append(results)
        lower, centre = centre, upper
    return out


def split(value):
    high = value.astype(jnp.bfloat16)
    low = (value - high.astype(jnp.float32)).astype(jnp.bfloat16)
    return high, low


def shifted_plane(field, plane, offset):
    height, width = field.shape[1:]
    columns = width // TILE
    turn, rest = offset // TILE, offset % TILE
    lane = lax.broadcasted_iota(jnp.int32, (height, TILE), 1)
    parts = [field[plane, :, pl.ds(c * TILE, TILE)].astype(jnp.float32) for c in range(columns)]
    rolled = [pltpu.roll(part, rest, 1) for part in parts]
    return [
        (lax.rem(c + turn, columns), jnp.where(lane >= rest, rolled[c], rolled[c - 1]))
        for c in range(columns)
    ]


def prelude_kernel(offset, field, courant, diffusivity, tile, panel, own, coef, start, kept):
    columns, height = own.shape[1:3]

    def load(plane, carry):
        for column, value in shifted_plane(field, plane, offset[0]):
            own[plane, column] = value
        return carry

    lax.fori_loop(0, field.shape[0], load, 0)
    kept[...] = panel[...]
    padding = jnp.zeros((6, height), jnp.float32)
    upright = jnp.concatenate([courant[...], diffusivity[...], padding], axis=0).T
    speed = jnp.broadcast_to(upright[:, 0:1], (height, TILE))
    rate = jnp.broadcast_to(upright[:, 1:2], (height, TILE))
    edge = jnp.zeros((1, TILE), jnp.float32)
    coef[0] = 1.0 - speed - 6.0 * rate
    coef[1] = speed + rate
    coef[2] = rate
    coef[3] = jnp.concatenate([rate[1:], edge], axis=0)
    coef[4] = jnp.concatenate([edge, rate[:-1]], axis=0)
    numbers = tile[...]
    inside = numbers & (columns * height - 1)
    numbers = (numbers - inside) + (inside & (columns - 1)) * height + inside // columns
    start[...] = numbers * STEPS


def adjoint_kernel(offset, coef, own, low, high, tiles, first, second):
    cells, columns, height = own.shape[:3]
    steps = STEPS
    edge = jnp.zeros((PAD, TILE), jnp.float32)
    tiles[:PAD, :] = edge
    tiles[tiles.shape[0] - PAD :, :] = edge
    inside = pl.ds(PAD, height)
    clear_pads(first)
    clear_pads(second)

    def load(plane, carry):
        for slab, field in ((0, low), (2, high)):
            for column, value in shifted_plane(field, plane, offset[0]):
                first[slab * cells + plane, column, inside, :] = value
        first[cells + plane, :, inside, :] = own[plane]
        return carry

    lax.fori_loop(0, cells, load, 0)
    buffers = (first, second)
    for step in range(steps):
        source, target = buffers[step % 2], buffers[(step + 1) % 2]

        def sweep(place, carry, source=source, target=target, step=step):
            planes = range(step + 1, 3 * cells - step - 1)
            row = place * 8
            for plane, block in zip(planes, sweep_rows(source, coef, planes, row, True)):
                for c in range(columns):
                    if step < steps - 1:
                        where = pl.ds(pl.multiple_of(PAD + row, 8), 8)
                        target[plane, c, where, :] = block[c]
                    if cells <= plane < 2 * cells:
                        number = ((plane - cells) * columns + c) * height + row
                        tiles[pl.ds(PAD + number * steps + step, 8, stride=steps), :] = block[c]
            return carry

        lax.fori_loop(0, height // 8, sweep, 0, unroll=8)


def forward_kernel(coef, own, low, high, out, first, second):
    cells, height, width = out.shape
    columns = width // TILE
    steps = STEPS
    clear_pads(first)
    clear_pads(second)
    for plane in range(cells):
        for c in range(columns):
            where = pl.ds(c * height, height)
            inside = pl.ds(PAD, height)
            first[cells + plane, c, inside, :] = own[plane, where, :]
            first[2 * cells + plane, c, inside, :] = high[plane, where, :].astype(jnp.float32)
            value = low[plane, where, :].astype(jnp.float32)
            if plane > 0:
                value = value + low[cells + plane - 1, where, :].astype(jnp.float32)
            first[plane, c, inside, :] = value
    buffers = (first, second)
    for step in range(steps):
        source, target = buffers[step % 2], buffers[(step + 1) % 2]

        def sweep(place, carry, source=source, target=target, step=step):
            planes = range(step + 1, 3 * cells - step - 1)
            row = place * 8
            for plane, block in zip(planes, sweep_rows(source, coef, planes, row, False)):
                for c in range(columns):
                    if step == steps - 1:
                        where = pl.ds(pl.multiple_of(row, 8), 8)
                        out[plane - cells, where, pl.ds(c * TILE, TILE)] = block[c]
                    else:
                        target[plane, c, pl.ds(pl.multiple_of(PAD + row, 8), 8), :] = block[c]
            return carry

        lax.fori_loop(0, height // 8, sweep, 0, unroll=8)


def project_kernel(places, shard, source, start, tiles, *refs):
    panels, (*before, out, wide) = refs[: len(places)], refs[len(places) :]
    for given in before:
        out[...] = given[...]
    first = lax.broadcasted_iota(jnp.int32, (8, TILE), 0) < STEPS
    lane = lax.broadcasted_iota(jnp.int32, (8, TILE), 1)
    for (chunk, offset), panel in zip(places, panels):
        wide[: panel.shape[0], :] = panel[...].astype(jnp.float32)

        def body(group, carry, chunk=chunk, offset=offset):
            number = source[chunk] * shard + offset + group
            sums = jnp.zeros((8, TILE), jnp.float32)
            for place in range(TILE):
                left = start[0, number * GROUP + place]
                right = start[0, number * GROUP + TILE + place]
                cells = jnp.where(
                    first, tiles[pl.ds(PAD + left, 8), :], tiles[pl.ds(PAD - STEPS + right, 8), :]
                )
                row = group * GROUP + place
                rows = jnp.where(first, wide[pl.ds(row, 1), :], wide[pl.ds(row + TILE, 1), :])
                total = jnp.sum(cells * rows, axis=1, keepdims=True)
                sums = jnp.where(lane == place, total, sums)
            out[number] = sums
            return carry

        groups = panel.shape[0] // GROUP
        lax.fori_loop(0, groups, body, 0, unroll=2 if groups % 2 == 0 else 1)


def deposit_kernel(order, places, shard, source, start, *refs):
    parts, panels = refs[: len(order)], refs[len(order) : -7]
    total, field, rightward, leftward, scaled, *chosen = refs[-7:]
    cells, per_plane = field.shape[0], field.shape[1]
    blocks = []
    for (chunk, offset), panel in zip(places, panels):
        for group in range(panel.shape[0] // GROUP):
            number = source[chunk] * shard + offset + group
            blocks += [(number, half, panel, group * GROUP + half * TILE) for half in range(2)]
    one, none = jnp.ones((), jnp.bfloat16), jnp.zeros((), jnp.bfloat16)
    tiles = []
    for number, half, _, _ in blocks:
        where = pl.ds(pl.multiple_of(number * GROUP + half * TILE, TILE), TILE)
        tiles.append(start[:, where].astype(jnp.int16))

    def choose(plane):
        target = chosen[plane % 2]
        rows = 64
        for top in range(0, per_plane, rows):
            first = (plane * per_plane + top) * STEPS
            by_row = lax.broadcasted_iota(jnp.int32, (rows, TILE), 0) * STEPS + first
            by_row = by_row.astype(jnp.int16)
            for place, tile in enumerate(tiles):
                found = jnp.where(tile == by_row, one, none)
                target[pl.ds(top, rows), pl.ds(place * TILE, TILE)] = found

    def finish(plane, sums):
        value = sums[:, :TILE] + sums[:, TILE:]
        field[plane] = value
        head, tail = split(value)
        leftward[plane] = head
        rightward[plane] = head
        if plane > 0:
            rightward[cells + plane - 1] = tail

    choose(0)
    summed = dict(zip(order, [part[...] for part in parts]))
    total[...] = tree_sum([summed[k] for k in range(len(parts))])
    last = [total[number, pl.ds(half * STEPS + STEPS - 1, 1), :] for number, half, _, _ in blocks]
    drive = jnp.concatenate(last, axis=0).T
    sums = jnp.zeros((per_plane, 2 * TILE), jnp.float32)
    for place, (_, half, panel, row) in enumerate(blocks):
        rows = panel[pl.ds(row, TILE), :].astype(jnp.float32)
        head, tail = split(drive[:, place : place + 1] * rows)
        scaled[pl.ds(place * TILE, TILE), pl.ds(0, TILE)] = head
        scaled[pl.ds(place * TILE, TILE), pl.ds(TILE, TILE)] = tail
        if half:
            where = pl.ds((place - 1) * TILE, GROUP)
            sums = sums + jnp.dot(
                chosen[0][:, where], scaled[where, :], preferred_element_type=jnp.float32
            )
    choose(1)
    finish(0, sums)
    for plane in range(1, cells):
        if plane < cells - 1:
            choose(plane + 1)
        finish(
            plane, jnp.dot(chosen[plane % 2][...], scaled[...], preferred_element_type=jnp.float32)
        )


def call(kernel, out_shape, vmem, scratch=(), smem=0, inputs=0):
    in_specs = [pl.BlockSpec(memory_space=pltpu.SMEM)] * smem
    in_specs += [pl.BlockSpec(memory_space=pltpu.VMEM)] * (inputs - smem)
    out_specs = jax.tree.map(lambda _: pl.BlockSpec(memory_space=pltpu.VMEM), out_shape)
    return pl.pallas_call(
        kernel,
        out_shape=out_shape,
        in_specs=in_specs,
        out_specs=out_specs,
        scratch_shapes=list(scratch),
        compiler_params=pltpu.CompilerParams(vmem_limit_bytes=vmem * 1024 * 1024),
        cost_estimate=pl.CostEstimate(flops=1024, bytes_accessed=1024, transcendentals=0),
    )


def gathered_panel(panel, axis, late, first):
    count = lax.axis_size(axis)
    shards, mask = {0: [panel]}, count // 2
    while mask:
        pairs = [(i, i ^ mask) for i in range(count)]
        for held in sorted(shards):
            pieces = shards[held]
            if held:
                pieces = [tied(piece, late) for piece in pieces]
            if len(shards) == 1:
                shards[mask] = [first]
                continue
            shards[held | mask] = [lax.ppermute(piece, axis, pairs) for piece in pieces]
        mask //= 2
    return [shards[k] for k in range(1, count)]


def layout(panels):
    places = []
    for chunk, pieces in panels:
        first = 0
        for piece in pieces:
            places.append((chunk, first))
            first += piece.shape[0] // GROUP
    return places


def tied(value, *others):
    return lax.optimization_barrier((value,) + others)[0]


def tree_sum(parts):
    while len(parts) > 1:
        parts = [parts[i] + parts[i + 1] for i in range(0, len(parts), 2)]
    return parts[0]


def summands(part, axis):
    count = lax.axis_size(axis)
    if count & (count - 1):
        return [lax.psum(part, axis)]
    done, parts = 1, [part]
    for span in (2, 4, 4, 4, 4):
        span = min(span, count // done)
        if span > 1:
            part = tree_sum(parts)
            came = {0: part}
            for k in range(span - 1, 0, -1):
                came[k] = lax.ppermute(part, axis, [(i, i ^ (k * done)) for i in range(count)])
            parts = [came[k] for k in range(span)]
            done *= span
    return parts


def local(sensor_field, courant, diffusivity, probe_offset, tile_index, actuator_panel):
    slabs, probes = lax.axis_size("state"), lax.axis_size("probe")
    own = sensor_field[0]
    cells, height, width = own.shape
    columns = width // TILE
    tile_total = cells * height * columns
    actuators = tile_index.shape[1]
    groups = actuators // GROUP
    shard = groups // probes
    planes = 3 * cells
    f32, bf16 = jnp.float32, jnp.bfloat16

    source = lax.axis_index("probe") ^ jnp.arange(probes, dtype=jnp.int32)
    high = lax.ppermute(own, "state", shift_pairs(slabs, -1))
    low = lax.ppermute(own.astype(bf16), "state", shift_pairs(slabs, 1))

    shifted, coef, start, panel = call(
        prelude_kernel,
        (
            jax.ShapeDtypeStruct((cells, columns, height, TILE), f32),
            jax.ShapeDtypeStruct((5, height, TILE), f32),
            jax.ShapeDtypeStruct(tile_index.shape, jnp.int32),
            jax.ShapeDtypeStruct(actuator_panel.shape[1:], bf16),
        ),
        vmem=8,
        smem=1,
        inputs=6,
    )(probe_offset, own, courant[None], diffusivity[None], tile_index, actuator_panel[0])

    half = probes // 2
    far = lax.ppermute(actuator_panel[0], "probe", [(i, i ^ half) for i in range(probes)])
    coef = tied(coef, far)
    field_shape = pltpu.VMEM((planes, columns, height + 2 * PAD, TILE), f32)
    tiles = call(
        adjoint_kernel,
        jax.ShapeDtypeStruct((tile_total * STEPS + 2 * PAD, TILE), f32),
        vmem=10,
        scratch=(field_shape, field_shape),
        smem=1,
        inputs=5,
    )(probe_offset, coef, shifted, low, high)

    panels = list(enumerate([[panel]] + gathered_panel(actuator_panel[0], "probe", coef, far)))

    def project(shards, *given):
        pieces = [piece for _, pieces in shards for piece in pieces]
        return call(
            lambda *refs: project_kernel(layout(shards), shard, *refs),
            jax.ShapeDtypeStruct((groups, 2 * STEPS, TILE), f32),
            vmem=6,
            scratch=(pltpu.VMEM((shard * GROUP, TILE), f32),),
            smem=2,
            inputs=3 + len(pieces) + len(given),
        )(source, start, tiles, *pieces, *given)

    before = project(panels[:-1])
    parts = summands(project(panels[-1:], before), "state")
    pieces = [piece for _, pieces in panels for piece in pieces]
    order = [len(parts) - 1] + list(range(1, len(parts) - 1)) + [0] if len(parts) > 1 else [0]
    payload = jax.ShapeDtypeStruct((2 * cells - 1, height * columns, TILE), bf16)
    heads = jax.ShapeDtypeStruct((cells, height * columns, TILE), bf16)
    total, forced, rightward, leftward = call(
        lambda *refs: deposit_kernel(order, layout(panels), shard, *refs),
        (
            jax.ShapeDtypeStruct(before.shape, f32),
            jax.ShapeDtypeStruct((cells, height * columns, TILE), f32),
            payload,
            heads,
        ),
        vmem=16,
        scratch=(
            pltpu.VMEM((actuators, 2 * TILE), bf16),
            pltpu.VMEM((height * columns, actuators), bf16),
            pltpu.VMEM((height * columns, actuators), bf16),
        ),
        smem=1,
        inputs=2 + len(parts) + len(pieces),
    )(source, start, *[parts[k] for k in order], *pieces)
    from_low = lax.ppermute(rightward, "state", shift_pairs(slabs, 1))
    from_high = lax.ppermute(leftward, "state", shift_pairs(slabs, -1))
    response = call(
        forward_kernel,
        jax.ShapeDtypeStruct((cells, height, width), f32),
        vmem=10,
        scratch=(field_shape, field_shape),
        inputs=4,
    )(coef, forced, from_low, from_high)
    projections = total.reshape(groups, 2, STEPS, TILE).transpose(2, 0, 1, 3)
    return projections.reshape(STEPS, 1, actuators), response[None]


def solution(mesh):
    return jax.shard_map(
        local,
        mesh=mesh,
        in_specs=(
            P("probe", "state", None, None),
            P(),
            P(),
            P("probe"),
            P("state", None),
            P("state", "probe", None),
        ),
        out_specs=(P(None, "probe", None), P("probe", "state", None, None)),
        check_vma=False,
    )
```

```python
import jax
import jax.numpy as jnp
from jax import lax
from jax.experimental import pallas as pl
from jax.experimental.pallas import tpu as pltpu
from jax.sharding import PartitionSpec as P

TILE = 128
STEPS = 4
PAD = 8
GROUP = 256


def shift_pairs(count, by):
    return [(i, (i + by) % count) for i in range(count)]


def clear_pads(buffer):
    planes, columns, rows, lanes = buffer.shape
    edge = jnp.zeros((columns, PAD, lanes), buffer.dtype)

    def body(plane, carry):
        buffer[plane, :, :PAD, :] = edge
        buffer[plane, :, rows - PAD :, :] = edge
        return carry

    lax.fori_loop(0, planes, body, 0)


def sweep_rows(source, coef, planes, row, adjoint):
    here = pl.ds(pl.multiple_of(PAD + row, 8), 8)
    block = pl.ds(pl.multiple_of(row, 8), 8)
    columns = source.shape[1]
    lane = lax.broadcasted_iota(jnp.int32, (8, TILE), 1)
    weights = [coef[place, block, :] for place in range(5)]
    lower, centre = source[planes[0] - 1, :, here, :], source[planes[0], :, here, :]
    out = []
    for plane in planes:
        upper = source[plane + 1, :, here, :]
        above = source[plane, :, pl.ds(PAD + row + 1, 8), :]
        below = source[plane, :, pl.ds(PAD + row - 1, 8), :]
        left = [pltpu.roll(centre[c], TILE - 1, 1) for c in range(columns)]
        right = [pltpu.roll(centre[c], 1, 1) for c in range(columns)]
        results = []
        for c in range(columns):
            upper_z = jnp.where(lane == TILE - 1, left[(c + 1) % columns], left[c])
            lower_z = jnp.where(lane == 0, right[(c - 1) % columns], right[c])
            total = weights[0] * centre[c]
            if adjoint:
                total = total + weights[1] * upper[c]
                total = total + weights[2] * (lower[c] + (upper_z + lower_z))
                total = total + (weights[3] * above[c] + weights[4] * below[c])
            else:
                total = total + weights[1] * lower[c]
                total = total + weights[2] * ((upper[c] + (upper_z + lower_z)) + (above[c] + below[c]))
            results.append(total)
        out.append(results)
        lower, centre = centre, upper
    return out


def split(value):
    high = value.astype(jnp.bfloat16)
    low = (value - high.astype(jnp.float32)).astype(jnp.bfloat16)
    return high, low


def shifted_plane(field, plane, offset):
    height, width = field.shape[1:]
    columns = width // TILE
    turn, rest = offset // TILE, offset % TILE
    lane = lax.broadcasted_iota(jnp.int32, (height, TILE), 1)
    parts = [field[plane, :, pl.ds(c * TILE, TILE)].astype(jnp.float32) for c in range(columns)]
    rolled = [pltpu.roll(part, rest, 1) for part in parts]
    return [
        (lax.rem(c + turn, columns), jnp.where(lane >= rest, rolled[c], rolled[c - 1]))
        for c in range(columns)
    ]


def prelude_kernel(offset, field, courant, diffusivity, tile, panel, own, coef, start, kept):
    columns, height = own.shape[1:3]

    def load(plane, carry):
        for column, value in shifted_plane(field, plane, offset[0]):
            own[plane, column] = value
        return carry

    lax.fori_loop(0, field.shape[0], load, 0)
    kept[...] = panel[...]
    padding = jnp.zeros((6, height), jnp.float32)
    upright = jnp.concatenate([courant[...], diffusivity[...], padding], axis=0).T
    speed = jnp.broadcast_to(upright[:, 0:1], (height, TILE))
    rate = jnp.broadcast_to(upright[:, 1:2], (height, TILE))
    edge = jnp.zeros((1, TILE), jnp.float32)
    coef[0] = 1.0 - speed - 6.0 * rate
    coef[1] = speed + rate
    coef[2] = rate
    coef[3] = jnp.concatenate([rate[1:], edge], axis=0)
    coef[4] = jnp.concatenate([edge, rate[:-1]], axis=0)
    numbers = tile[...]
    inside = numbers & (columns * height - 1)
    numbers = (numbers - inside) + (inside & (columns - 1)) * height + inside // columns
    start[...] = numbers * STEPS


def adjoint_kernel(offset, coef, own, low, high, tiles, first, second):
    cells, columns, height = own.shape[:3]
    steps = STEPS
    edge = jnp.zeros((PAD, TILE), jnp.float32)
    tiles[:PAD, :] = edge
    tiles[tiles.shape[0] - PAD :, :] = edge
    inside = pl.ds(PAD, height)
    clear_pads(first)
    clear_pads(second)

    def load(plane, carry):
        for slab, field in ((0, low), (2, high)):
            for column, value in shifted_plane(field, plane, offset[0]):
                first[slab * cells + plane, column, inside, :] = value
        first[cells + plane, :, inside, :] = own[plane]
        return carry

    lax.fori_loop(0, cells, load, 0)
    buffers = (first, second)
    for step in range(steps):
        source, target = buffers[step % 2], buffers[(step + 1) % 2]

        def sweep(place, carry, source=source, target=target, step=step):
            planes = range(step + 1, 3 * cells - step - 1)
            row = place * 8
            for plane, block in zip(planes, sweep_rows(source, coef, planes, row, True)):
                for c in range(columns):
                    if step < steps - 1:
                        where = pl.ds(pl.multiple_of(PAD + row, 8), 8)
                        target[plane, c, where, :] = block[c]
                    if cells <= plane < 2 * cells:
                        number = ((plane - cells) * columns + c) * height + row
                        tiles[pl.ds(PAD + number * steps + step, 8, stride=steps), :] = block[c]
            return carry

        lax.fori_loop(0, height // 8, sweep, 0, unroll=8)


def forward_kernel(coef, own, low, high, out, first, second):
    cells, height, width = out.shape
    columns = width // TILE
    steps = STEPS
    clear_pads(first)
    clear_pads(second)
    for plane in range(cells):
        for c in range(columns):
            where = pl.ds(c * height, height)
            inside = pl.ds(PAD, height)
            first[cells + plane, c, inside, :] = own[plane, where, :]
            first[2 * cells + plane, c, inside, :] = high[plane, where, :].astype(jnp.float32)
            value = low[plane, where, :].astype(jnp.float32)
            if plane > 0:
                value = value + low[cells + plane - 1, where, :].astype(jnp.float32)
            first[plane, c, inside, :] = value
    buffers = (first, second)
    for step in range(steps):
        source, target = buffers[step % 2], buffers[(step + 1) % 2]

        def sweep(place, carry, source=source, target=target, step=step):
            planes = range(step + 1, 3 * cells - step - 1)
            row = place * 8
            for plane, block in zip(planes, sweep_rows(source, coef, planes, row, False)):
                for c in range(columns):
                    if step == steps - 1:
                        where = pl.ds(pl.multiple_of(row, 8), 8)
                        out[plane - cells, where, pl.ds(c * TILE, TILE)] = block[c]
                    else:
                        target[plane, c, pl.ds(pl.multiple_of(PAD + row, 8), 8), :] = block[c]
            return carry

        lax.fori_loop(0, height // 8, sweep, 0, unroll=8)


def project_kernel(places, shard, source, start, tiles, *refs):
    panels, (*before, out, wide) = refs[: len(places)], refs[len(places) :]
    for given in before:
        out[...] = given[...]
    first = lax.broadcasted_iota(jnp.int32, (8, TILE), 0) < STEPS
    lane = lax.broadcasted_iota(jnp.int32, (8, TILE), 1)
    for (chunk, offset), panel in zip(places, panels):
        wide[: panel.shape[0], :] = panel[...].astype(jnp.float32)

        def body(group, carry, chunk=chunk, offset=offset):
            number = source[chunk] * shard + offset + group
            sums = jnp.zeros((8, TILE), jnp.float32)
            for place in range(TILE):
                left = start[0, number * GROUP + place]
                right = start[0, number * GROUP + TILE + place]
                cells = jnp.where(
                    first, tiles[pl.ds(PAD + left, 8), :], tiles[pl.ds(PAD - STEPS + right, 8), :]
                )
                row = group * GROUP + place
                rows = jnp.where(first, wide[pl.ds(row, 1), :], wide[pl.ds(row + TILE, 1), :])
                total = jnp.sum(cells * rows, axis=1, keepdims=True)
                sums = jnp.where(lane == place, total, sums)
            out[number] = sums
            return carry

        groups = panel.shape[0] // GROUP
        lax.fori_loop(0, groups, body, 0, unroll=min(4, groups))


def deposit_kernel(order, places, shard, source, start, *refs):
    parts, panels = refs[: len(order)], refs[len(order) : -7]
    total, field, rightward, leftward, scaled, *chosen = refs[-7:]
    cells, per_plane = field.shape[0], field.shape[1]
    blocks = []
    for (chunk, offset), panel in zip(places, panels):
        for group in range(panel.shape[0] // GROUP):
            number = source[chunk] * shard + offset + group
            blocks += [(number, half, panel, group * GROUP + half * TILE) for half in range(2)]
    one, none = jnp.ones((), jnp.bfloat16), jnp.zeros((), jnp.bfloat16)
    tiles = []
    for number, half, _, _ in blocks:
        where = pl.ds(pl.multiple_of(number * GROUP + half * TILE, TILE), TILE)
        tiles.append(start[:, where].astype(jnp.int16))

    def choose(plane):
        target = chosen[plane % 2]
        rows = 64
        for top in range(0, per_plane, rows):
            first = (plane * per_plane + top) * STEPS
            by_row = lax.broadcasted_iota(jnp.int32, (rows, TILE), 0) * STEPS + first
            by_row = by_row.astype(jnp.int16)
            for place, tile in enumerate(tiles):
                found = jnp.where(tile == by_row, one, none)
                target[pl.ds(top, rows), pl.ds(place * TILE, TILE)] = found

    def finish(plane, sums):
        value = sums[:, :TILE] + sums[:, TILE:]
        field[plane] = value
        head, tail = split(value)
        leftward[plane] = head
        rightward[plane] = head
        if plane > 0:
            rightward[cells + plane - 1] = tail

    choose(0)
    summed = dict(zip(order, [part[...] for part in parts]))
    total[...] = tree_sum([summed[k] for k in range(len(parts))])
    last = [total[number, pl.ds(half * STEPS + STEPS - 1, 1), :] for number, half, _, _ in blocks]
    drive = jnp.concatenate(last, axis=0).T
    sums = jnp.zeros((per_plane, 2 * TILE), jnp.float32)
    for place, (_, half, panel, row) in enumerate(blocks):
        rows = panel[pl.ds(row, TILE), :].astype(jnp.float32)
        head, tail = split(drive[:, place : place + 1] * rows)
        scaled[pl.ds(place * TILE, TILE), pl.ds(0, TILE)] = head
        scaled[pl.ds(place * TILE, TILE), pl.ds(TILE, TILE)] = tail
        if half:
            where = pl.ds((place - 1) * TILE, GROUP)
            sums = sums + jnp.dot(
                chosen[0][:, where], scaled[where, :], preferred_element_type=jnp.float32
            )
    choose(1)
    finish(0, sums)
    for plane in range(1, cells):
        if plane < cells - 1:
            choose(plane + 1)
        finish(
            plane, jnp.dot(chosen[plane % 2][...], scaled[...], preferred_element_type=jnp.float32)
        )


def call(kernel, out_shape, vmem, scratch=(), smem=0, inputs=0):
    in_specs = [pl.BlockSpec(memory_space=pltpu.SMEM)] * smem
    in_specs += [pl.BlockSpec(memory_space=pltpu.VMEM)] * (inputs - smem)
    out_specs = jax.tree.map(lambda _: pl.BlockSpec(memory_space=pltpu.VMEM), out_shape)
    return pl.pallas_call(
        kernel,
        out_shape=out_shape,
        in_specs=in_specs,
        out_specs=out_specs,
        scratch_shapes=list(scratch),
        compiler_params=pltpu.CompilerParams(vmem_limit_bytes=vmem * 1024 * 1024),
        cost_estimate=pl.CostEstimate(flops=1024, bytes_accessed=1024, transcendentals=0),
    )


def gathered_panel(panel, axis, soon, late, first):
    count = lax.axis_size(axis)
    shards, mask = {0: [panel]}, count // 2
    while mask:
        pairs = [(i, i ^ mask) for i in range(count)]
        for held in sorted(shards):
            pieces = shards[held]
            if held:
                pieces = [tied(piece, late) for piece in pieces]
            else:
                pieces = [tied(piece, soon) for piece in pieces]
            if len(shards) == 1:
                shards[mask] = [first]
                continue
            shards[held | mask] = [lax.ppermute(piece, axis, pairs) for piece in pieces]
        mask //= 2
    return [shards[k] for k in range(1, count)]


def layout(panels):
    places = []
    for chunk, pieces in panels:
        first = 0
        for piece in pieces:
            places.append((chunk, first))
            first += piece.shape[0] // GROUP
    return places


def tied(value, *others):
    return lax.optimization_barrier((value,) + others)[0]


def tree_sum(parts):
    while len(parts) > 1:
        parts = [parts[i] + parts[i + 1] for i in range(0, len(parts), 2)]
    return parts[0]


def summands(part, axis):
    count = lax.axis_size(axis)
    if count & (count - 1):
        return [lax.psum(part, axis)]
    done, parts = 1, [part]
    for span in (2, 4, 4, 4, 4):
        span = min(span, count // done)
        if span > 1:
            part = tree_sum(parts)
            came = {0: part}
            for k in range(span - 1, 0, -1):
                came[k] = lax.ppermute(part, axis, [(i, i ^ (k * done)) for i in range(count)])
            parts = [came[k] for k in range(span)]
            done *= span
    return parts


def local(sensor_field, courant, diffusivity, probe_offset, tile_index, actuator_panel):
    slabs, probes = lax.axis_size("state"), lax.axis_size("probe")
    own = sensor_field[0]
    cells, height, width = own.shape
    columns = width // TILE
    tile_total = cells * height * columns
    actuators = tile_index.shape[1]
    groups = actuators // GROUP
    shard = groups // probes
    planes = 3 * cells
    f32, bf16 = jnp.float32, jnp.bfloat16

    source = lax.axis_index("probe") ^ jnp.arange(probes, dtype=jnp.int32)
    high = lax.ppermute(own, "state", shift_pairs(slabs, -1))
    rounded = own.astype(bf16)
    low = lax.ppermute(rounded, "state", shift_pairs(slabs, 1))

    shifted, coef, start, panel = call(
        prelude_kernel,
        (
            jax.ShapeDtypeStruct((cells, columns, height, TILE), f32),
            jax.ShapeDtypeStruct((5, height, TILE), f32),
            jax.ShapeDtypeStruct(tile_index.shape, jnp.int32),
            jax.ShapeDtypeStruct(actuator_panel.shape[1:], bf16),
        ),
        vmem=8,
        smem=1,
        inputs=6,
    )(probe_offset, own, courant[None], diffusivity[None], tile_index, actuator_panel[0])

    half = probes // 2
    far = lax.ppermute(actuator_panel[0], "probe", [(i, i ^ half) for i in range(probes)])
    coef = tied(coef, far)
    field_shape = pltpu.VMEM((planes, columns, height + 2 * PAD, TILE), f32)
    tiles = call(
        adjoint_kernel,
        jax.ShapeDtypeStruct((tile_total * STEPS + 2 * PAD, TILE), f32),
        vmem=10,
        scratch=(field_shape, field_shape),
        smem=1,
        inputs=5,
    )(probe_offset, coef, shifted, low, high)

    panels = list(enumerate([[panel]] + gathered_panel(actuator_panel[0], "probe", rounded, coef, far)))

    def project(shards, *given):
        pieces = [piece for _, pieces in shards for piece in pieces]
        return call(
            lambda *refs: project_kernel(layout(shards), shard, *refs),
            jax.ShapeDtypeStruct((groups, 2 * STEPS, TILE), f32),
            vmem=6,
            scratch=(pltpu.VMEM((shard * GROUP, TILE), f32),),
            smem=2,
            inputs=3 + len(pieces) + len(given),
        )(source, start, tiles, *pieces, *given)

    before = project(panels[:-1])
    parts = summands(project(panels[-1:], before), "state")
    pieces = [piece for _, pieces in panels for piece in pieces]
    order = [len(parts) - 1] + list(range(1, len(parts) - 1)) + [0] if len(parts) > 1 else [0]
    payload = jax.ShapeDtypeStruct((2 * cells - 1, height * columns, TILE), bf16)
    heads = jax.ShapeDtypeStruct((cells, height * columns, TILE), bf16)
    total, forced, rightward, leftward = call(
        lambda *refs: deposit_kernel(order, layout(panels), shard, *refs),
        (
            jax.ShapeDtypeStruct(before.shape, f32),
            jax.ShapeDtypeStruct((cells, height * columns, TILE), f32),
            payload,
            heads,
        ),
        vmem=16,
        scratch=(
            pltpu.VMEM((actuators, 2 * TILE), bf16),
            pltpu.VMEM((height * columns, actuators), bf16),
            pltpu.VMEM((height * columns, actuators), bf16),
        ),
        smem=1,
        inputs=2 + len(parts) + len(pieces),
    )(source, start, *[parts[k] for k in order], *pieces)
    from_low = lax.ppermute(rightward, "state", shift_pairs(slabs, 1))
    from_high = lax.ppermute(leftward, "state", shift_pairs(slabs, -1))
    response = call(
        forward_kernel,
        jax.ShapeDtypeStruct((cells, height, width), f32),
        vmem=10,
        scratch=(field_shape, field_shape),
        inputs=4,
    )(coef, forced, from_low, from_high)
    projections = total.reshape(groups, 2, STEPS, TILE).transpose(2, 0, 1, 3)
    return projections.reshape(STEPS, 1, actuators), response[None]


def solution(mesh):
    return jax.shard_map(
        local,
        mesh=mesh,
        in_specs=(
            P("probe", "state", None, None),
            P(),
            P(),
            P("probe"),
            P("state", None),
            P("state", "probe", None),
        ),
        out_specs=(P(None, "probe", None), P("probe", "state", None, None)),
        check_vma=False,
    )
```

```python
import jax
import jax.numpy as jnp
from jax import lax
from jax.experimental import pallas as pl
from jax.experimental.pallas import tpu as pltpu
from jax.sharding import PartitionSpec as P

TILE = 128
STEPS = 4
PAD = 8
GROUP = 256


def shift_pairs(count, by):
    return [(i, (i + by) % count) for i in range(count)]


def clear_pads(buffer):
    planes, columns, rows, lanes = buffer.shape
    edge = jnp.zeros((columns, PAD, lanes), buffer.dtype)

    def body(plane, carry):
        buffer[plane, :, :PAD, :] = edge
        buffer[plane, :, rows - PAD :, :] = edge
        return carry

    lax.fori_loop(0, planes, body, 0)


def sweep_rows(source, coef, planes, row, adjoint):
    here = pl.ds(pl.multiple_of(PAD + row, 8), 8)
    block = pl.ds(pl.multiple_of(row, 8), 8)
    columns = source.shape[1]
    lane = lax.broadcasted_iota(jnp.int32, (8, TILE), 1)
    weights = [coef[place, block, :] for place in range(5)]
    lower, centre = source[planes[0] - 1, :, here, :], source[planes[0], :, here, :]
    out = []
    for plane in planes:
        upper = source[plane + 1, :, here, :]
        above = source[plane, :, pl.ds(PAD + row + 1, 8), :]
        below = source[plane, :, pl.ds(PAD + row - 1, 8), :]
        left = [pltpu.roll(centre[c], TILE - 1, 1) for c in range(columns)]
        right = [pltpu.roll(centre[c], 1, 1) for c in range(columns)]
        results = []
        for c in range(columns):
            upper_z = jnp.where(lane == TILE - 1, left[(c + 1) % columns], left[c])
            lower_z = jnp.where(lane == 0, right[(c - 1) % columns], right[c])
            total = weights[0] * centre[c]
            if adjoint:
                total = total + weights[1] * upper[c]
                total = total + weights[2] * (lower[c] + (upper_z + lower_z))
                total = total + (weights[3] * above[c] + weights[4] * below[c])
            else:
                total = total + weights[1] * lower[c]
                total = total + weights[2] * ((upper[c] + (upper_z + lower_z)) + (above[c] + below[c]))
            results.append(total)
        out.append(results)
        lower, centre = centre, upper
    return out


def split(value):
    high = value.astype(jnp.bfloat16)
    low = (value - high.astype(jnp.float32)).astype(jnp.bfloat16)
    return high, low


def shifted_plane(field, plane, offset):
    height, width = field.shape[1:]
    columns = width // TILE
    turn, rest = offset // TILE, offset % TILE
    lane = lax.broadcasted_iota(jnp.int32, (height, TILE), 1)
    parts = [field[plane, :, pl.ds(c * TILE, TILE)].astype(jnp.float32) for c in range(columns)]
    rolled = [pltpu.roll(part, rest, 1) for part in parts]
    return [
        (lax.rem(c + turn, columns), jnp.where(lane >= rest, rolled[c], rolled[c - 1]))
        for c in range(columns)
    ]


def prelude_kernel(offset, field, courant, diffusivity, tile, panel, own, coef, start, kept):
    columns, height = own.shape[1:3]

    def load(plane, carry):
        for column, value in shifted_plane(field, plane, offset[0]):
            own[plane, column] = value
        return carry

    lax.fori_loop(0, field.shape[0], load, 0)
    kept[...] = panel[...]
    padding = jnp.zeros((6, height), jnp.float32)
    upright = jnp.concatenate([courant[...], diffusivity[...], padding], axis=0).T
    speed = jnp.broadcast_to(upright[:, 0:1], (height, TILE))
    rate = jnp.broadcast_to(upright[:, 1:2], (height, TILE))
    edge = jnp.zeros((1, TILE), jnp.float32)
    coef[0] = 1.0 - speed - 6.0 * rate
    coef[1] = speed + rate
    coef[2] = rate
    coef[3] = jnp.concatenate([rate[1:], edge], axis=0)
    coef[4] = jnp.concatenate([edge, rate[:-1]], axis=0)
    numbers = tile[...]
    inside = numbers & (columns * height - 1)
    numbers = (numbers - inside) + (inside & (columns - 1)) * height + inside // columns
    start[...] = numbers * STEPS


def adjoint_kernel(offset, coef, own, low, high, tiles, first, second):
    cells, columns, height = own.shape[:3]
    steps = STEPS
    edge = jnp.zeros((PAD, TILE), jnp.float32)
    tiles[:PAD, :] = edge
    tiles[tiles.shape[0] - PAD :, :] = edge
    inside = pl.ds(PAD, height)
    clear_pads(first)
    clear_pads(second)

    def load(plane, carry):
        for slab, field in ((0, low), (2, high)):
            for column, value in shifted_plane(field, plane, offset[0]):
                first[slab * cells + plane, column, inside, :] = value
        first[cells + plane, :, inside, :] = own[plane]
        return carry

    lax.fori_loop(0, cells, load, 0)
    buffers = (first, second)
    for step in range(steps):
        source, target = buffers[step % 2], buffers[(step + 1) % 2]

        def sweep(place, carry, source=source, target=target, step=step):
            planes = range(step + 1, 3 * cells - step - 1)
            row = place * 8
            for plane, block in zip(planes, sweep_rows(source, coef, planes, row, True)):
                for c in range(columns):
                    if step < steps - 1:
                        where = pl.ds(pl.multiple_of(PAD + row, 8), 8)
                        target[plane, c, where, :] = block[c]
                    if cells <= plane < 2 * cells:
                        number = ((plane - cells) * columns + c) * height + row
                        tiles[pl.ds(PAD + number * steps + step, 8, stride=steps), :] = block[c]
            return carry

        lax.fori_loop(0, height // 8, sweep, 0, unroll=8)


def forward_kernel(coef, own, low, high, out, first, second):
    cells, height, width = out.shape
    columns = width // TILE
    steps = STEPS
    clear_pads(first)
    clear_pads(second)
    for plane in range(cells):
        for c in range(columns):
            where = pl.ds(c * height, height)
            inside = pl.ds(PAD, height)
            first[cells + plane, c, inside, :] = own[plane, where, :]
            first[2 * cells + plane, c, inside, :] = high[plane, where, :].astype(jnp.float32)
            value = low[plane, where, :].astype(jnp.float32)
            if plane > 0:
                value = value + low[cells + plane - 1, where, :].astype(jnp.float32)
            first[plane, c, inside, :] = value
    buffers = (first, second)
    for step in range(steps):
        source, target = buffers[step % 2], buffers[(step + 1) % 2]

        def sweep(place, carry, source=source, target=target, step=step):
            planes = range(step + 1, 3 * cells - step - 1)
            row = place * 8
            for plane, block in zip(planes, sweep_rows(source, coef, planes, row, False)):
                for c in range(columns):
                    if step == steps - 1:
                        where = pl.ds(pl.multiple_of(row, 8), 8)
                        out[plane - cells, where, pl.ds(c * TILE, TILE)] = block[c]
                    else:
                        target[plane, c, pl.ds(pl.multiple_of(PAD + row, 8), 8), :] = block[c]
            return carry

        lax.fori_loop(0, height // 8, sweep, 0, unroll=8)


def project_kernel(places, shard, source, start, tiles, *refs):
    panels, (*before, out, wide) = refs[: len(places)], refs[len(places) :]
    for given in before:
        out[...] = given[...]
    first = lax.broadcasted_iota(jnp.int32, (8, TILE), 0) < STEPS
    lane = lax.broadcasted_iota(jnp.int32, (8, TILE), 1)
    for (chunk, offset), panel in zip(places, panels):
        wide[: panel.shape[0], :] = panel[...].astype(jnp.float32)

        def body(group, carry, chunk=chunk, offset=offset):
            number = source[chunk] * shard + offset + group
            sums = jnp.zeros((8, TILE), jnp.float32)
            for place in range(TILE):
                left = start[0, number * GROUP + place]
                right = start[0, number * GROUP + TILE + place]
                cells = jnp.where(
                    first, tiles[pl.ds(PAD + left, 8), :], tiles[pl.ds(PAD - STEPS + right, 8), :]
                )
                row = group * GROUP + place
                rows = jnp.where(first, wide[pl.ds(row, 1), :], wide[pl.ds(row + TILE, 1), :])
                total = jnp.sum(cells * rows, axis=1, keepdims=True)
                sums = jnp.where(lane == place, total, sums)
            out[number] = sums
            return carry

        groups = panel.shape[0] // GROUP
        lax.fori_loop(0, groups, body, 0, unroll=min(4, groups))


def deposit_kernel(order, places, shard, source, start, *refs):
    parts, panels = refs[: len(order)], refs[len(order) : -7]
    total, field, rightward, leftward, scaled, *chosen = refs[-7:]
    cells, per_plane = field.shape[0], field.shape[1]
    blocks = []
    for (chunk, offset), panel in zip(places, panels):
        for group in range(panel.shape[0] // GROUP):
            number = source[chunk] * shard + offset + group
            blocks += [(number, half, panel, group * GROUP + half * TILE) for half in range(2)]
    one, none = jnp.ones((), jnp.bfloat16), jnp.zeros((), jnp.bfloat16)
    tiles = []
    for number, half, _, _ in blocks:
        where = pl.ds(pl.multiple_of(number * GROUP + half * TILE, TILE), TILE)
        tiles.append(start[:, where].astype(jnp.int16))

    def choose(plane):
        target = chosen[plane % 2]
        rows = 64
        for top in range(0, per_plane, rows):
            first = (plane * per_plane + top) * STEPS
            by_row = lax.broadcasted_iota(jnp.int32, (rows, TILE), 0) * STEPS + first
            by_row = by_row.astype(jnp.int16)
            for place, tile in enumerate(tiles):
                found = jnp.where(tile == by_row, one, none)
                target[pl.ds(top, rows), pl.ds(place * TILE, TILE)] = found

    def finish(plane, sums):
        value = sums[:, :TILE] + sums[:, TILE:]
        field[plane] = value
        head, tail = split(value)
        leftward[plane] = head
        rightward[plane] = head
        if plane > 0:
            rightward[cells + plane - 1] = tail

    choose(0)
    summed = dict(zip(order, [part[...] for part in parts]))
    total[...] = tree_sum([summed[k] for k in range(len(parts))])
    last = [total[number, pl.ds(half * STEPS + STEPS - 1, 1), :] for number, half, _, _ in blocks]
    drive = jnp.concatenate(last, axis=0).T
    sums = jnp.zeros((per_plane, 2 * TILE), jnp.float32)
    for place, (_, half, panel, row) in enumerate(blocks):
        rows = panel[pl.ds(row, TILE), :].astype(jnp.float32)
        head, tail = split(drive[:, place : place + 1] * rows)
        scaled[pl.ds(place * TILE, TILE), pl.ds(0, TILE)] = head
        scaled[pl.ds(place * TILE, TILE), pl.ds(TILE, TILE)] = tail
        if half:
            where = pl.ds((place - 1) * TILE, GROUP)
            sums = sums + jnp.dot(
                chosen[0][:, where], scaled[where, :], preferred_element_type=jnp.float32
            )
    choose(1)
    finish(0, sums)
    for plane in range(1, cells):
        if plane < cells - 1:
            choose(plane + 1)
        finish(
            plane, jnp.dot(chosen[plane % 2][...], scaled[...], preferred_element_type=jnp.float32)
        )


def call(kernel, out_shape, vmem, scratch=(), smem=0, inputs=0):
    in_specs = [pl.BlockSpec(memory_space=pltpu.SMEM)] * smem
    in_specs += [pl.BlockSpec(memory_space=pltpu.VMEM)] * (inputs - smem)
    out_specs = jax.tree.map(lambda _: pl.BlockSpec(memory_space=pltpu.VMEM), out_shape)
    return pl.pallas_call(
        kernel,
        out_shape=out_shape,
        in_specs=in_specs,
        out_specs=out_specs,
        scratch_shapes=list(scratch),
        compiler_params=pltpu.CompilerParams(vmem_limit_bytes=vmem * 1024 * 1024),
        cost_estimate=pl.CostEstimate(flops=1024, bytes_accessed=1024, transcendentals=0),
    )


def gathered_panel(panel, axis, late, first):
    count = lax.axis_size(axis)
    shards, mask = {0: [panel]}, count // 2
    while mask:
        pairs = [(i, i ^ mask) for i in range(count)]
        for held in sorted(shards):
            pieces = shards[held]
            if held:
                pieces = [tied(piece, late) for piece in pieces]
            if len(shards) == 1:
                shards[mask] = [first]
                continue
            shards[held | mask] = [lax.ppermute(piece, axis, pairs) for piece in pieces]
        mask //= 2
    return [shards[k] for k in range(1, count)]


def layout(panels):
    places = []
    for chunk, pieces in panels:
        first = 0
        for piece in pieces:
            places.append((chunk, first))
            first += piece.shape[0] // GROUP
    return places


def tied(value, *others):
    return lax.optimization_barrier((value,) + others)[0]


def tree_sum(parts):
    while len(parts) > 1:
        parts = [parts[i] + parts[i + 1] for i in range(0, len(parts), 2)]
    return parts[0]


def summands(part, axis):
    count = lax.axis_size(axis)
    if count & (count - 1):
        return [lax.psum(part, axis)]
    done, parts = 1, [part]
    for span in (2, 4, 4, 4, 4):
        span = min(span, count // done)
        if span > 1:
            part = tree_sum(parts)
            came = {0: part}
            for k in range(span - 1, 0, -1):
                came[k] = lax.ppermute(part, axis, [(i, i ^ (k * done)) for i in range(count)])
            parts = [came[k] for k in range(span)]
            done *= span
    return parts


def local(sensor_field, courant, diffusivity, probe_offset, tile_index, actuator_panel):
    slabs, probes = lax.axis_size("state"), lax.axis_size("probe")
    own = sensor_field[0]
    cells, height, width = own.shape
    columns = width // TILE
    tile_total = cells * height * columns
    actuators = tile_index.shape[1]
    groups = actuators // GROUP
    shard = groups // probes
    planes = 3 * cells
    f32, bf16 = jnp.float32, jnp.bfloat16

    source = lax.axis_index("probe") ^ jnp.arange(probes, dtype=jnp.int32)
    high = lax.ppermute(own, "state", shift_pairs(slabs, -1))
    low = lax.ppermute(own.astype(bf16), "state", shift_pairs(slabs, 1))

    shifted, coef, start, panel = call(
        prelude_kernel,
        (
            jax.ShapeDtypeStruct((cells, columns, height, TILE), f32),
            jax.ShapeDtypeStruct((5, height, TILE), f32),
            jax.ShapeDtypeStruct(tile_index.shape, jnp.int32),
            jax.ShapeDtypeStruct(actuator_panel.shape[1:], bf16),
        ),
        vmem=8,
        smem=1,
        inputs=6,
    )(probe_offset, own, courant[None], diffusivity[None], tile_index, actuator_panel[0])

    half = probes // 2
    far = lax.ppermute(actuator_panel[0], "probe", [(i, i ^ half) for i in range(probes)])
    coef = tied(coef, far)
    field_shape = pltpu.VMEM((planes, columns, height + 2 * PAD, TILE), f32)
    tiles = call(
        adjoint_kernel,
        jax.ShapeDtypeStruct((tile_total * STEPS + 2 * PAD, TILE), f32),
        vmem=10,
        scratch=(field_shape, field_shape),
        smem=1,
        inputs=5,
    )(probe_offset, coef, shifted, low, high)

    panels = list(enumerate([[panel]] + gathered_panel(actuator_panel[0], "probe", coef, far)))

    def project(shards, *given):
        pieces = [piece for _, pieces in shards for piece in pieces]
        return call(
            lambda *refs: project_kernel(layout(shards), shard, *refs),
            jax.ShapeDtypeStruct((groups, 2 * STEPS, TILE), f32),
            vmem=6,
            scratch=(pltpu.VMEM((shard * GROUP, TILE), f32),),
            smem=2,
            inputs=3 + len(pieces) + len(given),
        )(source, start, tiles, *pieces, *given)

    before = project(panels[:-1])
    parts = summands(project(panels[-1:], before), "state")
    pieces = [piece for _, pieces in panels for piece in pieces]
    order = [len(parts) - 1] + list(range(1, len(parts) - 1)) + [0] if len(parts) > 1 else [0]
    payload = jax.ShapeDtypeStruct((2 * cells - 1, height * columns, TILE), bf16)
    heads = jax.ShapeDtypeStruct((cells, height * columns, TILE), bf16)
    total, forced, rightward, leftward = call(
        lambda *refs: deposit_kernel(order, layout(panels), shard, *refs),
        (
            jax.ShapeDtypeStruct(before.shape, f32),
            jax.ShapeDtypeStruct((cells, height * columns, TILE), f32),
            payload,
            heads,
        ),
        vmem=16,
        scratch=(
            pltpu.VMEM((actuators, 2 * TILE), bf16),
            pltpu.VMEM((height * columns, actuators), bf16),
            pltpu.VMEM((height * columns, actuators), bf16),
        ),
        smem=1,
        inputs=2 + len(parts) + len(pieces),
    )(source, start, *[parts[k] for k in order], *pieces)
    from_low = lax.ppermute(rightward, "state", shift_pairs(slabs, 1))
    from_high = lax.ppermute(leftward, "state", shift_pairs(slabs, -1))
    response = call(
        forward_kernel,
        jax.ShapeDtypeStruct((cells, height, width), f32),
        vmem=10,
        scratch=(field_shape, field_shape),
        inputs=4,
    )(coef, forced, from_low, from_high)
    projections = total.reshape(groups, 2, STEPS, TILE).transpose(2, 0, 1, 3)
    return projections.reshape(STEPS, 1, actuators), response[None]


def solution(mesh):
    return jax.shard_map(
        local,
        mesh=mesh,
        in_specs=(
            P("probe", "state", None, None),
            P(),
            P(),
            P("probe"),
            P("state", None),
            P("state", "probe", None),
        ),
        out_specs=(P(None, "probe", None), P("probe", "state", None, None)),
        check_vma=False,
    )
```
